256 devices in a mesh: dp: 8 (over x, core), ctx: 32 (over y, z).
Axes of the slice: x: 4, y: 4, z: 8, core: 2. Of those that a mesh axis runs over, the one named last changes fastest.
Arguments:
- query_raw: bfloat16 [8, 8192, 128], P('dp', 'ctx'), may hold values from -6 to 6
- key_raw: bfloat16 [8, 8192, 128], P('dp', 'ctx'), may hold values from -6 to 6
- value_raw: bfloat16 [8, 8192, 1024], P('dp', 'ctx'), may hold values from -8 to 8
- conv_query: float32 [3, 128], replicated, may hold values from -2.5 to 2.5
- conv_key: float32 [3, 128], replicated, may hold values from -2.5 to 2.5
- conv_value: float32 [3, 1024], replicated, may hold values from -2.5 to 2.5
- norm_gain: float32 [1024], replicated, may hold values from 0.25 to 1.75
- doc_lengths: int32 [8, 8], P('dp'), may hold values from 1 to 4096, 8192 in all within a row
- out_grad: bfloat16 [8, 8192, 1024], P('dp', 'ctx'), may hold values from -6 to 6
Outputs:
- mixed: bfloat16 [8, 8192, 1024], P('dp', 'ctx')
- grad_query: bfloat16 [8, 8192, 128], P('dp', 'ctx')
- grad_key: bfloat16 [8, 8192, 128], P('dp', 'ctx')
- grad_value: bfloat16 [8, 8192, 1024], P('dp', 'ctx')
- grad_conv_query: float32 [3, 128], replicated
- grad_conv_key: float32 [3, 128], replicated
- grad_conv_value: float32 [3, 1024], replicated
- grad_gain: float32 [1024], replicated
The draws below stay inside these ranges and needn't reach their ends.
Inputs may be any that keep to these rules, and one draw needn't show every extreme that they name: `doc_lengths`: each row holds the lengths of the 8 documents of one sequence in order; they sum to 8192 and the longest is exactly 4096.
All inputs are finite; a program needn't handle non-finite values.
Results may differ from the reference program's by a relative error of at most 0.013.
The reference program's roundings to bfloat16 on the way (of `incoming_low`, `kernel`, `grad_attended`, `outgoing_low` and `grad_scores`) count: a program that leaves them out, or rounds other values in their place, can miss the bound.
Values may be sent and summed in bfloat16 or wider, within the bound.
A program may use at most 128 MiB of HBM per device.

```python
import math
import jax
import jax.numpy as jnp
import numpy as np
from jax import lax

HEADS = 8
F = 16
HD = 128
FEATS = 153
TOK_DEV = 256
DOCS = 8
SEQS = 8
SEQ_LEN = 8192
LONGEST = 4096


def draw_value_raw(key, part):
    key = jax.random.fold_in(key, 7)
    scale_key, noise_key = jax.random.split(key, 2)
    channel_scales = jnp.exp(jax.random.uniform(scale_key, (HEADS * HD,), jnp.float32, 0.0, jnp.log(10.0))) * 0.3
    noise = jax.random.normal(noise_key, (SEQS, SEQ_LEN, HEADS * HD), jnp.float32)
    return jnp.clip(noise * channel_scales, -8.0, 8.0).astype(jnp.bfloat16)


def block_scale(own_key, dims, shards, least, top_value):
    def one(dim, shards_of):
        draws = jax.random.uniform(jax.random.fold_in(jax.random.fold_in(own_key, 6), dim), (shards_of,), jnp.float32, least / len(shards), top_value / len(shards))
        return jnp.repeat(jnp.exp(draws), dims[dim] // shards_of).reshape((-1,) + (1,) * (len(dims) - dim - 1))

    loudness = one(*shards[0])
    for cut in shards[1:]:
        loudness = loudness * one(*cut)
    return loudness


def length_profile(number_of, total, limit, skew):
    weights = [(1 << 20) // math.isqrt(grade ** skew) + 1 for grade in range(2, number_of + 1)]
    spare, holding = total - limit - (number_of - 1), [1] * (number_of - 1)
    while spare > 0:
        free = [i for i in range(number_of - 1) if holding[i] < limit]
        whole, remaining = sum([weights[i] for i in free]), spare
        for i in free:
            addition = min(limit - holding[i], max(1, remaining * weights[i] // whole), spare)
            holding[i] = holding[i] + addition
            spare = spare - addition
    return np.array([limit] + holding)


def uneven_parts(key, amount, total, limit, lean):
    if amount == 2:
        one = jax.random.randint(key, (), max(1, total - limit), min(limit, total - 1) + 1)
        return jnp.stack([one, total - one])
    sizes = jnp.asarray(length_profile(amount, total, limit, lean), jnp.int32)
    couples = (amount - 1) // 2
    source_of, receiver = sizes[1:1 + 2 * couples:2], sizes[2:2 + 2 * couples:2]
    room = jnp.minimum(source_of - 1, limit - receiver)
    shifted = jax.random.randint(jax.random.fold_in(key, 1), (couples,), 0, 1 << 20) % (room + 1)
    sizes = sizes.at[1:1 + 2 * couples:2].set(source_of - shifted).at[2:2 + 2 * couples:2].set(receiver + shifted)
    return sizes[jax.random.permutation(jax.random.fold_in(key, 2), amount)]


def gaussian(rng, dims, deviation, reach, cuts=(), kind=jnp.bfloat16):
    factor_of = block_scale(rng, dims, cuts, -0.22, 0.18) if cuts else 1.0
    entries = jax.random.normal(rng, dims, jnp.float32) * deviation * factor_of
    return jnp.minimum(jnp.maximum(entries, -reach), reach).astype(kind)


def setup_inputs(seed: int = 0) -> dict:
    keys = jax.random.split(jax.random.key(seed), 10)
    return {
        "query_raw": gaussian(keys[0], (SEQS, SEQ_LEN, HEADS * F), 1.0, 6.0, ((0, 8), (1, 32))),
        "key_raw": gaussian(keys[1], (SEQS, SEQ_LEN, HEADS * F), 1.0, 6.0, ((0, 8), (1, 32))),
        "value_raw": draw_value_raw(jax.random.fold_in(keys[9], 71), 0),
        "conv_query": gaussian(keys[3], (3, HEADS * F), 0.6, 2.5, (), jnp.float32),
        "conv_key": gaussian(keys[4], (3, HEADS * F), 0.6, 2.5, (), jnp.float32),
        "conv_value": gaussian(keys[5], (3, HEADS * HD), 0.6, 2.5, (), jnp.float32),
        "norm_gain": jnp.clip(1.0 + 0.15 * jax.random.normal(keys[6], (HEADS * HD,), jnp.float32), 0.25, 1.75),
        "doc_lengths": jax.vmap(lambda own: uneven_parts(own, DOCS, SEQ_LEN, LONGEST, 2))(jax.random.split(keys[7], SEQS)).reshape((SEQS, DOCS)).astype(jnp.int32),
        "out_grad": gaussian(keys[8], (SEQS, SEQ_LEN, HEADS * HD), 1.0, 6.0, ((0, 8), (1, 32))),
    }


full_precision = lax.Precision.HIGHEST
norm_eps = 1e-06

def features(units):
    upper_rows, upper_cols = np.triu_indices(F)
    weight = np.where(upper_rows == upper_cols, 0.5 ** 0.5, 1.0).astype(np.float32)
    pairs = units[..., upper_rows] * units[..., upper_cols] * weight
    leading = jnp.ones(units.shape[:-1] + (1,), units.dtype)
    return jnp.concatenate([leading, units, pairs], axis=-1)

def scaled_features(units):
    return features(units * 0.5)

def state_product(form, left, right):
    return jnp.einsum(form, left.astype(jnp.float32), right.astype(jnp.float32), precision=full_precision)

def doc_index(lengths, positions):
    starts = (jnp.cumsum(lengths) - lengths).astype(jnp.int32)
    hits = (positions[:, None] >= starts[None, :]).astype(jnp.int32)
    return lax.optimization_barrier(jnp.sum(hits, axis=1)).astype(jnp.int32) - 1

def block_mask(docs):
    order = jnp.arange(docs.shape[0], dtype=jnp.int32)
    return (order[None, :] <= order[:, None]) & (docs[None, :] == docs[:, None])

def head_kernel(query_head, key_head, mask):
    scores = jnp.dot(query_head, key_head.T, preferred_element_type=jnp.float32) * 0.25
    kernel = jnp.where(mask, 1.0 + scores + 0.5 * scores * scores, 0.0).astype(jnp.bfloat16)
    return (kernel, scores)

def conv_forward(padded, weights, tokens):
    total = weights[0] * padded[2:] + weights[1] * padded[1:tokens + 1] + weights[2] * padded[:tokens]
    return total.astype(jnp.bfloat16)

def conv_backward(grads_padded, padded, weights, tokens):
    inner = grads_padded[:tokens]
    grad_signal = weights[0] * grads_padded[:tokens] + weights[1] * grads_padded[1:tokens + 1] + weights[2] * grads_padded[2:]
    grad_weights = jnp.stack([lax.optimization_barrier(jnp.sum(inner * padded[2:], axis=0)), lax.optimization_barrier(jnp.sum(inner * padded[1:tokens + 1], axis=0)), lax.optimization_barrier(jnp.sum(inner * padded[:tokens], axis=0))])
    return (grad_signal.astype(jnp.bfloat16), grad_weights)

def tail_state(key_conv, value_conv, use_next):
    tokens = key_conv.shape[0]
    phi_key = scaled_features(key_conv.reshape(tokens, HEADS, F).astype(jnp.float32)).astype(jnp.bfloat16)
    masked = phi_key * use_next.astype(jnp.bfloat16)[:, None, None]
    return state_product('thf,thd->hfd', masked, value_conv.reshape(tokens, HEADS, HD))

def block_kernels(query_conv, key_conv, docs):
    tokens = query_conv.shape[0]
    mask = block_mask(docs)
    query_heads = jnp.moveaxis(query_conv.reshape(tokens, HEADS, F), 1, 0)
    key_heads = jnp.moveaxis(key_conv.reshape(tokens, HEADS, F), 1, 0)
    return lax.map(lambda pieces: head_kernel(pieces[0], pieces[1], mask), (query_heads, key_heads))

def forward_block(query_conv, key_conv, value_conv, docs, use_prev, incoming, upstream_raw, norm_gain):
    tokens = query_conv.shape[0]
    mask = block_mask(docs)
    query_heads = jnp.moveaxis(query_conv.reshape(tokens, HEADS, F), 1, 0)
    key_heads = jnp.moveaxis(key_conv.reshape(tokens, HEADS, F), 1, 0)
    value_heads = jnp.moveaxis(value_conv.reshape(tokens, HEADS, HD), 1, 0)

    def per_head(pieces):
        kernel, scores = head_kernel(pieces[0], pieces[1], mask)
        inner = jnp.dot(kernel, pieces[2], preferred_element_type=jnp.float32)
        return (kernel, scores, inner)
    kernels, scores, inner = lax.map(per_head, (query_heads, key_heads, value_heads))
    phi_query = scaled_features(query_conv.reshape(tokens, HEADS, F).astype(jnp.float32)).astype(jnp.bfloat16)
    prev_mask = use_prev[:, None, None]
    cross = state_product('thf,hfd->thd', phi_query, incoming.astype(jnp.bfloat16))
    attended = jnp.moveaxis(inner, 0, 1) + cross * prev_mask
    scale = jnp.sqrt(lax.optimization_barrier(jnp.mean(attended * attended, axis=-1, keepdims=True)) + norm_eps)
    normed = attended / scale
    gains = norm_gain.reshape(HEADS, HD)
    mixed = (normed * gains).reshape(tokens, HEADS * HD).astype(jnp.bfloat16)
    upstream = upstream_raw.reshape(tokens, HEADS, HD).astype(jnp.float32)
    gain_part = lax.optimization_barrier(jnp.sum(upstream * normed, axis=0)).reshape(HEADS * HD)
    pulled = upstream * gains
    grad_attended = ((pulled - normed * lax.optimization_barrier(jnp.mean(pulled * normed, axis=-1, keepdims=True))) / scale).astype(jnp.bfloat16)
    masked_query = phi_query * use_prev.astype(jnp.bfloat16)[:, None, None]
    head_state = state_product('thf,thd->hfd', masked_query, grad_attended)
    return (mixed, grad_attended, gain_part, head_state, kernels, scores)

def backward_block(query_conv, key_conv, value_conv, docs, use_prev, use_next, incoming, outgoing, grad_attended, kernels, scores):
    tokens = query_conv.shape[0]
    mask = block_mask(docs)
    query_heads = jnp.moveaxis(query_conv.reshape(tokens, HEADS, F), 1, 0)
    key_heads = jnp.moveaxis(key_conv.reshape(tokens, HEADS, F), 1, 0)
    value_heads = jnp.moveaxis(value_conv.reshape(tokens, HEADS, HD), 1, 0)
    grad_heads = jnp.moveaxis(grad_attended.reshape(tokens, HEADS, HD), 1, 0)

    def per_head(pieces):
        query_head, key_head, value_head, grad_head, kernel, score = pieces
        grad_kernel = jnp.dot(grad_head, value_head.T, preferred_element_type=jnp.float32)
        grad_scores = jnp.where(mask, grad_kernel * (1.0 + score), 0.0).astype(jnp.bfloat16)
        grad_query = jnp.dot(grad_scores, key_head, preferred_element_type=jnp.float32) * 0.25
        grad_key = jnp.dot(grad_scores.T, query_head, preferred_element_type=jnp.float32) * 0.25
        grad_value = jnp.dot(kernel.T, grad_head, preferred_element_type=jnp.float32)
        return (grad_query, grad_key, grad_value)
    inner_query, inner_key, inner_value = lax.map(per_head, (query_heads, key_heads, value_heads, grad_heads, kernels, scores))
    query_units = query_conv.reshape(tokens, HEADS, F).astype(jnp.float32)
    key_units = key_conv.reshape(tokens, HEADS, F).astype(jnp.float32)
    values = value_conv.reshape(tokens, HEADS, HD)
    upstream = grad_attended.reshape(tokens, HEADS, HD)
    incoming_low = incoming.astype(jnp.bfloat16)
    outgoing_low = outgoing.astype(jnp.bfloat16)
    prev_mask = use_prev[:, None, None]
    next_mask = use_next[:, None, None]
    phi_query, pull_query = jax.vjp(scaled_features, query_units)
    phi_key, pull_key = jax.vjp(scaled_features, key_units)
    grad_phi_query = state_product('thd,hfd->thf', upstream, incoming_low) * prev_mask
    grad_phi_key = state_product('thd,hfd->thf', values, outgoing_low) * next_mask
    cross_value = state_product('thf,hfd->thd', phi_key.astype(jnp.bfloat16), outgoing_low) * next_mask
    total_query = jnp.moveaxis(inner_query, 0, 1) + pull_query(grad_phi_query)[0]
    total_key = jnp.moveaxis(inner_key, 0, 1) + pull_key(grad_phi_key)[0]
    total_value = jnp.moveaxis(inner_value, 0, 1) + cross_value
    return (total_query.reshape(tokens, HEADS * F), total_key.reshape(tokens, HEADS * F), total_value.reshape(tokens, HEADS * HD))

def carry_state(carry, pieces):
    return (pieces[0] + (1.0 - pieces[1]) * carry, carry)

def one_sequence(query_raw, key_raw, value_raw, lengths, out_grad, conv_query, conv_key, conv_value, norm_gain):
    length = query_raw.shape[0]
    blocks = length // TOK_DEV
    query_padded = jnp.pad(query_raw.astype(jnp.float32), ((2, 0), (0, 0)))
    key_padded = jnp.pad(key_raw.astype(jnp.float32), ((2, 0), (0, 0)))
    value_padded = jnp.pad(value_raw.astype(jnp.float32), ((2, 0), (0, 0)))
    query_conv = conv_forward(query_padded, conv_query, length)
    key_conv = conv_forward(key_padded, conv_key, length)
    value_conv = conv_forward(value_padded, conv_value, length)
    docs = doc_index(lengths, jnp.arange(length, dtype=jnp.int32))
    firsts = jnp.arange(blocks, dtype=jnp.int32) * TOK_DEV
    prev_doc = doc_index(lengths, firsts - 1)
    last_doc = doc_index(lengths, firsts + TOK_DEV - 1)
    doc_blocks = docs.reshape(blocks, TOK_DEV)
    use_prev = (doc_blocks == prev_doc[:, None]).astype(jnp.float32)
    use_next = (doc_blocks == last_doc[:, None]).astype(jnp.float32)
    resets = (prev_doc != last_doc).astype(jnp.float32)
    query_blocks = query_conv.reshape(blocks, TOK_DEV, HEADS * F)
    key_blocks = key_conv.reshape(blocks, TOK_DEV, HEADS * F)
    value_blocks = value_conv.reshape(blocks, TOK_DEV, HEADS * HD)
    upstream_blocks = out_grad.reshape(blocks, TOK_DEV, HEADS * HD)
    tails = lax.map(lambda pieces: tail_state(pieces[0], pieces[1], pieces[2]), (key_blocks, value_blocks, use_next))
    zero_state = jnp.zeros((HEADS, FEATS, HD), jnp.float32)
    finished, incoming = lax.scan(carry_state, zero_state, (tails, resets))

    def forward_piece(pieces):
        outputs = forward_block(pieces[0], pieces[1], pieces[2], pieces[3], pieces[4], pieces[5], pieces[6], norm_gain)
        return (outputs[0], outputs[1], outputs[2], outputs[3])
    mixed, grad_attended, gain_parts, head_states = lax.map(forward_piece, (query_blocks, key_blocks, value_blocks, doc_blocks, use_prev, incoming, upstream_blocks))
    started, outgoing = lax.scan(carry_state, zero_state, (head_states, resets), reverse=True)

    def backward_piece(pieces):
        kernels, scores = block_kernels(pieces[0], pieces[1], pieces[3])
        return backward_block(pieces[0], pieces[1], pieces[2], pieces[3], pieces[4], pieces[5], pieces[6], pieces[7], pieces[8], kernels, scores)
    grad_q_conv, grad_k_conv, grad_v_conv = lax.map(backward_piece, (query_blocks, key_blocks, value_blocks, doc_blocks, use_prev, use_next, incoming, outgoing, grad_attended))
    grad_query, conv_grad_query = conv_backward(jnp.pad(grad_q_conv.reshape(length, HEADS * F), ((0, 2), (0, 0))), query_padded, conv_query, length)
    grad_key, conv_grad_key = conv_backward(jnp.pad(grad_k_conv.reshape(length, HEADS * F), ((0, 2), (0, 0))), key_padded, conv_key, length)
    grad_value, conv_grad_value = conv_backward(jnp.pad(grad_v_conv.reshape(length, HEADS * HD), ((0, 2), (0, 0))), value_padded, conv_value, length)
    return (mixed.reshape(length, HEADS * HD), grad_query, grad_key, grad_value, conv_grad_query, conv_grad_key, conv_grad_value, lax.optimization_barrier(jnp.sum(gain_parts, axis=0)))

def reference(query_raw, key_raw, value_raw, conv_query, conv_key, conv_value, norm_gain, doc_lengths, out_grad):

    def per_sequence(pieces):
        return one_sequence(pieces[0], pieces[1], pieces[2], pieces[3], pieces[4], conv_query, conv_key, conv_value, norm_gain)
    results = lax.map(per_sequence, (query_raw, key_raw, value_raw, doc_lengths, out_grad))
    mixed, grad_query, grad_key, grad_value, conv_grad_query, conv_grad_key, conv_grad_value, gain_sums = results
    return (mixed, grad_query, grad_key, grad_value, lax.optimization_barrier(jnp.sum(conv_grad_query, axis=0)), lax.optimization_barrier(jnp.sum(conv_grad_key, axis=0)), lax.optimization_barrier(jnp.sum(conv_grad_value, axis=0)), lax.optimization_barrier(jnp.sum(gain_sums, axis=0)))
```

```python
import functools

import jax
import jax.numpy as jnp
from jax import lax
from jax.experimental import pallas as pl
from jax.experimental.pallas import tpu as pltpu
from jax.sharding import PartitionSpec as P

HEADS = 8
F = 16
HD = 128
T = 256
DOCS = 8
ROWS = 160
ZN = 8
EPS = 1e-06
MESH = pl.DeviceIdType.MESH
F32 = jnp.float32
BF16 = jnp.bfloat16


def dot(a, b, ca, cb):
    return lax.dot_general(a, b, (((ca,), (cb,)), ((), ())), preferred_element_type=F32)


def turned(u, d):
    return pltpu.roll(u, F - d, 0) if d else u


def put_features(out, h, u, ones):
    out[h, 0:16, :] = (u * u * (0.5**0.5)).astype(BF16)
    for d in range(1, 8):
        out[h, 16 * d : 16 * d + 16, :] = (u * turned(u, d)).astype(BF16)
    out[h, 128:144, :] = u.astype(BF16)
    rest = jnp.where(lax.broadcasted_iota(jnp.int32, (8, T), 0) == 0, ones, 0.0)
    out[h, 144:160, :] = jnp.concatenate([u[0:8] * u[8:16], rest], axis=0).astype(BF16)


def pull_features(g, u, ones):
    total = g[128:144] * ones + (2.0 * 0.5**0.5) * g[0:16] * u
    for d in range(1, 8):
        own = g[16 * d : 16 * d + 16]
        total = total + own * turned(u, d) + pltpu.roll(own * u, d, 0)
    half = g[144:152]
    total = total + jnp.concatenate([half * u[8:16], half * u[0:8]], axis=0)
    return 0.5 * total


def kernel(
    n_dp,
    n_ctx,
    lens,
    q_ref,
    k_ref,
    v_ref,
    og_ref,
    wq_ref,
    wk_ref,
    wv_ref,
    gain_ref,
    mixed_ref,
    gq_ref,
    gk_ref,
    gv_ref,
    gwq_ref,
    gwk_ref,
    gwv_ref,
    gg_ref,
    xq,
    xk,
    xv,
    qc,
    kc,
    qt,
    kt,
    uq,
    uk,
    vc,
    mask_ref,
    kern,
    saved,
    inner,
    phiq,
    phik,
    ga_ref,
    gvs,
    gqt,
    gkt,
    gqs,
    gks,
    local,
    halo_q,
    halo_k,
    halo_v,
    back_q,
    back_k,
    back_v,
    tail1,
    got1,
    tot1,
    ytot1,
    send1,
    inc,
    tail2,
    got2,
    tot2,
    ytot2,
    send2,
    outg,
    part,
    red_z,
    one_z,
    red_y,
    one_y,
    red_d,
    one_d,
    all_z,
    halo_ss,
    halo_rs,
    back_ss,
    back_rs,
    a_ss,
    a_rs,
    y_ss,
    y_rs,
    b_ss,
    b_rs,
    rz_ss,
    rz_rs,
    ry_ss,
    ry_rs,
    rd_ss,
    rd_rs,
    az_ss,
    az_rs,
):
    n_y = n_ctx // ZN
    me = lax.axis_index("ctx")
    dp = lax.axis_index("dp")
    y = me // ZN
    z = me % ZN
    after = (me + 1) % n_ctx
    before = (me + n_ctx - 1) % n_ctx

    def z_peer(zz):
        return {"ctx": y * ZN + zz}

    def y_peer(yy):
        return {"ctx": yy * ZN + z}

    barrier = pltpu.get_barrier_semaphore()
    greeted = [z_peer((z + j) % ZN) for j in range(1, ZN)]
    greeted += [y_peer((y + j) % n_y) for j in range(1, n_y)]
    greeted += [{"dp": (dp + j) % n_dp} for j in range(1, n_dp)]
    greeted += [{"ctx": after}, {"ctx": before}]
    for peer in greeted:
        pl.semaphore_signal(barrier, inc=1, device_id=peer, device_id_type=MESH)

    starts = []
    total = jnp.int32(0)
    for d in range(DOCS):
        starts.append(total)
        total = total + lens[0, d]
    first = me * T

    def doc_of(position):
        found = jnp.where(position >= starts[0], 1, 0)
        for d in range(1, DOCS):
            found = found + jnp.where(position >= starts[d], 1, 0)
        return found

    row_pos = first + lax.broadcasted_iota(jnp.int32, (1, T), 1)
    col_pos = first + lax.broadcasted_iota(jnp.int32, (T, 1), 0)
    row_doc, col_doc = doc_of(row_pos), doc_of(col_pos)
    prev_doc, last_doc = doc_of(first - 1), doc_of(first + T - 1)
    use_prev = jnp.where(row_doc == prev_doc, 1.0, 0.0)
    use_next = jnp.where(row_doc == last_doc, 1.0, 0.0)
    mask_ref[...] = jnp.where((row_pos <= col_pos) & (row_doc == col_doc), 1.0, 0.0)

    def keep_of(block):
        value = jnp.float32(1.0)
        for d in range(DOCS):
            value = jnp.where(starts[d] // T == block, 0.0, value)
        return value

    def keep_group(group):
        value = jnp.float32(1.0)
        for d in range(DOCS):
            value = jnp.where(starts[d] // (T * ZN) == group, 0.0, value)
        return value

    xq[8:, :] = q_ref[...].astype(F32)
    xk[8:, :] = k_ref[...].astype(F32)
    for h in range(HEADS):
        xv[h, 8:, :] = v_ref[:, h * HD : (h + 1) * HD].astype(F32)

    pl.semaphore_wait(barrier, len(greeted))

    def remote(src, dst, ss, rs, peer):
        return pltpu.make_async_remote_copy(
            src_ref=src, dst_ref=dst, send_sem=ss, recv_sem=rs, device_id=peer, device_id_type=MESH
        )

    halos = [
        remote(ref.at[T - 16 :, :], dst, halo_ss.at[i], halo_rs.at[i], {"ctx": after})
        for i, (ref, dst) in enumerate([(q_ref, halo_q), (k_ref, halo_k), (v_ref, halo_v)])
    ]
    for c in halos:
        c.start()
    for c in halos:
        c.wait_recv()
    inside = jnp.where(me > 0, 1.0, 0.0)
    xq[0:8, :] = halo_q[...].astype(F32)[8:16] * inside
    xk[0:8, :] = halo_k[...].astype(F32)[8:16] * inside
    for h in range(HEADS):
        xv[h, 0:8, :] = halo_v[:, h * HD : (h + 1) * HD].astype(F32)[8:16] * inside

    def conv(x, w):
        return w[0:1] * x[8 : 8 + T] + w[1:2] * x[7 : 7 + T] + w[2:3] * x[6 : 6 + T]

    q = conv(xq, wq_ref[...]).astype(BF16)
    k = conv(xk, wk_ref[...]).astype(BF16)
    qc[...] = q
    kc[...] = k
    q_turned = q.astype(F32).T
    k_turned = k.astype(F32).T
    qt[...] = q_turned.astype(BF16)
    kt[...] = k_turned.astype(BF16)
    uq[...] = q_turned * (0.5 * use_prev)
    uk[...] = k_turned * (0.5 * use_next)

    def head_rows(h):
        return pl.ds(pl.multiple_of(h * F, F), F)

    def head_cols(h):
        return pl.ds(pl.multiple_of(h * HD, HD), HD)

    def a_copy(tail, got, phase, h):
        return remote(
            tail.at[h], got.at[z], a_ss.at[phase, h], a_rs.at[phase, z], z_peer(h)
        )

    def a_arrival(tail, got, phase, zz):
        return remote(
            tail.at[zz], got.at[zz], a_ss.at[phase, zz], a_rs.at[phase, zz], z_peer(zz)
        )

    def b_copy(send, take, phase, zz):
        return remote(send.at[zz], take.at[z], b_ss.at[phase, zz], b_rs.at[phase, z], z_peer(zz))

    def b_arrival(send, take, phase, h):
        return remote(send.at[h], take.at[h], b_ss.at[phase, h], b_rs.at[phase, h], z_peer(h))

    def tail_head(h):
        cols = head_cols(h)
        w = wv_ref[:, cols]
        x = xv.at[h]
        value = (
            w[0:1] * x[8 : 8 + T, :] + w[1:2] * x[7 : 7 + T, :] + w[2:3] * x[6 : 6 + T, :]
        ).astype(BF16)
        vc[h] = value
        put_features(phik, h, uk[head_rows(h), :], use_next)
        tail1[h] = dot(phik[h], value, 1, 0).astype(BF16)

    def tail_step(j, _):
        h = (z + 1 + j) % ZN
        tail_head(h)
        a_copy(tail1, got1, 0, h).start()
        return 0

    lax.fori_loop(0, ZN - 1, tail_step, 0)
    tail_head(z)
    got1[z] = tail1[z]

    lane_head = lax.broadcasted_iota(jnp.int32, (1, HEADS * F), 1) // F

    def inner_step(h, _):
        chosen = jnp.where(lane_head == h, 0.25, 0.0).astype(BF16)
        scores = dot(qc[...] * chosen, kc[...], 1, 1)
        m = mask_ref[...]
        kernel_h = (m * (1.0 + scores + 0.5 * scores * scores)).astype(BF16)
        kern[h] = kernel_h
        saved[h] = m * (1.0 + scores)
        inner[h] = dot(kernel_h, vc[h], 1, 0)
        put_features(phiq, h, uq[head_rows(h), :], use_prev)
        return 0

    lax.fori_loop(0, HEADS, inner_step, 0)

    def scan(tail, got, tot, ytot, send, take, phase, reverse):
        def wait_a(j, _):
            a_arrival(tail, got, phase, (z + j) % ZN).wait_recv()
            return 0

        lax.fori_loop(1, ZN, wait_a, 0)
        order = range(ZN - 1, -1, -1) if reverse else range(ZN)
        running = jnp.zeros((ROWS, HD), F32)
        keeps = {}
        for i in order:
            keeps[i] = keep_of(y * ZN + i)
            running = got[i].astype(F32) + keeps[i] * running
        tot[...] = running.astype(BF16)
        ytot[y] = running.astype(BF16)

        def y_copy(j):
            yy = (y + j) % n_y
            return remote(tot, ytot.at[y], y_ss.at[phase, yy], y_rs.at[phase, y], y_peer(yy))

        def y_arrival(j):
            yy = (y + j) % n_y
            return remote(tot, ytot.at[yy], y_ss.at[phase, yy], y_rs.at[phase, yy], y_peer(yy))

        for j in range(1, n_y):
            y_copy(j).start()
        for j in range(1, n_y):
            y_arrival(j).wait_recv()
        carry = jnp.zeros((ROWS, HD), F32)
        for g in range(n_y - 1, 0, -1) if reverse else range(n_y - 1):
            counts = jnp.where(g > y if reverse else g < y, 1.0, 0.0)
            onward = ytot[g].astype(F32) + keep_group(g) * carry
            carry = counts * onward + (1.0 - counts) * carry
        running = carry
        for i in order:
            send[i] = running.astype(BF16)
            running = got[i].astype(F32) + keeps[i] * running

        def send_b(j, _):
            b_copy(send, take, phase, (z + j) % ZN).start()
            return 0

        lax.fori_loop(1, ZN, send_b, 0)
        take[z] = send[z]

    scan(tail1, got1, tot1, ytot1, send1, inc, 0, False)

    def forward_head(h):
        cols = head_cols(h)
        attended = inner[h] + dot(phiq[h], inc[h], 0, 0)
        r = lax.rsqrt(jnp.mean(attended * attended, axis=-1, keepdims=True) + EPS)
        normed = attended * r
        gains = gain_ref[:, cols]
        mixed_ref[:, cols] = (normed * gains).astype(BF16)
        upstream = og_ref[:, cols].astype(F32)
        local[h, 3:4, :] = jnp.sum(upstream * normed, axis=0, keepdims=True)
        pulled = upstream * gains
        along = jnp.mean(pulled * normed, axis=-1, keepdims=True)
        grad = ((pulled - normed * along) * r).astype(BF16)
        ga_ref[h] = grad
        tail2[h] = dot(phiq[h], grad, 1, 0).astype(BF16)

    local[...] = jnp.zeros(local.shape, F32)
    forward_head(z)
    got2[z] = tail2[z]

    def nearest(j):
        away = (j + 1) // 2
        return (z + ZN + away * (1 - 2 * (j % 2))) % ZN

    def forward_step(j, _):
        h = nearest(j)
        b_arrival(send1, inc, 0, h).wait_recv()
        forward_head(h)
        a_copy(tail2, got2, 1, h).start()
        return 0

    lax.fori_loop(1, ZN, forward_step, 0)

    def backward_step(h, _):
        grad = ga_ref[h]
        grad_scores = (dot(grad, vc[h], 1, 1) * saved[h]).astype(BF16)
        rows = head_rows(h)
        grad_phi = dot(inc[h], grad, 1, 1)
        gqt[rows, :] = 0.25 * dot(kt[rows, :], grad_scores, 1, 1) + pull_features(
            grad_phi, uq[rows, :], use_prev
        )
        gkt[rows, :] = 0.25 * dot(qt[rows, :], grad_scores, 1, 0)
        gvs[h, 0:T, :] = dot(kern[h], grad, 0, 0)
        return 0

    lax.fori_loop(0, HEADS, backward_step, 0)

    scan(tail2, got2, tot2, ytot2, send2, outg, 1, True)

    def taps(g, x):
        return [jnp.sum(g * x[8 - j : 8 - j + T], axis=0, keepdims=True) for j in range(3)]

    def last_head(h):
        rows = head_rows(h)
        later = outg[h]
        grad_phi = dot(later, vc[h], 1, 1)
        gkt[rows, :] = gkt[rows, :] + pull_features(grad_phi, uk[rows, :], use_next)
        g = gvs[h, 0:T, :] + dot(phik[h], later, 0, 0)
        gvs[h, 0:T, :] = g
        for j in range(3):
            local[h, j : j + 1, :] = jnp.sum(
                g * xv[h, 8 - j : 8 - j + T, :], axis=0, keepdims=True
            )

    last_head(z)

    def last_step(j, _):
        h = nearest(j)
        b_arrival(send2, outg, 1, h).wait_recv()
        last_head(h)
        return 0

    lax.fori_loop(1, ZN, last_step, 0)
    gq = gqt[...].T
    gk = gkt[...].T
    gqs[0:T, :] = gq
    gks[0:T, :] = gk

    backs = [
        remote(src, dst, back_ss.at[i], back_rs.at[i], {"ctx": before})
        for i, (src, dst) in enumerate(
            [
                (gqs.at[0:8, :], back_q),
                (gks.at[0:8, :], back_k),
                (gvs.at[:, 0:8, :], back_v),
            ]
        )
    ]
    for c in backs:
        c.start()

    for j in range(3):
        local[0, 4 + j : 5 + j, :] = jnp.sum(gq * xq[8 - j : 8 - j + T, :], axis=0, keepdims=True)
        local[1, 4 + j : 5 + j, :] = jnp.sum(gk * xk[8 - j : 8 - j + T, :], axis=0, keepdims=True)

    def rz_copy(zz):
        return remote(local.at[zz], red_z.at[z], rz_ss.at[zz], rz_rs.at[z], z_peer(zz))

    def rz_arrival(zz):
        return remote(local.at[zz], red_z.at[zz], rz_ss.at[zz], rz_rs.at[zz], z_peer(zz))

    for j in range(1, ZN):
        rz_copy((z + j) % ZN).start()
    red_z[z] = local[z]

    for c in backs:
        c.wait_recv()
    inside_next = jnp.where(me < n_ctx - 1, 1.0, 0.0)
    gqs[T : T + 8, :] = back_q[...] * inside_next
    gks[T : T + 8, :] = back_k[...] * inside_next
    for c in backs:
        c.wait_send()
    gvs[:, T : T + 8, :] = back_v[...] * inside_next

    def conv_back(g, w):
        return (w[0:1] * g[0:T] + w[1:2] * g[1 : 1 + T] + w[2:3] * g[2 : 2 + T]).astype(BF16)

    gq_ref[...] = conv_back(gqs, wq_ref[...])
    gk_ref[...] = conv_back(gks, wk_ref[...])

    def value_step(h, _):
        cols = head_cols(h)
        w = wv_ref[:, cols]
        gv_ref[:, cols] = (
            w[0:1] * gvs[h, 0:T, :]
            + w[1:2] * gvs[h, 1 : 1 + T, :]
            + w[2:3] * gvs[h, 2 : 2 + T, :]
        ).astype(BF16)
        return 0

    lax.fori_loop(0, HEADS, value_step, 0)

    for j in range(1, ZN):
        rz_arrival((z + j) % ZN).wait_recv()
    tile = jnp.sum(red_z[...], axis=0)
    one_y[...] = tile
    red_y[y] = tile

    def ry(yy, slot):
        return remote(one_y, red_y.at[slot], ry_ss.at[yy], ry_rs.at[slot], y_peer(yy))

    for j in range(1, n_y):
        ry((y + j) % n_y, y).start()
    for j in range(1, n_y):
        ry((y + j) % n_y, (y + j) % n_y).wait_recv()
    tile = jnp.sum(red_y[...], axis=0)
    one_d[...] = tile
    red_d[dp] = tile

    def rd(dd, slot):
        return remote(one_d, red_d.at[slot], rd_ss.at[dd], rd_rs.at[slot], {"dp": dd})

    for j in range(1, n_dp):
        rd((dp + j) % n_dp, dp).start()
    for j in range(1, n_dp):
        rd((dp + j) % n_dp, (dp + j) % n_dp).wait_recv()
    tile = jnp.sum(red_d[...], axis=0)
    one_z[...] = tile
    all_z[z] = tile

    def az(zz, slot):
        return remote(one_z, all_z.at[slot], az_ss.at[zz], az_rs.at[slot], z_peer(zz))

    for j in range(1, ZN):
        az((z + j) % ZN, z).start()
    for j in range(1, ZN):
        az((z + j) % ZN, (z + j) % ZN).wait_recv()
    gwq_ref[...] = all_z[0, 4:7, :]
    gwk_ref[...] = all_z[1, 4:7, :]
    for h in range(HEADS):
        gwv_ref[:, h * HD : (h + 1) * HD] = all_z[h, 0:3, :]
        gg_ref[:, h * HD : (h + 1) * HD] = all_z[h, 3:4, :]

    for c in halos:
        c.wait_send()

    def left(j, _):
        zz = (z + j) % ZN
        a_copy(tail1, got1, 0, zz).wait_send()
        a_copy(tail2, got2, 1, zz).wait_send()
        b_copy(send1, inc, 0, zz).wait_send()
        b_copy(send2, outg, 1, zz).wait_send()
        rz_copy(zz).wait_send()
        az(zz, z).wait_send()
        return 0

    lax.fori_loop(1, ZN, left, 0)
    for j in range(1, n_y):
        yy = (y + j) % n_y
        remote(tot1, ytot1.at[y], y_ss.at[0, yy], y_rs.at[0, y], y_peer(yy)).wait_send()
        remote(tot2, ytot2.at[y], y_ss.at[1, yy], y_rs.at[1, y], y_peer(yy)).wait_send()
        ry(yy, y).wait_send()
    for j in range(1, n_dp):
        rd((dp + j) % n_dp, dp).wait_send()


def solution(mesh):
    n_dp, n_ctx = mesh.shape["dp"], mesh.shape["ctx"]
    n_y = n_ctx // ZN
    wide = HEADS * HD
    thin = HEADS * F

    def shards(q, k, v, wq, wk, wv, gain, lens, og):
        vmem = pl.BlockSpec(memory_space=pltpu.VMEM)
        state = (ROWS, HD)
        scratch = [
            pltpu.VMEM((T + 8, thin), F32),
            pltpu.VMEM((T + 8, thin), F32),
            pltpu.VMEM((HEADS, T + 8, HD), F32),
            pltpu.VMEM((T, thin), BF16),
            pltpu.VMEM((T, thin), BF16),
            pltpu.VMEM((thin, T), BF16),
            pltpu.VMEM((thin, T), BF16),
            pltpu.VMEM((thin, T), F32),
            pltpu.VMEM((thin, T), F32),
            pltpu.VMEM((HEADS, T, HD), BF16),
            pltpu.VMEM((T, T), F32),
            pltpu.VMEM((HEADS, T, T), BF16),
            pltpu.VMEM((HEADS, T, T), F32),
            pltpu.VMEM((HEADS, T, HD), F32),
            pltpu.VMEM((HEADS, ROWS, T), BF16),
            pltpu.VMEM((HEADS, ROWS, T), BF16),
            pltpu.VMEM((HEADS, T, HD), BF16),
            pltpu.VMEM((HEADS, T + 8, HD), F32),
            pltpu.VMEM((thin, T), F32),
            pltpu.VMEM((thin, T), F32),
            pltpu.VMEM((T + 8, thin), F32),
            pltpu.VMEM((T + 8, thin), F32),
            pltpu.VMEM((HEADS, 8, HD), F32),
            pltpu.VMEM((16, thin), BF16),
            pltpu.VMEM((16, thin), BF16),
            pltpu.VMEM((16, wide), BF16),
            pltpu.VMEM((8, thin), F32),
            pltpu.VMEM((8, thin), F32),
            pltpu.VMEM((HEADS, 8, HD), F32),
        ]
        for _ in range(2):
            scratch += [
                pltpu.VMEM((HEADS,) + state, BF16),
                pltpu.VMEM((ZN,) + state, BF16),
                pltpu.VMEM(state, BF16),
                pltpu.VMEM((n_y,) + state, BF16),
                pltpu.VMEM((ZN,) + state, BF16),
                pltpu.VMEM((HEADS,) + state, BF16),
            ]
        tile = (8, HD)
        scratch += [
            pltpu.VMEM(tile, F32),
            pltpu.VMEM((ZN,) + tile, F32),
            pltpu.VMEM(tile, F32),
            pltpu.VMEM((n_y,) + tile, F32),
            pltpu.VMEM(tile, F32),
            pltpu.VMEM((n_dp,) + tile, F32),
            pltpu.VMEM(tile, F32),
            pltpu.VMEM((ZN,) + tile, F32),
        ]
        dma = pltpu.SemaphoreType.DMA
        for counts in ((3,), (3,), (2, ZN), (2, n_y), (2, ZN), (ZN,), (n_y,), (n_dp,), (ZN,)):
            scratch += [dma(counts), dma(counts)]
        outs = pl.pallas_call(
            functools.partial(kernel, n_dp, n_ctx),
            out_shape=(
                jax.ShapeDtypeStruct((T, wide), BF16),
                jax.ShapeDtypeStruct((T, thin), BF16),
                jax.ShapeDtypeStruct((T, thin), BF16),
                jax.ShapeDtypeStruct((T, wide), BF16),
                jax.ShapeDtypeStruct((3, thin), F32),
                jax.ShapeDtypeStruct((3, thin), F32),
                jax.ShapeDtypeStruct((3, wide), F32),
                jax.ShapeDtypeStruct((1, wide), F32),
            ),
            in_specs=[pl.BlockSpec(memory_space=pltpu.SMEM)] + [vmem] * 8,
            out_specs=(vmem,) * 8,
            scratch_shapes=scratch,
            compiler_params=pltpu.CompilerParams(
                collective_id=0, has_side_effects=True, vmem_limit_bytes=48 * 2**20
            ),
        )(lens, q[0], k[0], v[0], og[0], wq, wk, wv, gain[None])
        mixed, gq, gk, gv, gwq, gwk, gwv, gg = outs
        return mixed[None], gq[None], gk[None], gv[None], gwq, gwk, gwv, gg[0]

    tokens = P("dp", "ctx", None)
    return jax.shard_map(
        shards,
        mesh=mesh,
        in_specs=(tokens, tokens, tokens, P(), P(), P(), P(), P("dp", None), tokens),
        out_specs=(tokens, tokens, tokens, tokens, P(), P(), P(), P()),
        check_vma=False,
    )
```

```python
import functools

import jax
import jax.numpy as jnp
from jax import lax
from jax.experimental import pallas as pl
from jax.experimental.pallas import tpu as pltpu
from jax.sharding import PartitionSpec as P

HEADS = 8
F = 16
HD = 128
T = 256
DOCS = 8
ROWS = 160
ZN = 8
EPS = 1e-06
MESH = pl.DeviceIdType.MESH
F32 = jnp.float32
BF16 = jnp.bfloat16


def dot(a, b, ca, cb):
    return lax.dot_general(a, b, (((ca,), (cb,)), ((), ())), preferred_element_type=F32)


def turned(u, d):
    return pltpu.roll(u, F - d, 0) if d else u


def put_features(out, h, u, ones):
    out[h, 0:16, :] = (u * u * (0.5**0.5)).astype(BF16)
    for d in range(1, 8):
        out[h, 16 * d : 16 * d + 16, :] = (u * turned(u, d)).astype(BF16)
    out[h, 128:144, :] = u.astype(BF16)
    rest = jnp.where(lax.broadcasted_iota(jnp.int32, (8, T), 0) == 0, ones, 0.0)
    out[h, 144:160, :] = jnp.concatenate([u[0:8] * u[8:16], rest], axis=0).astype(BF16)


def pull_features(g, u, ones):
    total = g[128:144] * ones + (2.0 * 0.5**0.5) * g[0:16] * u
    for d in range(1, 8):
        own = g[16 * d : 16 * d + 16]
        total = total + own * turned(u, d) + pltpu.roll(own * u, d, 0)
    half = g[144:152]
    total = total + jnp.concatenate([half * u[8:16], half * u[0:8]], axis=0)
    return 0.5 * total


def kernel(
    n_dp,
    n_ctx,
    lens_hbm,
    q_hbm,
    k_hbm,
    v_hbm,
    og_hbm,
    wq_hbm,
    wk_hbm,
    wv_hbm,
    gain_hbm,
    mixed_hbm,
    gq_hbm,
    gk_hbm,
    gv_hbm,
    sums_ref,
    mixed_ref,
    gq_ref,
    gk_ref,
    gv_ref,
    out_s,
    lens,
    q_ref,
    k_ref,
    v_ref,
    og_ref,
    wq_ref,
    wk_ref,
    wv_ref,
    gain_ref,
    xq,
    xk,
    xv,
    qc,
    kc,
    qt,
    kt,
    uq,
    uk,
    vc,
    mask_ref,
    kern,
    saved,
    inner,
    phiq,
    phik,
    ga_ref,
    gvs,
    gqt,
    gkt,
    gqs,
    gks,
    local,
    halo_q,
    halo_k,
    halo_v,
    back_q,
    back_k,
    back_v,
    tail1,
    got1,
    tot1,
    ytot1,
    send1,
    inc,
    tail2,
    got2,
    tot2,
    ytot2,
    send2,
    outg,
    halves,
    red_c,
    red_xy,
    one_xy,
    red_z,
    one_z,
    one_c,
    in_s,
    halo_ss,
    halo_rs,
    back_ss,
    back_rs,
    a_ss,
    a_rs,
    y_ss,
    y_rs,
    b_ss,
    b_rs,
    rc_ss,
    rc_rs,
    rxy_ss,
    rxy_rs,
    rz_ss,
    rz_rs,
    ac_ss,
    ac_rs,
):
    n_y = n_ctx // ZN
    me = lax.axis_index("ctx")
    dp = lax.axis_index("dp")
    n_x = n_dp // 2
    core = dp % 2
    x = dp // 2
    y = me // ZN
    z = me % ZN
    after = (me + 1) % n_ctx
    before = (me + n_ctx - 1) % n_ctx

    def z_peer(zz):
        return {"ctx": y * ZN + zz}

    def y_peer(yy):
        return {"ctx": yy * ZN + z}

    barrier = pltpu.get_barrier_semaphore()
    greeted = [z_peer((z + j) % ZN) for j in range(1, ZN)]
    other = {"dp": dp + 1 - 2 * core}
    plane = []
    for j in range(1, n_x * n_y):
        xx = (x + j // n_y) % n_x
        yy = (y + j % n_y) % n_y
        plane.append((xx * n_y + yy, {"dp": xx * 2 + core, "ctx": yy * ZN + z}))
    greeted += [peer for _, peer in plane]
    greeted += [other, {"ctx": after}, {"ctx": before}]
    for peer in greeted:
        pl.semaphore_signal(barrier, inc=1, device_id=peer, device_id_type=MESH)

    loads = [
        pltpu.make_async_copy(src, dst, in_s.at[i])
        for i, (src, dst) in enumerate(
            [
                (lens_hbm, lens),
                (q_hbm, q_ref),
                (k_hbm, k_ref),
                (wq_hbm, wq_ref),
                (wk_hbm, wk_ref),
                (v_hbm, v_ref),
                (wv_hbm, wv_ref),
                (gain_hbm, gain_ref),
                (og_hbm, og_ref),
            ]
        )
    ]
    for c in loads:
        c.start()
    for c in loads[:5]:
        c.wait()

    starts = []
    total = jnp.int32(0)
    for d in range(DOCS):
        starts.append(total)
        total = total + lens[0, d]
    first = me * T

    def doc_of(position):
        found = jnp.where(position >= starts[0], 1, 0)
        for d in range(1, DOCS):
            found = found + jnp.where(position >= starts[d], 1, 0)
        return found

    row_pos = first + lax.broadcasted_iota(jnp.int32, (1, T), 1)
    col_pos = first + lax.broadcasted_iota(jnp.int32, (T, 1), 0)
    row_doc, col_doc = doc_of(row_pos), doc_of(col_pos)
    prev_doc, last_doc = doc_of(first - 1), doc_of(first + T - 1)
    use_prev = jnp.where(row_doc == prev_doc, 1.0, 0.0)
    use_next = jnp.where(row_doc == last_doc, 1.0, 0.0)
    mask_ref[...] = jnp.where((row_pos <= col_pos) & (row_doc == col_doc), 1.0, 0.0)

    def keep_of(block):
        value = jnp.float32(1.0)
        for d in range(DOCS):
            value = jnp.where(starts[d] // T == block, 0.0, value)
        return value

    def keep_group(group):
        value = jnp.float32(1.0)
        for d in range(DOCS):
            value = jnp.where(starts[d] // (T * ZN) == group, 0.0, value)
        return value

    def conv(xs, w, rows):
        return (
            w[0:1] * xs[8 : 8 + rows, :] + w[1:2] * xs[7 : 7 + rows, :] + w[2:3] * xs[6 : 6 + rows, :]
        ).astype(BF16)

    def head_rows(h):
        return pl.ds(pl.multiple_of(h * F, F), F)

    def head_cols(h):
        return pl.ds(pl.multiple_of(h * HD, HD), HD)

    xq[0:8, :] = jnp.zeros((8, HEADS * F), F32)
    xk[0:8, :] = jnp.zeros((8, HEADS * F), F32)
    xq[8:, :] = q_ref[...].astype(F32)
    xk[8:, :] = k_ref[...].astype(F32)
    qc[...] = conv(xq, wq_ref[...], T)
    kc[...] = conv(xk, wk_ref[...], T)

    def turn(tokens):
        q_turned = qc[0:tokens, :].astype(F32).T
        k_turned = kc[0:tokens, :].astype(F32).T
        qt[:, 0:tokens] = q_turned.astype(BF16)
        kt[:, 0:tokens] = k_turned.astype(BF16)
        uq[:, 0:tokens] = q_turned * (0.5 * use_prev[:, 0:tokens])
        uk[:, 0:tokens] = k_turned * (0.5 * use_next[:, 0:tokens])

    turn(T)
    for c in loads[5:]:
        c.wait()

    def value_head(h, _):
        cols = head_cols(h)
        xv[h, 0:8, :] = jnp.zeros((8, HD), F32)
        xv[h, 8:, :] = v_ref[:, cols].astype(F32)
        vc[h] = conv(xv.at[h], wv_ref[:, cols], T)
        return 0

    lax.fori_loop(0, HEADS, value_head, 0)

    pl.semaphore_wait(barrier, len(greeted))

    def remote(src, dst, ss, rs, peer):
        return pltpu.make_async_remote_copy(
            src_ref=src, dst_ref=dst, send_sem=ss, recv_sem=rs, device_id=peer, device_id_type=MESH
        )

    halos = [
        remote(ref.at[T - 16 :, :], dst, halo_ss.at[i], halo_rs.at[i], {"ctx": after})
        for i, (ref, dst) in enumerate([(q_ref, halo_q), (k_ref, halo_k), (v_ref, halo_v)])
    ]
    for c in halos:
        c.start()
    for c in halos:
        c.wait_recv()
    inside = jnp.where(me > 0, 1.0, 0.0)
    xq[0:8, :] = halo_q[...].astype(F32)[8:16] * inside
    xk[0:8, :] = halo_k[...].astype(F32)[8:16] * inside
    qc[0:16, :] = conv(xq, wq_ref[...], 16)
    kc[0:16, :] = conv(xk, wk_ref[...], 16)
    turn(128)

    def a_copy(tail, got, phase, h):
        return remote(
            tail.at[h], got.at[z], a_ss.at[phase, h], a_rs.at[phase, z], z_peer(h)
        )

    def a_arrival(tail, got, phase, zz):
        return remote(
            tail.at[zz], got.at[zz], a_ss.at[phase, zz], a_rs.at[phase, zz], z_peer(zz)
        )

    def b_copy(send, take, phase, zz):
        return remote(send.at[zz], take.at[z], b_ss.at[phase, zz], b_rs.at[phase, z], z_peer(zz))

    def b_arrival(send, take, phase, h):
        return remote(send.at[h], take.at[h], b_ss.at[phase, h], b_rs.at[phase, h], z_peer(h))

    def tail_head(h):
        cols = head_cols(h)
        xv[h, 0:8, :] = halo_v[:, cols].astype(F32)[8:16] * inside
        vc[h, 0:16, :] = conv(xv.at[h], wv_ref[:, cols], 16)
        value = vc[h]
        put_features(phik, h, uk[head_rows(h), :], use_next)
        tail1[h] = dot(phik[h], value, 1, 0).astype(BF16)

    def tail_step(h, _):
        tail_head(h)

        @pl.when(h != z)
        def _():
            a_copy(tail1, got1, 0, h).start()

        return 0

    lax.fori_loop(0, HEADS, tail_step, 0)
    got1[z] = tail1[z]

    lane_head = lax.broadcasted_iota(jnp.int32, (1, HEADS * F), 1) // F

    def inner_step(h, _):
        chosen = jnp.where(lane_head == h, 0.25, 0.0).astype(BF16)
        scores = dot(qc[...] * chosen, kc[...], 1, 1)
        m = mask_ref[...]
        kernel_h = (m * (1.0 + scores + 0.5 * scores * scores)).astype(BF16)
        kern[h] = kernel_h
        saved[h] = m * (1.0 + scores)
        inner[h] = dot(kernel_h, vc[h], 1, 0)
        put_features(phiq, h, uq[head_rows(h), :], use_prev)
        return 0

    lax.fori_loop(0, HEADS, inner_step, 0)

    def scan(tail, got, tot, ytot, send, take, phase, reverse):
        def wait_a(j, _):
            a_arrival(tail, got, phase, (z + j) % ZN).wait_recv()
            return 0

        lax.fori_loop(1, ZN, wait_a, 0)
        order = range(ZN - 1, -1, -1) if reverse else range(ZN)
        running = jnp.zeros((ROWS, HD), F32)
        keeps = {}
        for i in order:
            keeps[i] = keep_of(y * ZN + i)
            running = got[i].astype(F32) + keeps[i] * running
        tot[...] = running.astype(BF16)
        ytot[y] = running.astype(BF16)

        def y_copy(j):
            yy = (y + j) % n_y
            return remote(tot, ytot.at[y], y_ss.at[phase, yy], y_rs.at[phase, y], y_peer(yy))

        def y_arrival(j):
            yy = (y + j) % n_y
            return remote(tot, ytot.at[yy], y_ss.at[phase, yy], y_rs.at[phase, yy], y_peer(yy))

        for j in range(1, n_y):
            y_copy(j).start()
        for j in range(1, n_y):
            y_arrival(j).wait_recv()
        carry = jnp.zeros((ROWS, HD), F32)
        for g in range(n_y - 1, 0, -1) if reverse else range(n_y - 1):
            counts = jnp.where(g > y if reverse else g < y, 1.0, 0.0)
            onward = ytot[g].astype(F32) + keep_group(g) * carry
            carry = counts * onward + (1.0 - counts) * carry
        running = carry
        for i in order:
            send[i] = running.astype(BF16)
            running = got[i].astype(F32) + keeps[i] * running

        for away in (4, 3, 5, 2, 6, 1, 7):
            b_copy(send, take, phase, (z + away) % ZN).start()
        take[z] = send[z]

    scan(tail1, got1, tot1, ytot1, send1, inc, 0, False)

    def forward_head(h):
        cols = head_cols(h)
        attended = inner[h] + dot(phiq[h], inc[h], 0, 0)
        r = lax.rsqrt(jnp.mean(attended * attended, axis=-1, keepdims=True) + EPS)
        normed = attended * r
        gains = gain_ref[:, cols]
        mixed_ref[:, cols] = (normed * gains).astype(BF16)
        upstream = og_ref[:, cols].astype(F32)
        local[h, 3:4, :] = jnp.sum(upstream * normed, axis=0, keepdims=True)
        pulled = upstream * gains
        along = jnp.mean(pulled * normed, axis=-1, keepdims=True)
        grad = ((pulled - normed * along) * r).astype(BF16)
        ga_ref[h] = grad
        tail2[h] = dot(phiq[h], grad, 1, 0).astype(BF16)

    local[...] = jnp.zeros(local.shape, F32)

    def forward_step(h, _):
        @pl.when(h != z)
        def _():
            b_arrival(send1, inc, 0, h).wait_recv()

        forward_head(h)

        @pl.when(h != z)
        def _():
            a_copy(tail2, got2, 1, h).start()

        return 0

    lax.fori_loop(0, HEADS, forward_step, 0)
    got2[z] = tail2[z]

    store_mixed = pltpu.make_async_copy(mixed_ref, mixed_hbm, out_s.at[0])
    store_mixed.start()

    def backward_step(h, _):
        grad = ga_ref[h]
        grad_scores = (dot(grad, vc[h], 1, 1) * saved[h]).astype(BF16)
        rows = head_rows(h)
        grad_phi = dot(inc[h], grad, 1, 1)
        gqt[rows, :] = 0.25 * dot(kt[rows, :], grad_scores, 1, 1) + pull_features(
            grad_phi, uq[rows, :], use_prev
        )
        gkt[rows, :] = 0.25 * dot(qt[rows, :], grad_scores, 1, 0)
        gvs[h, 0:T, :] = dot(kern[h], grad, 0, 0)
        return 0

    lax.fori_loop(0, HEADS, backward_step, 0)

    scan(tail2, got2, tot2, ytot2, send2, outg, 1, True)

    def taps(g, x):
        return [jnp.sum(g * x[8 - j : 8 - j + T], axis=0, keepdims=True) for j in range(3)]

    def last_head(h):
        rows = head_rows(h)
        later = outg[h]
        grad_phi = dot(later, vc[h], 1, 1)
        gkt[rows, :] = gkt[rows, :] + pull_features(grad_phi, uk[rows, :], use_next)
        g = gvs[h, 0:T, :] + dot(phik[h], later, 0, 0)
        gvs[h, 0:T, :] = g
        for j in range(3):
            local[h, j : j + 1, :] = jnp.sum(
                g * xv[h, 8 - j : 8 - j + T, :], axis=0, keepdims=True
            )

    def last_step(h, _):
        @pl.when(h != z)
        def _():
            b_arrival(send2, outg, 1, h).wait_recv()

        last_head(h)
        return 0

    lax.fori_loop(0, HEADS, last_step, 0)
    gq = gqt[...].T
    gk = gkt[...].T
    gqs[0:T, :] = gq
    gks[0:T, :] = gk

    backs = [
        remote(src, dst, back_ss.at[i], back_rs.at[i], {"ctx": before})
        for i, (src, dst) in enumerate(
            [
                (gqs.at[0:8, :], back_q),
                (gks.at[0:8, :], back_k),
                (gvs.at[:, 0:8, :], back_v),
            ]
        )
    ]
    for c in backs:
        c.start()

    for j in range(3):
        local[0, 4 + j : 5 + j, :] = jnp.sum(gq * xq[8 - j : 8 - j + T, :], axis=0, keepdims=True)
        local[1, 4 + j : 5 + j, :] = jnp.sum(gk * xk[8 - j : 8 - j + T, :], axis=0, keepdims=True)

    halves[0, 16:24, :] = local[0]
    halves[1, 16:24, :] = local[1]
    for h in range(HEADS):
        halves[h // 4, 4 * (h % 4) : 4 * (h % 4) + 4, :] = local[h, 0:4, :]
    to_core = remote(halves.at[1 - core], red_c, rc_ss.at[0], rc_rs.at[0], other)
    to_core.start()
    to_core.wait_recv()
    mine = halves[core] + red_c[...]
    one_xy[...] = mine
    here = x * n_y + y
    red_xy[here] = mine
    to_plane = [
        (
            remote(one_xy, red_xy.at[here], rxy_ss.at[slot], rxy_rs.at[here], peer),
            remote(one_xy, red_xy.at[slot], rxy_ss.at[slot], rxy_rs.at[slot], peer),
        )
        for slot, peer in plane
    ]
    for c, _ in to_plane:
        c.start()

    for c in backs:
        c.wait_recv()
    inside_next = jnp.where(me < n_ctx - 1, 1.0, 0.0)
    gqs[T : T + 8, :] = back_q[...] * inside_next
    gks[T : T + 8, :] = back_k[...] * inside_next
    for c in backs:
        c.wait_send()
    gvs[:, T : T + 8, :] = back_v[...] * inside_next

    def conv_back(g, w):
        return (w[0:1] * g[0:T] + w[1:2] * g[1 : 1 + T] + w[2:3] * g[2 : 2 + T]).astype(BF16)

    gq_ref[...] = conv_back(gqs, wq_ref[...])
    gk_ref[...] = conv_back(gks, wk_ref[...])

    def value_step(h, _):
        cols = head_cols(h)
        w = wv_ref[:, cols]
        gv_ref[:, cols] = (
            w[0:1] * gvs[h, 0:T, :]
            + w[1:2] * gvs[h, 1 : 1 + T, :]
            + w[2:3] * gvs[h, 2 : 2 + T, :]
        ).astype(BF16)
        return 0

    lax.fori_loop(0, HEADS, value_step, 0)
    stores = [store_mixed]
    for i, (src, dst) in enumerate([(gq_ref, gq_hbm), (gk_ref, gk_hbm), (gv_ref, gv_hbm)]):
        stores.append(pltpu.make_async_copy(src, dst, out_s.at[1 + i]))
        stores[-1].start()

    for _, c in to_plane:
        c.wait_recv()
    mine = jnp.sum(red_xy[...], axis=0)
    one_z[...] = mine
    red_z[z] = mine

    def rz(zz, slot):
        return remote(one_z, red_z.at[slot], rz_ss.at[zz], rz_rs.at[slot], z_peer(zz))

    for away in (4, 3, 5, 2, 6, 1, 7):
        rz((z + away) % ZN, z).start()
    for j in range(1, ZN):
        rz((z + j) % ZN, (z + j) % ZN).wait_recv()
    mine = jnp.sum(red_z[...], axis=0)
    one_c[core] = mine
    back_to_core = remote(one_c.at[core], one_c.at[core], ac_ss.at[0], ac_rs.at[0], other)
    back_to_core.start()
    remote(one_c.at[core], one_c.at[1 - core], ac_ss.at[0], ac_rs.at[0], other).wait_recv()
    sums_ref[...] = one_c[...]

    for c in stores:
        c.wait()
    for c in halos:
        c.wait_send()

    def left(j, _):
        zz = (z + j) % ZN
        a_copy(tail1, got1, 0, zz).wait_send()
        a_copy(tail2, got2, 1, zz).wait_send()
        b_copy(send1, inc, 0, zz).wait_send()
        b_copy(send2, outg, 1, zz).wait_send()
        rz(zz, z).wait_send()
        return 0

    lax.fori_loop(1, ZN, left, 0)
    for j in range(1, n_y):
        yy = (y + j) % n_y
        remote(tot1, ytot1.at[y], y_ss.at[0, yy], y_rs.at[0, y], y_peer(yy)).wait_send()
        remote(tot2, ytot2.at[y], y_ss.at[1, yy], y_rs.at[1, y], y_peer(yy)).wait_send()
    for c, _ in to_plane:
        c.wait_send()
    to_core.wait_send()
    back_to_core.wait_send()


def writer(mixed, gq, gk, gv, sums, mixed_o, gq_o, gk_o, gv_o, gwq_o, gwk_o, gwv_o, gg_o, gwq, gwk, gwv, gg, sems):
    copies = [
        pltpu.make_async_copy(src, dst, sems.at[i])
        for i, (src, dst) in enumerate(
            [
                (mixed, mixed_o),
                (gv, gv_o),
                (gq, gq_o),
                (gk, gk_o),
                (gwq, gwq_o),
                (gwk, gwk_o),
                (gwv, gwv_o),
                (gg, gg_o),
            ]
        )
    ]
    for c in copies[:4]:
        c.start()
    gwq[...] = sums[0, 20:23, :]
    gwk[...] = sums[1, 20:23, :]
    for h in range(HEADS):
        base = 4 * (h % 4)
        gwv[:, h * HD : (h + 1) * HD] = sums[h // 4, base : base + 3, :]
        gg[:, h * HD : (h + 1) * HD] = sums[h // 4, base + 3 : base + 4, :]
    for c in copies[4:]:
        c.start()
    for c in copies:
        c.wait()


def solution(mesh):
    n_dp, n_ctx = mesh.shape["dp"], mesh.shape["ctx"]
    n_y = n_ctx // ZN
    wide = HEADS * HD
    thin = HEADS * F

    def shards(q, k, v, wq, wk, wv, gain, lens, og):
        vmem = pl.BlockSpec(memory_space=pltpu.VMEM)
        state = (ROWS, HD)
        hbm = pl.BlockSpec(memory_space=pltpu.HBM)
        scratch = [
            pltpu.VMEM((T, wide), BF16),
            pltpu.VMEM((T, thin), BF16),
            pltpu.VMEM((T, thin), BF16),
            pltpu.VMEM((T, wide), BF16),
            pltpu.SemaphoreType.DMA((4,)),
            pltpu.SMEM((1, DOCS), jnp.int32),
            pltpu.VMEM((T, thin), BF16),
            pltpu.VMEM((T, thin), BF16),
            pltpu.VMEM((T, wide), BF16),
            pltpu.VMEM((T, wide), BF16),
            pltpu.VMEM((3, thin), F32),
            pltpu.VMEM((3, thin), F32),
            pltpu.VMEM((3, wide), F32),
            pltpu.VMEM((1, wide), F32),
            pltpu.VMEM((T + 8, thin), F32),
            pltpu.VMEM((T + 8, thin), F32),
            pltpu.VMEM((HEADS, T + 8, HD), F32),
            pltpu.VMEM((T, thin), BF16),
            pltpu.VMEM((T, thin), BF16),
            pltpu.VMEM((thin, T), BF16),
            pltpu.VMEM((thin, T), BF16),
            pltpu.VMEM((thin, T), F32),
            pltpu.VMEM((thin, T), F32),
            pltpu.VMEM((HEADS, T, HD), BF16),
            pltpu.VMEM((T, T), F32),
            pltpu.VMEM((HEADS, T, T), BF16),
            pltpu.VMEM((HEADS, T, T), F32),
            pltpu.VMEM((HEADS, T, HD), F32),
            pltpu.VMEM((HEADS, ROWS, T), BF16),
            pltpu.VMEM((HEADS, ROWS, T), BF16),
            pltpu.VMEM((HEADS, T, HD), BF16),
            pltpu.VMEM((HEADS, T + 8, HD), F32),
            pltpu.VMEM((thin, T), F32),
            pltpu.VMEM((thin, T), F32),
            pltpu.VMEM((T + 8, thin), F32),
            pltpu.VMEM((T + 8, thin), F32),
            pltpu.VMEM((HEADS, 8, HD), F32),
            pltpu.VMEM((16, thin), BF16),
            pltpu.VMEM((16, thin), BF16),
            pltpu.VMEM((16, wide), BF16),
            pltpu.VMEM((8, thin), F32),
            pltpu.VMEM((8, thin), F32),
            pltpu.VMEM((HEADS, 8, HD), F32),
        ]
        for _ in range(2):
            scratch += [
                pltpu.VMEM((HEADS,) + state, BF16),
                pltpu.VMEM((ZN,) + state, BF16),
                pltpu.VMEM(state, BF16),
                pltpu.VMEM((n_y,) + state, BF16),
                pltpu.VMEM((ZN,) + state, BF16),
                pltpu.VMEM((HEADS,) + state, BF16),
            ]
        half = (24, HD)
        scratch += [
            pltpu.VMEM((2,) + half, F32),
            pltpu.VMEM(half, F32),
            pltpu.VMEM((n_dp // 2 * n_y,) + half, F32),
            pltpu.VMEM(half, F32),
            pltpu.VMEM((ZN,) + half, F32),
            pltpu.VMEM(half, F32),
            pltpu.VMEM((2,) + half, F32),
            pltpu.SemaphoreType.DMA((9,)),
        ]
        dma = pltpu.SemaphoreType.DMA
        for counts in ((3,), (3,), (2, ZN), (2, n_y), (2, ZN), (1,), (n_dp // 2 * n_y,), (ZN,), (1,)):
            scratch += [dma(counts), dma(counts)]
        outs = pl.pallas_call(
            functools.partial(kernel, n_dp, n_ctx),
            out_shape=(
                jax.ShapeDtypeStruct((T, wide), BF16),
                jax.ShapeDtypeStruct((T, thin), BF16),
                jax.ShapeDtypeStruct((T, thin), BF16),
                jax.ShapeDtypeStruct((T, wide), BF16),
                jax.ShapeDtypeStruct((2,) + half, F32),
            ),
            in_specs=[hbm] * 9,
            out_specs=(hbm,) * 4 + (vmem,),
            scratch_shapes=scratch,
            compiler_params=pltpu.CompilerParams(
                collective_id=0, has_side_effects=True, vmem_limit_bytes=64 * 2**20 - 2**18
            ),
        )(lens, q[0], k[0], v[0], og[0], wq, wk, wv, gain[None])
        outs = pl.pallas_call(
            writer,
            out_shape=(
                jax.ShapeDtypeStruct((T, wide), BF16),
                jax.ShapeDtypeStruct((T, thin), BF16),
                jax.ShapeDtypeStruct((T, thin), BF16),
                jax.ShapeDtypeStruct((T, wide), BF16),
                jax.ShapeDtypeStruct((3, thin), F32),
                jax.ShapeDtypeStruct((3, thin), F32),
                jax.ShapeDtypeStruct((3, wide), F32),
                jax.ShapeDtypeStruct((1, wide), F32),
            ),
            in_specs=[hbm] * 4 + [vmem],
            out_specs=(hbm,) * 8,
            scratch_shapes=[
                pltpu.VMEM((3, thin), F32),
                pltpu.VMEM((3, thin), F32),
                pltpu.VMEM((3, wide), F32),
                pltpu.VMEM((1, wide), F32),
                pltpu.SemaphoreType.DMA((8,)),
            ],
        )(*outs)
        mixed, gq, gk, gv, gwq, gwk, gwv, gg = outs
        return mixed[None], gq[None], gk[None], gv[None], gwq, gwk, gwv, gg[0]

    tokens = P("dp", "ctx", None)
    return jax.shard_map(
        shards,
        mesh=mesh,
        in_specs=(tokens, tokens, tokens, P(), P(), P(), P(), P("dp", None), tokens),
        out_specs=(tokens, tokens, tokens, tokens, P(), P(), P(), P()),
        check_vma=False,
    )
```

```python
import functools

import jax
import jax.numpy as jnp
from jax import lax
from jax.experimental import pallas as pl
from jax.experimental.pallas import tpu as pltpu
from jax.sharding import PartitionSpec as P

HEADS = 8
F = 16
HD = 128
T = 256
DOCS = 8
ROWS = 160
ZN = 8
EPS = 1e-06
MESH = pl.DeviceIdType.MESH
F32 = jnp.float32
BF16 = jnp.bfloat16


def dot(a, b, ca, cb):
    return lax.dot_general(a, b, (((ca,), (cb,)), ((), ())), preferred_element_type=F32)


def turned(u, d):
    return pltpu.roll(u, F - d, 0) if d else u


def put_features(out, h, u, ones):
    out[h, 0:16, :] = (u * u * (0.5**0.5)).astype(BF16)
    for d in range(1, 8):
        out[h, 16 * d : 16 * d + 16, :] = (u * turned(u, d)).astype(BF16)
    out[h, 128:144, :] = u.astype(BF16)
    rest = jnp.where(lax.broadcasted_iota(jnp.int32, (8, T), 0) == 0, ones, 0.0)
    out[h, 144:160, :] = jnp.concatenate([u[0:8] * u[8:16], rest], axis=0).astype(BF16)


def pull_features(g, u, ones):
    total = g[128:144] * ones + (2.0 * 0.5**0.5) * g[0:16] * u
    for d in range(1, 8):
        own = g[16 * d : 16 * d + 16]
        total = total + own * turned(u, d) + pltpu.roll(own * u, d, 0)
    half = g[144:152]
    total = total + jnp.concatenate([half * u[8:16], half * u[0:8]], axis=0)
    return 0.5 * total


def kernel(
    n_dp,
    n_ctx,
    lens_hbm,
    q_hbm,
    k_hbm,
    v_hbm,
    og_hbm,
    wq_hbm,
    wk_hbm,
    wv_hbm,
    gain_hbm,
    mixed_hbm,
    gq_hbm,
    gk_hbm,
    gv_hbm,
    sums_ref,
    mixed_ref,
    gq_ref,
    gk_ref,
    gv_ref,
    out_s,
    lens,
    q_ref,
    k_ref,
    v_ref,
    og_ref,
    wq_ref,
    wk_ref,
    wv_ref,
    gain_ref,
    xq,
    xk,
    xv,
    qc,
    kc,
    qt,
    kt,
    uq,
    uk,
    vc,
    mask_ref,
    kern,
    saved,
    inner,
    phiq,
    phik,
    ga_ref,
    gvs,
    gqt,
    gkt,
    gqs,
    gks,
    local,
    halo_q,
    halo_k,
    halo_v,
    back_q,
    back_k,
    back_v,
    tail1,
    got1,
    tot1,
    ytot1,
    send1,
    inc,
    tail2,
    got2,
    tot2,
    ytot2,
    send2,
    outg,
    halves,
    red_c,
    red_xy,
    one_xy,
    red_z,
    one_z,
    one_c,
    in_s,
    halo_ss,
    halo_rs,
    back_ss,
    back_rs,
    a_ss,
    a_rs,
    y_ss,
    y_rs,
    b_ss,
    b_rs,
    rc_ss,
    rc_rs,
    rxy_ss,
    rxy_rs,
    rz_ss,
    rz_rs,
    ac_ss,
    ac_rs,
):
    n_y = n_ctx // ZN
    me = lax.axis_index("ctx")
    dp = lax.axis_index("dp")
    n_x = n_dp // 2
    core = dp % 2
    x = dp // 2
    y = me // ZN
    z = me % ZN
    after = (me + 1) % n_ctx
    before = (me + n_ctx - 1) % n_ctx

    def z_peer(zz):
        return {"ctx": y * ZN + zz}

    def y_peer(yy):
        return {"ctx": yy * ZN + z}

    barrier = pltpu.get_barrier_semaphore()
    greeted = [z_peer((z + j) % ZN) for j in range(1, ZN)]
    other = {"dp": dp + 1 - 2 * core}
    plane = []
    for j in range(1, n_x * n_y):
        xx = (x + j // n_y) % n_x
        yy = (y + j % n_y) % n_y
        plane.append((xx * n_y + yy, {"dp": xx * 2 + core, "ctx": yy * ZN + z}))
    greeted += [peer for _, peer in plane]
    greeted += [other, {"ctx": after}, {"ctx": before}]
    for peer in greeted:
        pl.semaphore_signal(barrier, inc=1, device_id=peer, device_id_type=MESH)

    loads = [
        pltpu.make_async_copy(src, dst, in_s.at[i])
        for i, (src, dst) in enumerate(
            [
                (lens_hbm, lens),
                (q_hbm, q_ref),
                (k_hbm, k_ref),
                (wq_hbm, wq_ref),
                (wk_hbm, wk_ref),
                (v_hbm, v_ref),
                (wv_hbm, wv_ref),
                (gain_hbm, gain_ref),
                (og_hbm, og_ref),
            ]
        )
    ]
    for c in loads:
        c.start()
    for c in loads[:5]:
        c.wait()

    starts = []
    total = jnp.int32(0)
    for d in range(DOCS):
        starts.append(total)
        total = total + lens[0, d]
    first = me * T

    def doc_of(position):
        found = jnp.where(position >= starts[0], 1, 0)
        for d in range(1, DOCS):
            found = found + jnp.where(position >= starts[d], 1, 0)
        return found

    row_pos = first + lax.broadcasted_iota(jnp.int32, (1, T), 1)
    col_pos = first + lax.broadcasted_iota(jnp.int32, (T, 1), 0)
    row_doc, col_doc = doc_of(row_pos), doc_of(col_pos)
    prev_doc, last_doc = doc_of(first - 1), doc_of(first + T - 1)
    use_prev = jnp.where(row_doc == prev_doc, 1.0, 0.0)
    use_next = jnp.where(row_doc == last_doc, 1.0, 0.0)
    mask_ref[...] = jnp.where((row_pos <= col_pos) & (row_doc == col_doc), 1.0, 0.0)

    def keep_of(block):
        value = jnp.float32(1.0)
        for d in range(DOCS):
            value = jnp.where(starts[d] // T == block, 0.0, value)
        return value

    def keep_group(group):
        value = jnp.float32(1.0)
        for d in range(DOCS):
            value = jnp.where(starts[d] // (T * ZN) == group, 0.0, value)
        return value

    def conv(xs, w, rows):
        return (
            w[0:1] * xs[8 : 8 + rows, :] + w[1:2] * xs[7 : 7 + rows, :] + w[2:3] * xs[6 : 6 + rows, :]
        ).astype(BF16)

    def head_rows(h):
        return pl.ds(pl.multiple_of(h * F, F), F)

    def head_cols(h):
        return pl.ds(pl.multiple_of(h * HD, HD), HD)

    xq[0:8, :] = jnp.zeros((8, HEADS * F), F32)
    xk[0:8, :] = jnp.zeros((8, HEADS * F), F32)
    xq[8:, :] = q_ref[...].astype(F32)
    xk[8:, :] = k_ref[...].astype(F32)
    qc[...] = conv(xq, wq_ref[...], T)
    kc[...] = conv(xk, wk_ref[...], T)

    def turn(tokens):
        q_turned = qc[0:tokens, :].astype(F32).T
        k_turned = kc[0:tokens, :].astype(F32).T
        qt[:, 0:tokens] = q_turned.astype(BF16)
        kt[:, 0:tokens] = k_turned.astype(BF16)
        uq[:, 0:tokens] = q_turned * (0.5 * use_prev[:, 0:tokens])
        uk[:, 0:tokens] = k_turned * (0.5 * use_next[:, 0:tokens])

    turn(T)
    for c in loads[5:]:
        c.wait()

    def value_head(h, _):
        cols = head_cols(h)
        xv[h, 0:8, :] = jnp.zeros((8, HD), F32)
        xv[h, 8:, :] = v_ref[:, cols].astype(F32)
        vc[h] = conv(xv.at[h], wv_ref[:, cols], T)
        return 0

    lax.fori_loop(0, HEADS, value_head, 0)

    pl.semaphore_wait(barrier, len(greeted))

    def remote(src, dst, ss, rs, peer):
        return pltpu.make_async_remote_copy(
            src_ref=src, dst_ref=dst, send_sem=ss, recv_sem=rs, device_id=peer, device_id_type=MESH
        )

    halos = [
        remote(ref.at[T - 16 :, :], dst, halo_ss.at[i], halo_rs.at[i], {"ctx": after})
        for i, (ref, dst) in enumerate([(q_ref, halo_q), (k_ref, halo_k), (v_ref, halo_v)])
    ]
    for c in halos:
        c.start()
    for c in halos:
        c.wait_recv()
    inside = jnp.where(me > 0, 1.0, 0.0)
    xq[0:8, :] = halo_q[...].astype(F32)[8:16] * inside
    xk[0:8, :] = halo_k[...].astype(F32)[8:16] * inside
    qc[0:16, :] = conv(xq, wq_ref[...], 16)
    kc[0:16, :] = conv(xk, wk_ref[...], 16)
    turn(128)

    def a_copy(tail, got, phase, h):
        return remote(
            tail.at[h], got.at[z], a_ss.at[phase, h], a_rs.at[phase, z], z_peer(h)
        )

    def a_arrival(tail, got, phase, zz):
        return remote(
            tail.at[zz], got.at[zz], a_ss.at[phase, zz], a_rs.at[phase, zz], z_peer(zz)
        )

    def b_copy(send, take, phase, zz):
        return remote(send.at[zz], take.at[z], b_ss.at[phase, zz], b_rs.at[phase, z], z_peer(zz))

    def b_arrival(send, take, phase, h):
        return remote(send.at[h], take.at[h], b_ss.at[phase, h], b_rs.at[phase, h], z_peer(h))

    def tail_head(h):
        cols = head_cols(h)
        xv[h, 0:8, :] = halo_v[:, cols].astype(F32)[8:16] * inside
        vc[h, 0:16, :] = conv(xv.at[h], wv_ref[:, cols], 16)
        value = vc[h]
        put_features(phik, h, uk[head_rows(h), :], use_next)
        tail1[h] = dot(phik[h], value, 1, 0).astype(BF16)

    def tail_step(h, _):
        tail_head(h)

        @pl.when(h != z)
        def _():
            a_copy(tail1, got1, 0, h).start()

        return 0

    lax.fori_loop(0, HEADS, tail_step, 0)
    got1[z] = tail1[z]

    lane_head = lax.broadcasted_iota(jnp.int32, (1, HEADS * F), 1) // F

    def inner_step(h, _):
        chosen = jnp.where(lane_head == h, 0.25, 0.0).astype(BF16)
        scores = dot(qc[...] * chosen, kc[...], 1, 1)
        m = mask_ref[...]
        kernel_h = (m * (1.0 + scores + 0.5 * scores * scores)).astype(BF16)
        kern[h] = kernel_h
        saved[h] = m * (1.0 + scores)
        inner[h] = dot(kernel_h, vc[h], 1, 0)
        put_features(phiq, h, uq[head_rows(h), :], use_prev)
        return 0

    lax.fori_loop(0, HEADS, inner_step, 0)

    def scan(tail, got, tot, ytot, send, take, phase, reverse):
        def wait_a(j, _):
            a_arrival(tail, got, phase, (z + j) % ZN).wait_recv()
            return 0

        lax.fori_loop(1, ZN, wait_a, 0)
        order = range(ZN - 1, -1, -1) if reverse else range(ZN)
        running = jnp.zeros((ROWS, HD), F32)
        keeps = {}
        for i in order:
            keeps[i] = keep_of(y * ZN + i)
            running = got[i].astype(F32) + keeps[i] * running
        tot[...] = running.astype(BF16)
        ytot[y] = running.astype(BF16)

        def y_copy(j):
            yy = (y + j) % n_y
            return remote(tot, ytot.at[y], y_ss.at[phase, yy], y_rs.at[phase, y], y_peer(yy))

        def y_arrival(j):
            yy = (y + j) % n_y
            return remote(tot, ytot.at[yy], y_ss.at[phase, yy], y_rs.at[phase, yy], y_peer(yy))

        for j in range(1, n_y):
            y_copy(j).start()
        for j in range(1, n_y):
            y_arrival(j).wait_recv()
        carry = jnp.zeros((ROWS, HD), F32)
        for g in range(n_y - 1, 0, -1) if reverse else range(n_y - 1):
            counts = jnp.where(g > y if reverse else g < y, 1.0, 0.0)
            onward = ytot[g].astype(F32) + keep_group(g) * carry
            carry = counts * onward + (1.0 - counts) * carry
        running = carry
        for i in order:
            send[i] = running.astype(BF16)
            running = got[i].astype(F32) + keeps[i] * running

        for away in (4, 3, 5, 2, 6, 1, 7):
            b_copy(send, take, phase, (z + away) % ZN).start()
        take[z] = send[z]

    scan(tail1, got1, tot1, ytot1, send1, inc, 0, False)

    def forward_head(h):
        cols = head_cols(h)
        attended = inner[h] + dot(phiq[h], inc[h], 0, 0)
        r = lax.rsqrt(jnp.mean(attended * attended, axis=-1, keepdims=True) + EPS)
        normed = attended * r
        gains = gain_ref[:, cols]
        mixed_ref[:, cols] = (normed * gains).astype(BF16)
        upstream = og_ref[:, cols].astype(F32)
        local[h, 3:4, :] = jnp.sum(upstream * normed, axis=0, keepdims=True)
        pulled = upstream * gains
        along = jnp.mean(pulled * normed, axis=-1, keepdims=True)
        grad = ((pulled - normed * along) * r).astype(BF16)
        ga_ref[h] = grad
        tail2[h] = dot(phiq[h], grad, 1, 0).astype(BF16)

    local[...] = jnp.zeros(local.shape, F32)

    def forward_step(h, _):
        @pl.when(h != z)
        def _():
            b_arrival(send1, inc, 0, h).wait_recv()

        forward_head(h)

        @pl.when(h != z)
        def _():
            a_copy(tail2, got2, 1, h).start()

        return 0

    lax.fori_loop(0, HEADS, forward_step, 0)
    got2[z] = tail2[z]

    store_mixed = pltpu.make_async_copy(mixed_ref, mixed_hbm, out_s.at[0])
    store_mixed.start()

    def backward_step(h, _):
        grad = ga_ref[h]
        grad_scores = (dot(grad, vc[h], 1, 1) * saved[h]).astype(BF16)
        rows = head_rows(h)
        grad_phi = dot(inc[h], grad, 1, 1)
        gqt[rows, :] = 0.25 * dot(kt[rows, :], grad_scores, 1, 1) + pull_features(
            grad_phi, uq[rows, :], use_prev
        )
        gkt[rows, :] = 0.25 * dot(qt[rows, :], grad_scores, 1, 0)
        gvs[h, 0:T, :] = dot(kern[h], grad, 0, 0)
        return 0

    lax.fori_loop(0, HEADS, backward_step, 0)

    scan(tail2, got2, tot2, ytot2, send2, outg, 1, True)

    def taps(g, x):
        return [jnp.sum(g * x[8 - j : 8 - j + T], axis=0, keepdims=True) for j in range(3)]

    def last_head(h):
        rows = head_rows(h)
        later = outg[h]
        grad_phi = dot(later, vc[h], 1, 1)
        gkt[rows, :] = gkt[rows, :] + pull_features(grad_phi, uk[rows, :], use_next)
        g = gvs[h, 0:T, :] + dot(phik[h], later, 0, 0)
        gvs[h, 0:T, :] = g
        for j in range(3):
            local[h, j : j + 1, :] = jnp.sum(
                g * xv[h, 8 - j : 8 - j + T, :], axis=0, keepdims=True
            )

    def last_step(h, _):
        @pl.when(h != z)
        def _():
            b_arrival(send2, outg, 1, h).wait_recv()

        last_head(h)
        return 0

    lax.fori_loop(0, HEADS, last_step, 0)
    gq = gqt[...].T
    gk = gkt[...].T
    gqs[0:T, :] = gq
    gks[0:T, :] = gk

    backs = [
        remote(src, dst, back_ss.at[i], back_rs.at[i], {"ctx": before})
        for i, (src, dst) in enumerate(
            [
                (gqs.at[0:8, :], back_q),
                (gks.at[0:8, :], back_k),
                (gvs.at[:, 0:8, :], back_v),
            ]
        )
    ]
    for c in backs:
        c.start()

    for j in range(3):
        local[0, 4 + j : 5 + j, :] = jnp.sum(gq * xq[8 - j : 8 - j + T, :], axis=0, keepdims=True)
        local[1, 4 + j : 5 + j, :] = jnp.sum(gk * xk[8 - j : 8 - j + T, :], axis=0, keepdims=True)

    halves[0, 16:24, :] = local[0]
    halves[1, 16:24, :] = local[1]
    for h in range(HEADS):
        halves[h // 4, 4 * (h % 4) : 4 * (h % 4) + 4, :] = local[h, 0:4, :]
    to_core = remote(halves.at[1 - core], red_c, rc_ss.at[0], rc_rs.at[0], other)
    to_core.start()
    to_core.wait_recv()
    mine = halves[core] + red_c[...]
    one_xy[...] = mine
    here = x * n_y + y
    red_xy[here] = mine
    to_plane = [
        (
            remote(one_xy, red_xy.at[here], rxy_ss.at[slot], rxy_rs.at[here], peer),
            remote(one_xy, red_xy.at[slot], rxy_ss.at[slot], rxy_rs.at[slot], peer),
        )
        for slot, peer in plane
    ]
    for c, _ in to_plane:
        c.start()

    for c in backs:
        c.wait_recv()
    inside_next = jnp.where(me < n_ctx - 1, 1.0, 0.0)
    gqs[T : T + 8, :] = back_q[...] * inside_next
    gks[T : T + 8, :] = back_k[...] * inside_next
    for c in backs:
        c.wait_send()
    gvs[:, T : T + 8, :] = back_v[...] * inside_next

    def conv_back(g, w):
        return (w[0:1] * g[0:T] + w[1:2] * g[1 : 1 + T] + w[2:3] * g[2 : 2 + T]).astype(BF16)

    gq_ref[...] = conv_back(gqs, wq_ref[...])
    gk_ref[...] = conv_back(gks, wk_ref[...])

    def value_step(h, _):
        cols = head_cols(h)
        w = wv_ref[:, cols]
        gv_ref[:, cols] = (
            w[0:1] * gvs[h, 0:T, :]
            + w[1:2] * gvs[h, 1 : 1 + T, :]
            + w[2:3] * gvs[h, 2 : 2 + T, :]
        ).astype(BF16)
        return 0

    lax.fori_loop(0, HEADS, value_step, 0)
    stores = [store_mixed]
    for i, (src, dst) in enumerate([(gq_ref, gq_hbm), (gk_ref, gk_hbm), (gv_ref, gv_hbm)]):
        stores.append(pltpu.make_async_copy(src, dst, out_s.at[1 + i]))
        stores[-1].start()

    for _, c in to_plane:
        c.wait_recv()
    mine = jnp.sum(red_xy[...], axis=0)
    one_z[...] = mine
    red_z[z] = mine

    def rz(zz, slot):
        return remote(one_z, red_z.at[slot], rz_ss.at[zz], rz_rs.at[slot], z_peer(zz))

    for away in (4, 3, 5, 2, 6, 1, 7):
        rz((z + away) % ZN, z).start()
    for j in range(1, ZN):
        rz((z + j) % ZN, (z + j) % ZN).wait_recv()
    mine = jnp.sum(red_z[...], axis=0)
    one_c[core] = mine
    back_to_core = remote(one_c.at[core], one_c.at[core], ac_ss.at[0], ac_rs.at[0], other)
    back_to_core.start()
    remote(one_c.at[core], one_c.at[1 - core], ac_ss.at[0], ac_rs.at[0], other).wait_recv()
    sums_ref[...] = one_c[...]

    for c in stores:
        c.wait()
    for c in halos:
        c.wait_send()

    def left(j, _):
        zz = (z + j) % ZN
        a_copy(tail1, got1, 0, zz).wait_send()
        a_copy(tail2, got2, 1, zz).wait_send()
        b_copy(send1, inc, 0, zz).wait_send()
        b_copy(send2, outg, 1, zz).wait_send()
        rz(zz, z).wait_send()
        return 0

    lax.fori_loop(1, ZN, left, 0)
    for j in range(1, n_y):
        yy = (y + j) % n_y
        remote(tot1, ytot1.at[y], y_ss.at[0, yy], y_rs.at[0, y], y_peer(yy)).wait_send()
        remote(tot2, ytot2.at[y], y_ss.at[1, yy], y_rs.at[1, y], y_peer(yy)).wait_send()
    for c, _ in to_plane:
        c.wait_send()
    to_core.wait_send()
    back_to_core.wait_send()


def writer(*refs):
    mixed, gq, gk, gv, sums_hbm = refs[:5]
    outs = refs[5:13]
    held = refs[13:17]
    sums, gwq, gwk, gwv, gg, in_s, out_s = refs[17:]
    ins = [
        pltpu.make_async_copy(src, dst, in_s.at[i])
        for i, (src, dst) in enumerate(
            [(sums_hbm, sums), (mixed, held[0]), (gv, held[3]), (gq, held[1]), (gk, held[2])]
        )
    ]
    stores = [
        pltpu.make_async_copy(src, dst, out_s.at[i])
        for i, (src, dst) in enumerate(
            [
                (held[0], outs[0]),
                (held[3], outs[3]),
                (held[1], outs[1]),
                (held[2], outs[2]),
                (gwq, outs[4]),
                (gwk, outs[5]),
                (gwv, outs[6]),
                (gg, outs[7]),
            ]
        )
    ]
    for c in ins:
        c.start()
    for i in (1, 2, 3, 4):
        ins[i].wait()
        stores[i - 1].start()
    ins[0].wait()
    gwq[...] = sums[0, 20:23, :]
    gwk[...] = sums[1, 20:23, :]
    for h in range(HEADS):
        base = 4 * (h % 4)
        gwv[:, h * HD : (h + 1) * HD] = sums[h // 4, base : base + 3, :]
        gg[:, h * HD : (h + 1) * HD] = sums[h // 4, base + 3 : base + 4, :]
    for c in stores[4:]:
        c.start()
    for c in stores:
        c.wait()


def solution(mesh):
    n_dp, n_ctx = mesh.shape["dp"], mesh.shape["ctx"]
    n_y = n_ctx // ZN
    wide = HEADS * HD
    thin = HEADS * F

    def shards(q, k, v, wq, wk, wv, gain, lens, og):
        vmem = pl.BlockSpec(memory_space=pltpu.VMEM)
        state = (ROWS, HD)
        hbm = pl.BlockSpec(memory_space=pltpu.HBM)
        scratch = [
            pltpu.VMEM((T, wide), BF16),
            pltpu.VMEM((T, thin), BF16),
            pltpu.VMEM((T, thin), BF16),
            pltpu.VMEM((T, wide), BF16),
            pltpu.SemaphoreType.DMA((4,)),
            pltpu.SMEM((1, DOCS), jnp.int32),
            pltpu.VMEM((T, thin), BF16),
            pltpu.VMEM((T, thin), BF16),
            pltpu.VMEM((T, wide), BF16),
            pltpu.VMEM((T, wide), BF16),
            pltpu.VMEM((3, thin), F32),
            pltpu.VMEM((3, thin), F32),
            pltpu.VMEM((3, wide), F32),
            pltpu.VMEM((1, wide), F32),
            pltpu.VMEM((T + 8, thin), F32),
            pltpu.VMEM((T + 8, thin), F32),
            pltpu.VMEM((HEADS, T + 8, HD), F32),
            pltpu.VMEM((T, thin), BF16),
            pltpu.VMEM((T, thin), BF16),
            pltpu.VMEM((thin, T), BF16),
            pltpu.VMEM((thin, T), BF16),
            pltpu.VMEM((thin, T), F32),
            pltpu.VMEM((thin, T), F32),
            pltpu.VMEM((HEADS, T, HD), BF16),
            pltpu.VMEM((T, T), F32),
            pltpu.VMEM((HEADS, T, T), BF16),
            pltpu.VMEM((HEADS, T, T), F32),
            pltpu.VMEM((HEADS, T, HD), F32),
            pltpu.VMEM((HEADS, ROWS, T), BF16),
            pltpu.VMEM((HEADS, ROWS, T), BF16),
            pltpu.VMEM((HEADS, T, HD), BF16),
            pltpu.VMEM((HEADS, T + 8, HD), F32),
            pltpu.VMEM((thin, T), F32),
            pltpu.VMEM((thin, T), F32),
            pltpu.VMEM((T + 8, thin), F32),
            pltpu.VMEM((T + 8, thin), F32),
            pltpu.VMEM((HEADS, 8, HD), F32),
            pltpu.VMEM((16, thin), BF16),
            pltpu.VMEM((16, thin), BF16),
            pltpu.VMEM((16, wide), BF16),
            pltpu.VMEM((8, thin), F32),
            pltpu.VMEM((8, thin), F32),
            pltpu.VMEM((HEADS, 8, HD), F32),
        ]
        for _ in range(2):
            scratch += [
                pltpu.VMEM((HEADS,) + state, BF16),
                pltpu.VMEM((ZN,) + state, BF16),
                pltpu.VMEM(state, BF16),
                pltpu.VMEM((n_y,) + state, BF16),
                pltpu.VMEM((ZN,) + state, BF16),
                pltpu.VMEM((HEADS,) + state, BF16),
            ]
        half = (24, HD)
        scratch += [
            pltpu.VMEM((2,) + half, F32),
            pltpu.VMEM(half, F32),
            pltpu.VMEM((n_dp // 2 * n_y,) + half, F32),
            pltpu.VMEM(half, F32),
            pltpu.VMEM((ZN,) + half, F32),
            pltpu.VMEM(half, F32),
            pltpu.VMEM((2,) + half, F32),
            pltpu.SemaphoreType.DMA((9,)),
        ]
        dma = pltpu.SemaphoreType.DMA
        for counts in ((3,), (3,), (2, ZN), (2, n_y), (2, ZN), (1,), (n_dp // 2 * n_y,), (ZN,), (1,)):
            scratch += [dma(counts), dma(counts)]
        outs = pl.pallas_call(
            functools.partial(kernel, n_dp, n_ctx),
            out_shape=(
                jax.ShapeDtypeStruct((T, wide), BF16),
                jax.ShapeDtypeStruct((T, thin), BF16),
                jax.ShapeDtypeStruct((T, thin), BF16),
                jax.ShapeDtypeStruct((T, wide), BF16),
                jax.ShapeDtypeStruct((2,) + half, F32),
            ),
            in_specs=[hbm] * 9,
            out_specs=(hbm,) * 4 + (vmem,),
            scratch_shapes=scratch,
            compiler_params=pltpu.CompilerParams(
                collective_id=0, has_side_effects=True, vmem_limit_bytes=64 * 2**20 - 2**18
            ),
        )(lens, q[0], k[0], v[0], og[0], wq, wk, wv, gain[None])
        outs = pl.pallas_call(
            writer,
            out_shape=(
                jax.ShapeDtypeStruct((T, wide), BF16),
                jax.ShapeDtypeStruct((T, thin), BF16),
                jax.ShapeDtypeStruct((T, thin), BF16),
                jax.ShapeDtypeStruct((T, wide), BF16),
                jax.ShapeDtypeStruct((3, thin), F32),
                jax.ShapeDtypeStruct((3, thin), F32),
                jax.ShapeDtypeStruct((3, wide), F32),
                jax.ShapeDtypeStruct((1, wide), F32),
            ),
            in_specs=[hbm] * 5,
            out_specs=(hbm,) * 8,
            scratch_shapes=[
                pltpu.VMEM((T, wide), BF16),
                pltpu.VMEM((T, thin), BF16),
                pltpu.VMEM((T, thin), BF16),
                pltpu.VMEM((T, wide), BF16),
                pltpu.VMEM((2,) + half, F32),
                pltpu.VMEM((3, thin), F32),
                pltpu.VMEM((3, thin), F32),
                pltpu.VMEM((3, wide), F32),
                pltpu.VMEM((1, wide), F32),
                pltpu.SemaphoreType.DMA((5,)),
                pltpu.SemaphoreType.DMA((8,)),
            ],
        )(*outs)
        mixed, gq, gk, gv, gwq, gwk, gwv, gg = outs
        return mixed[None], gq[None], gk[None], gv[None], gwq, gwk, gwv, gg[0]

    tokens = P("dp", "ctx", None)
    return jax.shard_map(
        shards,
        mesh=mesh,
        in_specs=(tokens, tokens, tokens, P(), P(), P(), P(), P("dp", None), tokens),
        out_specs=(tokens, tokens, tokens, tokens, P(), P(), P(), P()),
        check_vma=False,
    )
```

```python
import functools

import jax
import jax.numpy as jnp
from jax import lax
from jax.experimental import pallas as pl
from jax.experimental.pallas import tpu as pltpu
from jax.sharding import PartitionSpec as P

HEADS = 8
F = 16
HD = 128
T = 256
DOCS = 8
ROWS = 160
PART = ROWS // 2
GROUP = HEADS // 2
ZN = 8
EPS = 1e-06
MESH = pl.DeviceIdType.MESH
F32 = jnp.float32
BF16 = jnp.bfloat16


def dot(a, b, ca, cb):
    return lax.dot_general(a, b, (((ca,), (cb,)), ((), ())), preferred_element_type=F32)


def turned(u, d):
    return pltpu.roll(u, F - d, 0) if d else u


def put_features(out, h, u, ones):
    out[h, 0:16, :] = (u * u * (0.5**0.5)).astype(BF16)
    for d in range(1, 8):
        out[h, 16 * d : 16 * d + 16, :] = (u * turned(u, d)).astype(BF16)
    out[h, 128:144, :] = u.astype(BF16)
    rest = jnp.where(lax.broadcasted_iota(jnp.int32, (8, T), 0) == 0, ones, 0.0)
    out[h, 144:160, :] = jnp.concatenate([u[0:8] * u[8:16], rest], axis=0).astype(BF16)


def pull_features(g, u, ones):
    total = g[128:144] * ones + (2.0 * 0.5**0.5) * g[0:16] * u
    for d in range(1, 8):
        own = g[16 * d : 16 * d + 16]
        total = total + own * turned(u, d) + pltpu.roll(own * u, d, 0)
    half = g[144:152]
    total = total + jnp.concatenate([half * u[8:16], half * u[0:8]], axis=0)
    return 0.5 * total


def kernel(
    n_dp,
    n_ctx,
    lens_hbm,
    q_hbm,
    k_hbm,
    v_hbm,
    og_hbm,
    wq_hbm,
    wk_hbm,
    wv_hbm,
    gain_hbm,
    mixed_hbm,
    gq_hbm,
    gk_hbm,
    gv_hbm,
    sums_ref,
    mixed_ref,
    gq_ref,
    gk_ref,
    gv_ref,
    out_s,
    lens,
    q_ref,
    k_ref,
    v_ref,
    og_ref,
    wq_ref,
    wk_ref,
    wv_ref,
    gain_ref,
    xq,
    xk,
    xv,
    qc,
    kc,
    qt,
    kt,
    uq,
    uk,
    vc,
    mask_ref,
    kern,
    saved,
    inner,
    phiq,
    phik,
    ga_ref,
    gvs,
    gqt,
    gkt,
    gqs,
    gks,
    local,
    halo_q,
    halo_k,
    halo_v,
    back_q,
    back_k,
    back_v,
    tail1,
    got1,
    tot1,
    ytot1,
    send1,
    inc,
    tail2,
    got2,
    tot2,
    ytot2,
    send2,
    outg,
    halves,
    red_c,
    red_xy,
    one_xy,
    red_z,
    one_z,
    one_c,
    in_s,
    halo_ss,
    halo_rs,
    back_ss,
    back_rs,
    a_ss,
    a_rs,
    y_ss,
    y_rs,
    b_ss,
    b_rs,
    rc_ss,
    rc_rs,
    rxy_ss,
    rxy_rs,
    rz_ss,
    rz_rs,
    ac_ss,
    ac_rs,
):
    n_y = n_ctx // ZN
    me = lax.axis_index("ctx")
    dp = lax.axis_index("dp")
    n_x = n_dp // 2
    core = dp % 2
    x = dp // 2
    y = me // ZN
    z = me % ZN
    after = (me + 1) % n_ctx
    before = (me + n_ctx - 1) % n_ctx

    def z_peer(zz):
        return {"ctx": y * ZN + zz}

    def y_peer(yy):
        return {"ctx": yy * ZN + z}

    barrier = pltpu.get_barrier_semaphore()
    greeted = [z_peer((z + j) % ZN) for j in range(1, ZN)]
    other = {"dp": dp + 1 - 2 * core}
    plane = []
    for j in range(1, n_x * n_y):
        xx = (x + j // n_y) % n_x
        yy = (y + j % n_y) % n_y
        plane.append((xx * n_y + yy, {"dp": xx * 2 + core, "ctx": yy * ZN + z}))
    greeted += [peer for _, peer in plane]
    greeted += [other, {"ctx": after}, {"ctx": before}]
    for peer in greeted:
        pl.semaphore_signal(barrier, inc=1, device_id=peer, device_id_type=MESH)

    loads = [
        pltpu.make_async_copy(src, dst, in_s.at[i])
        for i, (src, dst) in enumerate(
            [
                (lens_hbm, lens),
                (q_hbm, q_ref),
                (k_hbm, k_ref),
                (wq_hbm, wq_ref),
                (wk_hbm, wk_ref),
                (v_hbm, v_ref),
                (wv_hbm, wv_ref),
                (gain_hbm, gain_ref),
                (og_hbm, og_ref),
            ]
        )
    ]
    for c in loads:
        c.start()
    for c in loads[:5]:
        c.wait()

    starts = []
    total = jnp.int32(0)
    for d in range(DOCS):
        starts.append(total)
        total = total + lens[0, d]
    first = me * T

    def doc_of(position):
        found = jnp.where(position >= starts[0], 1, 0)
        for d in range(1, DOCS):
            found = found + jnp.where(position >= starts[d], 1, 0)
        return found

    row_pos = first + lax.broadcasted_iota(jnp.int32, (1, T), 1)
    col_pos = first + lax.broadcasted_iota(jnp.int32, (T, 1), 0)
    row_doc, col_doc = doc_of(row_pos), doc_of(col_pos)
    prev_doc, last_doc = doc_of(first - 1), doc_of(first + T - 1)
    use_prev = jnp.where(row_doc == prev_doc, 1.0, 0.0)
    use_next = jnp.where(row_doc == last_doc, 1.0, 0.0)
    mask_ref[...] = jnp.where((row_pos <= col_pos) & (row_doc == col_doc), 1.0, 0.0)

    def keep_of(block):
        value = jnp.float32(1.0)
        for d in range(DOCS):
            value = jnp.where(starts[d] // T == block, 0.0, value)
        return value

    def keep_group(group):
        value = jnp.float32(1.0)
        for d in range(DOCS):
            value = jnp.where(starts[d] // (T * ZN) == group, 0.0, value)
        return value

    def conv(xs, w, rows):
        return (
            w[0:1] * xs[8 : 8 + rows, :] + w[1:2] * xs[7 : 7 + rows, :] + w[2:3] * xs[6 : 6 + rows, :]
        ).astype(BF16)

    def head_rows(h):
        return pl.ds(pl.multiple_of(h * F, F), F)

    def head_cols(h):
        return pl.ds(pl.multiple_of(h * HD, HD), HD)

    xq[0:8, :] = jnp.zeros((8, HEADS * F), F32)
    xk[0:8, :] = jnp.zeros((8, HEADS * F), F32)
    xq[8:, :] = q_ref[...].astype(F32)
    xk[8:, :] = k_ref[...].astype(F32)
    qc[...] = conv(xq, wq_ref[...], T)
    kc[...] = conv(xk, wk_ref[...], T)

    def turn(tokens):
        q_turned = qc[0:tokens, :].astype(F32).T
        k_turned = kc[0:tokens, :].astype(F32).T
        qt[:, 0:tokens] = q_turned.astype(BF16)
        kt[:, 0:tokens] = k_turned.astype(BF16)
        uq[:, 0:tokens] = q_turned * (0.5 * use_prev[:, 0:tokens])
        uk[:, 0:tokens] = k_turned * (0.5 * use_next[:, 0:tokens])

    turn(T)
    for c in loads[5:]:
        c.wait()

    def value_head(h, _):
        cols = head_cols(h)
        xv[h, 0:8, :] = jnp.zeros((8, HD), F32)
        xv[h, 8:, :] = v_ref[:, cols].astype(F32)
        vc[h] = conv(xv.at[h], wv_ref[:, cols], T)
        return 0

    lax.fori_loop(0, HEADS, value_head, 0)

    pl.semaphore_wait(barrier, len(greeted))

    def remote(src, dst, ss, rs, peer):
        return pltpu.make_async_remote_copy(
            src_ref=src, dst_ref=dst, send_sem=ss, recv_sem=rs, device_id=peer, device_id_type=MESH
        )

    halos = [
        remote(ref.at[T - 16 :, :], dst, halo_ss.at[i], halo_rs.at[i], {"ctx": after})
        for i, (ref, dst) in enumerate([(q_ref, halo_q), (k_ref, halo_k), (v_ref, halo_v)])
    ]
    for c in halos:
        c.start()
    for c in halos:
        c.wait_recv()
    inside = jnp.where(me > 0, 1.0, 0.0)
    xq[0:8, :] = halo_q[...].astype(F32)[8:16] * inside
    xk[0:8, :] = halo_k[...].astype(F32)[8:16] * inside
    qc[0:16, :] = conv(xq, wq_ref[...], 16)
    kc[0:16, :] = conv(xk, wk_ref[...], 16)
    turn(128)

    def owned(zz):
        return pl.ds(pl.multiple_of(PART * (zz % 2), 16), PART)

    def a_copy(tail, got, phase, g, zz):
        return remote(
            tail.at[GROUP * g + zz // 2, owned(zz), :],
            got.at[g, z],
            a_ss.at[phase, g, zz],
            a_rs.at[phase, g, z],
            z_peer(zz),
        )

    def a_arrival(tail, got, phase, g, zz):
        return remote(
            tail.at[GROUP * g + zz // 2, owned(zz), :],
            got.at[g, zz],
            a_ss.at[phase, g, zz],
            a_rs.at[phase, g, zz],
            z_peer(zz),
        )

    def b_copy(send, take, phase, g, zz):
        return remote(
            send.at[g, zz],
            take.at[GROUP * g + z // 2, owned(z), :],
            b_ss.at[phase, g, zz],
            b_rs.at[phase, g, z],
            z_peer(zz),
        )

    def b_arrival(send, take, phase, g, zz):
        return remote(
            send.at[g, zz],
            take.at[GROUP * g + zz // 2, owned(zz), :],
            b_ss.at[phase, g, zz],
            b_rs.at[phase, g, zz],
            z_peer(zz),
        )

    def send_tail(tail, got, phase, g, p):
        for zz in (2 * p, 2 * p + 1):

            @pl.when(zz != z)
            def _():
                a_copy(tail, got, phase, g, zz).start()

    def wait_state(send, take, phase, g, p):
        for zz in (2 * p, 2 * p + 1):

            @pl.when(zz != z)
            def _():
                b_arrival(send, take, phase, g, zz).wait_recv()

    def tail_head(h):
        cols = head_cols(h)
        xv[h, 0:8, :] = halo_v[:, cols].astype(F32)[8:16] * inside
        vc[h, 0:16, :] = conv(xv.at[h], wv_ref[:, cols], 16)
        value = vc[h]
        put_features(phik, h, uk[head_rows(h), :], use_next)
        tail1[h] = dot(phik[h], value, 1, 0).astype(BF16)

    for g in range(2):

        def tail_step(i, _, g=g):
            p = (z // 2 + 2 + i) % GROUP
            tail_head(GROUP * g + p)
            send_tail(tail1, got1, 0, g, p)
            return 0

        lax.fori_loop(0, GROUP, tail_step, 0)

    lane_head = lax.broadcasted_iota(jnp.int32, (1, HEADS * F), 1) // F

    def inner_step(h, _):
        chosen = jnp.where(lane_head == h, 0.25, 0.0).astype(BF16)
        scores = dot(qc[...] * chosen, kc[...], 1, 1)
        m = mask_ref[...]
        kernel_h = (m * (1.0 + scores + 0.5 * scores * scores)).astype(BF16)
        kern[h] = kernel_h
        saved[h] = m * (1.0 + scores)
        inner[h] = dot(kernel_h, vc[h], 1, 0)
        put_features(phiq, h, uq[head_rows(h), :], use_prev)
        return 0

    lax.fori_loop(0, HEADS, inner_step, 0)

    def scan(tail, got, tot, ytot, send, take, phase, reverse):
        order = range(ZN - 1, -1, -1) if reverse else range(ZN)
        keeps = [keep_of(y * ZN + i) for i in range(ZN)]

        def y_copy(g, j):
            yy = (y + j) % n_y
            return remote(
                tot.at[g], ytot.at[g, y], y_ss.at[phase, g, yy], y_rs.at[phase, g, y], y_peer(yy)
            )

        def y_arrival(g, j):
            yy = (y + j) % n_y
            return remote(
                tot.at[g], ytot.at[g, yy], y_ss.at[phase, g, yy], y_rs.at[phase, g, yy], y_peer(yy)
            )

        for g in range(2):
            got[g, z] = tail[GROUP * g + z // 2, owned(z), :]

            def wait_a(j, _, g=g):
                a_arrival(tail, got, phase, g, (z + j) % ZN).wait_recv()
                return 0

            lax.fori_loop(1, ZN, wait_a, 0)
            running = jnp.zeros((PART, HD), F32)
            for i in order:
                running = got[g, i].astype(F32) + keeps[i] * running
            total = running.astype(BF16)
            tot[g] = total
            ytot[g, y] = total
            for j in range(1, n_y):
                y_copy(g, j).start()
        for g in range(2):
            for j in range(1, n_y):
                y_arrival(g, j).wait_recv()
            carry = jnp.zeros((PART, HD), F32)
            for r in range(n_y - 1, 0, -1) if reverse else range(n_y - 1):
                counts = jnp.where(r > y if reverse else r < y, 1.0, 0.0)
                onward = ytot[g, r].astype(F32) + keep_group(r) * carry
                carry = counts * onward + (1.0 - counts) * carry
            running = carry
            for i in order:
                send[g, i] = running.astype(BF16)
                running = got[g, i].astype(F32) + keeps[i] * running
            for away in (4, 3, 5, 2, 6, 1, 7):
                b_copy(send, take, phase, g, (z + away) % ZN).start()
            take[GROUP * g + z // 2, owned(z), :] = send[g, z]

    scan(tail1, got1, tot1, ytot1, send1, inc, 0, False)

    def forward_head(h):
        cols = head_cols(h)
        attended = inner[h] + dot(phiq[h], inc[h], 0, 0)
        r = lax.rsqrt(jnp.mean(attended * attended, axis=-1, keepdims=True) + EPS)
        normed = attended * r
        gains = gain_ref[:, cols]
        mixed_ref[:, cols] = (normed * gains).astype(BF16)
        upstream = og_ref[:, cols].astype(F32)
        local[h, 3:4, :] = jnp.sum(upstream * normed, axis=0, keepdims=True)
        pulled = upstream * gains
        along = jnp.mean(pulled * normed, axis=-1, keepdims=True)
        grad = ((pulled - normed * along) * r).astype(BF16)
        ga_ref[h] = grad
        tail2[h] = dot(phiq[h], grad, 1, 0).astype(BF16)

    local[...] = jnp.zeros(local.shape, F32)

    for g in range(2):

        def forward_step(i, _, g=g):
            p = (z // 2 + 1 + i) % GROUP
            wait_state(send1, inc, 0, g, p)
            forward_head(GROUP * g + p)
            send_tail(tail2, got2, 1, g, p)
            return 0

        lax.fori_loop(0, GROUP, forward_step, 0)

    store_mixed = pltpu.make_async_copy(mixed_ref, mixed_hbm, out_s.at[0])
    store_mixed.start()

    def backward_step(h, _):
        grad = ga_ref[h]
        grad_scores = (dot(grad, vc[h], 1, 1) * saved[h]).astype(BF16)
        rows = head_rows(h)
        grad_phi = dot(inc[h], grad, 1, 1)
        gqt[rows, :] = 0.25 * dot(kt[rows, :], grad_scores, 1, 1) + pull_features(
            grad_phi, uq[rows, :], use_prev
        )
        gkt[rows, :] = 0.25 * dot(qt[rows, :], grad_scores, 1, 0)
        gvs[h, 0:T, :] = dot(kern[h], grad, 0, 0)
        return 0

    lax.fori_loop(0, HEADS, backward_step, 0)

    scan(tail2, got2, tot2, ytot2, send2, outg, 1, True)

    def taps(g, x):
        return [jnp.sum(g * x[8 - j : 8 - j + T], axis=0, keepdims=True) for j in range(3)]

    def last_head(h):
        rows = head_rows(h)
        later = outg[h]
        grad_phi = dot(later, vc[h], 1, 1)
        gkt[rows, :] = gkt[rows, :] + pull_features(grad_phi, uk[rows, :], use_next)
        g = gvs[h, 0:T, :] + dot(phik[h], later, 0, 0)
        gvs[h, 0:T, :] = g
        for j in range(3):
            local[h, j : j + 1, :] = jnp.sum(
                g * xv[h, 8 - j : 8 - j + T, :], axis=0, keepdims=True
            )

    for g in range(2):

        def last_step(i, _, g=g):
            p = (z // 2 + 1 + i) % GROUP
            wait_state(send2, outg, 1, g, p)
            last_head(GROUP * g + p)
            return 0

        lax.fori_loop(0, GROUP, last_step, 0)
    gq = gqt[...].T
    gk = gkt[...].T
    gqs[0:T, :] = gq
    gks[0:T, :] = gk

    backs = [
        remote(src, dst, back_ss.at[i], back_rs.at[i], {"ctx": before})
        for i, (src, dst) in enumerate(
            [
                (gqs.at[0:8, :], back_q),
                (gks.at[0:8, :], back_k),
                (gvs.at[:, 0:8, :], back_v),
            ]
        )
    ]
    for c in backs:
        c.start()

    for j in range(3):
        local[0, 4 + j : 5 + j, :] = jnp.sum(gq * xq[8 - j : 8 - j + T, :], axis=0, keepdims=True)
        local[1, 4 + j : 5 + j, :] = jnp.sum(gk * xk[8 - j : 8 - j + T, :], axis=0, keepdims=True)

    halves[0, 16:24, :] = local[0]
    halves[1, 16:24, :] = local[1]
    for h in range(HEADS):
        halves[h // 4, 4 * (h % 4) : 4 * (h % 4) + 4, :] = local[h, 0:4, :]
    to_core = remote(halves.at[1 - core], red_c, rc_ss.at[0], rc_rs.at[0], other)
    to_core.start()
    to_core.wait_recv()
    mine = halves[core] + red_c[...]
    one_xy[...] = mine
    here = x * n_y + y
    red_xy[here] = mine
    to_plane = [
        (
            remote(one_xy, red_xy.at[here], rxy_ss.at[slot], rxy_rs.at[here], peer),
            remote(one_xy, red_xy.at[slot], rxy_ss.at[slot], rxy_rs.at[slot], peer),
        )
        for slot, peer in plane
    ]
    for c, _ in to_plane:
        c.start()

    for c in backs:
        c.wait_recv()
    inside_next = jnp.where(me < n_ctx - 1, 1.0, 0.0)
    gqs[T : T + 8, :] = back_q[...] * inside_next
    gks[T : T + 8, :] = back_k[...] * inside_next
    for c in backs:
        c.wait_send()
    gvs[:, T : T + 8, :] = back_v[...] * inside_next

    def conv_back(g, w):
        return (w[0:1] * g[0:T] + w[1:2] * g[1 : 1 + T] + w[2:3] * g[2 : 2 + T]).astype(BF16)

    gq_ref[...] = conv_back(gqs, wq_ref[...])
    gk_ref[...] = conv_back(gks, wk_ref[...])

    def value_step(h, _):
        cols = head_cols(h)
        w = wv_ref[:, cols]
        gv_ref[:, cols] = (
            w[0:1] * gvs[h, 0:T, :]
            + w[1:2] * gvs[h, 1 : 1 + T, :]
            + w[2:3] * gvs[h, 2 : 2 + T, :]
        ).astype(BF16)
        return 0

    lax.fori_loop(0, HEADS, value_step, 0)
    stores = [store_mixed]
    for i, (src, dst) in enumerate([(gq_ref, gq_hbm), (gk_ref, gk_hbm), (gv_ref, gv_hbm)]):
        stores.append(pltpu.make_async_copy(src, dst, out_s.at[1 + i]))
        stores[-1].start()

    for _, c in to_plane:
        c.wait_recv()
    mine = jnp.sum(red_xy[...], axis=0)
    one_z[...] = mine
    red_z[z] = mine

    def rz(zz, slot):
        return remote(one_z, red_z.at[slot], rz_ss.at[zz], rz_rs.at[slot], z_peer(zz))

    for away in (4, 3, 5, 2, 6, 1, 7):
        rz((z + away) % ZN, z).start()
    for j in range(1, ZN):
        rz((z + j) % ZN, (z + j) % ZN).wait_recv()
    mine = jnp.sum(red_z[...], axis=0)
    one_c[core] = mine
    back_to_core = remote(one_c.at[core], one_c.at[core], ac_ss.at[0], ac_rs.at[0], other)
    back_to_core.start()
    remote(one_c.at[core], one_c.at[1 - core], ac_ss.at[0], ac_rs.at[0], other).wait_recv()
    sums_ref[...] = one_c[...]

    for c in stores:
        c.wait()
    for c in halos:
        c.wait_send()

    def left(j, _):
        zz = (z + j) % ZN
        for g in range(2):
            a_copy(tail1, got1, 0, g, zz).wait_send()
            a_copy(tail2, got2, 1, g, zz).wait_send()
            b_copy(send1, inc, 0, g, zz).wait_send()
            b_copy(send2, outg, 1, g, zz).wait_send()
        rz(zz, z).wait_send()
        return 0

    lax.fori_loop(1, ZN, left, 0)
    for j in range(1, n_y):
        yy = (y + j) % n_y
        for g in range(2):
            for phase, tot, ytot in ((0, tot1, ytot1), (1, tot2, ytot2)):
                remote(
                    tot.at[g], ytot.at[g, y], y_ss.at[phase, g, yy], y_rs.at[phase, g, y], y_peer(yy)
                ).wait_send()
    for c, _ in to_plane:
        c.wait_send()
    to_core.wait_send()
    back_to_core.wait_send()


def writer(*refs):
    mixed, gq, gk, gv, sums_hbm = refs[:5]
    outs = refs[5:13]
    held = refs[13:17]
    sums, gwq, gwk, gwv, gg, in_s, out_s = refs[17:]
    ins = [
        pltpu.make_async_copy(src, dst, in_s.at[i])
        for i, (src, dst) in enumerate(
            [(sums_hbm, sums), (mixed, held[0]), (gv, held[3]), (gq, held[1]), (gk, held[2])]
        )
    ]
    stores = [
        pltpu.make_async_copy(src, dst, out_s.at[i])
        for i, (src, dst) in enumerate(
            [
                (held[0], outs[0]),
                (held[3], outs[3]),
                (held[1], outs[1]),
                (held[2], outs[2]),
                (gwq, outs[4]),
                (gwk, outs[5]),
                (gwv, outs[6]),
                (gg, outs[7]),
            ]
        )
    ]
    for c in ins:
        c.start()
    for i in (1, 2, 3, 4):
        ins[i].wait()
        stores[i - 1].start()
    ins[0].wait()
    gwq[...] = sums[0, 20:23, :]
    gwk[...] = sums[1, 20:23, :]
    for h in range(HEADS):
        base = 4 * (h % 4)
        gwv[:, h * HD : (h + 1) * HD] = sums[h // 4, base : base + 3, :]
        gg[:, h * HD : (h + 1) * HD] = sums[h // 4, base + 3 : base + 4, :]
    for c in stores[4:]:
        c.start()
    for c in stores:
        c.wait()


def solution(mesh):
    n_dp, n_ctx = mesh.shape["dp"], mesh.shape["ctx"]
    n_y = n_ctx // ZN
    wide = HEADS * HD
    thin = HEADS * F

    def shards(q, k, v, wq, wk, wv, gain, lens, og):
        vmem = pl.BlockSpec(memory_space=pltpu.VMEM)
        state = (ROWS, HD)
        hbm = pl.BlockSpec(memory_space=pltpu.HBM)
        scratch = [
            pltpu.VMEM((T, wide), BF16),
            pltpu.VMEM((T, thin), BF16),
            pltpu.VMEM((T, thin), BF16),
            pltpu.VMEM((T, wide), BF16),
            pltpu.SemaphoreType.DMA((4,)),
            pltpu.SMEM((1, DOCS), jnp.int32),
            pltpu.VMEM((T, thin), BF16),
            pltpu.VMEM((T, thin), BF16),
            pltpu.VMEM((T, wide), BF16),
            pltpu.VMEM((T, wide), BF16),
            pltpu.VMEM((3, thin), F32),
            pltpu.VMEM((3, thin), F32),
            pltpu.VMEM((3, wide), F32),
            pltpu.VMEM((1, wide), F32),
            pltpu.VMEM((T + 8, thin), F32),
            pltpu.VMEM((T + 8, thin), F32),
            pltpu.VMEM((HEADS, T + 8, HD), F32),
            pltpu.VMEM((T, thin), BF16),
            pltpu.VMEM((T, thin), BF16),
            pltpu.VMEM((thin, T), BF16),
            pltpu.VMEM((thin, T), BF16),
            pltpu.VMEM((thin, T), F32),
            pltpu.VMEM((thin, T), F32),
            pltpu.VMEM((HEADS, T, HD), BF16),
            pltpu.VMEM((T, T), F32),
            pltpu.VMEM((HEADS, T, T), BF16),
            pltpu.VMEM((HEADS, T, T), F32),
            pltpu.VMEM((HEADS, T, HD), F32),
            pltpu.VMEM((HEADS, ROWS, T), BF16),
            pltpu.VMEM((HEADS, ROWS, T), BF16),
            pltpu.VMEM((HEADS, T, HD), BF16),
            pltpu.VMEM((HEADS, T + 8, HD), F32),
            pltpu.VMEM((thin, T), F32),
            pltpu.VMEM((thin, T), F32),
            pltpu.VMEM((T + 8, thin), F32),
            pltpu.VMEM((T + 8, thin), F32),
            pltpu.VMEM((HEADS, 8, HD), F32),
            pltpu.VMEM((16, thin), BF16),
            pltpu.VMEM((16, thin), BF16),
            pltpu.VMEM((16, wide), BF16),
            pltpu.VMEM((8, thin), F32),
            pltpu.VMEM((8, thin), F32),
            pltpu.VMEM((HEADS, 8, HD), F32),
        ]
        for _ in range(2):
            scratch += [
                pltpu.VMEM((HEADS,) + state, BF16),
                pltpu.VMEM((2, ZN, PART, HD), BF16),
                pltpu.VMEM((2, PART, HD), BF16),
                pltpu.VMEM((2, n_y, PART, HD), BF16),
                pltpu.VMEM((2, ZN, PART, HD), BF16),
                pltpu.VMEM((HEADS,) + state, BF16),
            ]
        half = (24, HD)
        scratch += [
            pltpu.VMEM((2,) + half, F32),
            pltpu.VMEM(half, F32),
            pltpu.VMEM((n_dp // 2 * n_y,) + half, F32),
            pltpu.VMEM(half, F32),
            pltpu.VMEM((ZN,) + half, F32),
            pltpu.VMEM(half, F32),
            pltpu.VMEM((2,) + half, F32),
            pltpu.SemaphoreType.DMA((9,)),
        ]
        dma = pltpu.SemaphoreType.DMA
        for counts in ((3,), (3,), (2, 2, ZN), (2, 2, n_y), (2, 2, ZN), (1,), (n_dp // 2 * n_y,), (ZN,), (1,)):
            scratch += [dma(counts), dma(counts)]
        outs = pl.pallas_call(
            functools.partial(kernel, n_dp, n_ctx),
            out_shape=(
                jax.ShapeDtypeStruct((T, wide), BF16),
                jax.ShapeDtypeStruct((T, thin), BF16),
                jax.ShapeDtypeStruct((T, thin), BF16),
                jax.ShapeDtypeStruct((T, wide), BF16),
                jax.ShapeDtypeStruct((2,) + half, F32),
            ),
            in_specs=[hbm] * 9,
            out_specs=(hbm,) * 4 + (vmem,),
            scratch_shapes=scratch,
            compiler_params=pltpu.CompilerParams(
                collective_id=0, has_side_effects=True, vmem_limit_bytes=64 * 2**20 - 2**18
            ),
        )(lens, q[0], k[0], v[0], og[0], wq, wk, wv, gain[None])
        outs = pl.pallas_call(
            writer,
            out_shape=(
                jax.ShapeDtypeStruct((T, wide), BF16),
                jax.ShapeDtypeStruct((T, thin), BF16),
                jax.ShapeDtypeStruct((T, thin), BF16),
                jax.ShapeDtypeStruct((T, wide), BF16),
                jax.ShapeDtypeStruct((3, thin), F32),
                jax.ShapeDtypeStruct((3, thin), F32),
                jax.ShapeDtypeStruct((3, wide), F32),
                jax.ShapeDtypeStruct((1, wide), F32),
            ),
            in_specs=[hbm] * 5,
            out_specs=(hbm,) * 8,
            scratch_shapes=[
                pltpu.VMEM((T, wide), BF16),
                pltpu.VMEM((T, thin), BF16),
                pltpu.VMEM((T, thin), BF16),
                pltpu.VMEM((T, wide), BF16),
                pltpu.VMEM((2,) + half, F32),
                pltpu.VMEM((3, thin), F32),
                pltpu.VMEM((3, thin), F32),
                pltpu.VMEM((3, wide), F32),
                pltpu.VMEM((1, wide), F32),
                pltpu.SemaphoreType.DMA((5,)),
                pltpu.SemaphoreType.DMA((8,)),
            ],
        )(*outs)
        mixed, gq, gk, gv, gwq, gwk, gwv, gg = outs
        return mixed[None], gq[None], gk[None], gv[None], gwq, gwk, gwv, gg[0]

    tokens = P("dp", "ctx", None)
    return jax.shard_map(
        shards,
        mesh=mesh,
        in_specs=(tokens, tokens, tokens, P(), P(), P(), P(), P("dp", None), tokens),
        out_specs=(tokens, tokens, tokens, tokens, P(), P(), P(), P()),
        check_vma=False,
    )
```

```python
import functools

import jax
import jax.numpy as jnp
from jax import lax
from jax.experimental import pallas as pl
from jax.experimental.pallas import tpu as pltpu
from jax.sharding import PartitionSpec as P

HEADS = 8
F = 16
HD = 128
T = 256
DOCS = 8
ROWS = 160
PART = ROWS // 2
GROUP = HEADS // 2
ZN = 8
EPS = 1e-06
MESH = pl.DeviceIdType.MESH
F32 = jnp.float32
BF16 = jnp.bfloat16


def dot(a, b, ca, cb):
    return lax.dot_general(a, b, (((ca,), (cb,)), ((), ())), preferred_element_type=F32)


def turned(u, d):
    return pltpu.roll(u, F - d, 0) if d else u


def put_features(out, h, u, ones):
    n = u.shape[1]
    out[h, 0:16, 0:n] = (u * u * (0.5**0.5)).astype(BF16)
    for d in range(1, 8):
        out[h, 16 * d : 16 * d + 16, 0:n] = (u * turned(u, d)).astype(BF16)
    out[h, 128:144, 0:n] = u.astype(BF16)
    rest = jnp.where(lax.broadcasted_iota(jnp.int32, (8, n), 0) == 0, ones, 0.0)
    out[h, 144:160, 0:n] = jnp.concatenate([u[0:8] * u[8:16], rest], axis=0).astype(BF16)


def pull_features(g, u, ones):
    total = g[128:144] * ones + (2.0 * 0.5**0.5) * g[0:16] * u
    for d in range(1, 8):
        own = g[16 * d : 16 * d + 16]
        total = total + own * turned(u, d) + pltpu.roll(own * u, d, 0)
    half = g[144:152]
    total = total + jnp.concatenate([half * u[8:16], half * u[0:8]], axis=0)
    return 0.5 * total


def kernel(
    n_dp,
    n_ctx,
    lens_hbm,
    q_hbm,
    k_hbm,
    v_hbm,
    og_hbm,
    wq_hbm,
    wk_hbm,
    wv_hbm,
    gain_hbm,
    mixed_hbm,
    gq_hbm,
    gk_hbm,
    gv_hbm,
    sums_ref,
    mixed_ref,
    gq_ref,
    gk_ref,
    gv_ref,
    out_s,
    lens,
    q_ref,
    k_ref,
    v_ref,
    og_ref,
    wq_ref,
    wk_ref,
    wv_ref,
    gain_ref,
    xq,
    xk,
    xv,
    qc,
    kc,
    qt,
    kt,
    uq,
    uk,
    vc,
    mask_ref,
    kern,
    saved,
    inner,
    phiq,
    phik,
    ga_ref,
    gvs,
    gqt,
    gkt,
    gqs,
    gks,
    local,
    rim,
    rim_got,
    back_rim,
    back_got,
    tail1,
    got1,
    tot1,
    ytot1,
    send1,
    inc,
    tail2,
    got2,
    tot2,
    ytot2,
    send2,
    outg,
    halves,
    red_c,
    red_xy,
    one_xy,
    red_z,
    one_z,
    one_c,
    in_s,
    halo_ss,
    halo_rs,
    back_ss,
    back_rs,
    a_ss,
    a_rs,
    y_ss,
    y_rs,
    b_ss,
    b_rs,
    rc_ss,
    rc_rs,
    rxy_ss,
    rxy_rs,
    rz_ss,
    rz_rs,
    ac_ss,
    ac_rs,
):
    n_y = n_ctx // ZN
    me = lax.axis_index("ctx")
    dp = lax.axis_index("dp")
    n_x = n_dp // 2
    core = dp % 2
    x = dp // 2
    y = me // ZN
    z = me % ZN
    after = (me + 1) % n_ctx
    before = (me + n_ctx - 1) % n_ctx

    def z_peer(zz):
        return {"ctx": y * ZN + zz}

    def y_peer(yy):
        return {"ctx": yy * ZN + z}

    barrier = pltpu.get_barrier_semaphore()
    greeted = [z_peer((z + j) % ZN) for j in range(1, ZN)]
    other = {"dp": dp + 1 - 2 * core}
    plane = []
    for j in range(1, n_x * n_y):
        xx = (x + j // n_y) % n_x
        yy = (y + j % n_y) % n_y
        plane.append((xx * n_y + yy, {"dp": xx * 2 + core, "ctx": yy * ZN + z}))
    greeted += [peer for _, peer in plane]
    greeted += [other, {"ctx": after}, {"ctx": before}]
    for peer in greeted:
        pl.semaphore_signal(barrier, inc=1, device_id=peer, device_id_type=MESH)

    loads = [
        pltpu.make_async_copy(src, dst, in_s.at[i])
        for i, (src, dst) in enumerate(
            [
                (lens_hbm, lens),
                (q_hbm, q_ref),
                (k_hbm, k_ref),
                (wq_hbm, wq_ref),
                (wk_hbm, wk_ref),
                (v_hbm, v_ref),
                (wv_hbm, wv_ref),
                (gain_hbm, gain_ref),
                (og_hbm, og_ref),
            ]
        )
    ]
    for c in loads:
        c.start()
    for c in loads[:5]:
        c.wait()

    starts = []
    total = jnp.int32(0)
    for d in range(DOCS):
        starts.append(total)
        total = total + lens[0, d]
    first = me * T

    def doc_of(position):
        found = jnp.where(position >= starts[0], 1, 0)
        for d in range(1, DOCS):
            found = found + jnp.where(position >= starts[d], 1, 0)
        return found

    row_pos = first + lax.broadcasted_iota(jnp.int32, (1, T), 1)
    col_pos = first + lax.broadcasted_iota(jnp.int32, (T, 1), 0)
    row_doc, col_doc = doc_of(row_pos), doc_of(col_pos)
    prev_doc, last_doc = doc_of(first - 1), doc_of(first + T - 1)
    use_prev = jnp.where(row_doc == prev_doc, 1.0, 0.0)
    use_next = jnp.where(row_doc == last_doc, 1.0, 0.0)
    mask_ref[...] = jnp.where((row_pos <= col_pos) & (row_doc == col_doc), 1.0, 0.0)

    def keep_of(block):
        value = jnp.float32(1.0)
        for d in range(DOCS):
            value = jnp.where(starts[d] // T == block, 0.0, value)
        return value

    def keep_group(group):
        value = jnp.float32(1.0)
        for d in range(DOCS):
            value = jnp.where(starts[d] // (T * ZN) == group, 0.0, value)
        return value

    def conv(xs, w, rows):
        return (
            w[0:1] * xs[8 : 8 + rows, :] + w[1:2] * xs[7 : 7 + rows, :] + w[2:3] * xs[6 : 6 + rows, :]
        ).astype(BF16)

    def head_rows(h):
        return pl.ds(h * F if isinstance(h, int) else pl.multiple_of(h * F, F), F)

    def head_cols(h):
        return pl.ds(h * HD if isinstance(h, int) else pl.multiple_of(h * HD, HD), HD)

    xq[0:8, :] = jnp.zeros((8, HEADS * F), F32)
    xk[0:8, :] = jnp.zeros((8, HEADS * F), F32)
    xq[8:, :] = q_ref[...].astype(F32)
    xk[8:, :] = k_ref[...].astype(F32)
    qc[...] = conv(xq, wq_ref[...], T)
    kc[...] = conv(xk, wk_ref[...], T)

    def turn(tokens):
        q_turned = qc[0:tokens, :].astype(F32).T
        k_turned = kc[0:tokens, :].astype(F32).T
        qt[:, 0:tokens] = q_turned.astype(BF16)
        kt[:, 0:tokens] = k_turned.astype(BF16)
        uq[:, 0:tokens] = q_turned * (0.5 * use_prev[:, 0:tokens])
        uk[:, 0:tokens] = k_turned * (0.5 * use_next[:, 0:tokens])

    turn(T)
    for c in loads[5:]:
        c.wait()

    def value_head(h, _):
        cols = head_cols(h)
        xv[h, 0:8, :] = jnp.zeros((8, HD), F32)
        xv[h, 8:, :] = v_ref[:, cols].astype(F32)
        vc[h] = conv(xv.at[h], wv_ref[:, cols], T)
        return 0

    for h in range(HEADS):
        value_head(h, 0)

    pl.semaphore_wait(barrier, len(greeted))

    def remote(src, dst, ss, rs, peer):
        return pltpu.make_async_remote_copy(
            src_ref=src, dst_ref=dst, send_sem=ss, recv_sem=rs, device_id=peer, device_id_type=MESH
        )

    rim[16:24, :] = jnp.zeros((8, HD), F32)
    for j in range(2):
        row = T + 6 + j
        for h in range(HEADS):
            rim[8 * j + h : 8 * j + h + 1, :] = xv[h, row : row + 1, :]
        rim[16 + j : 17 + j, :] = xq[row : row + 1, :]
        rim[18 + j : 19 + j, :] = xk[row : row + 1, :]
    halo = remote(rim, rim_got, halo_ss.at[0], halo_rs.at[0], {"ctx": after})
    halo.start()
    for h in range(HEADS):
        put_features(phik, h, uk[head_rows(h), :], use_next)
    halo.wait_recv()
    inside = jnp.where(me > 0, 1.0, 0.0)
    for j in range(2):
        for h in range(HEADS):
            xv[h, 6 + j : 7 + j, :] = rim_got[8 * j + h : 8 * j + h + 1, :] * inside
        xq[6 + j : 7 + j, :] = rim_got[16 + j : 17 + j, :] * inside
        xk[6 + j : 7 + j, :] = rim_got[18 + j : 19 + j, :] * inside
    qc[0:16, :] = conv(xq, wq_ref[...], 16)
    kc[0:16, :] = conv(xk, wk_ref[...], 16)
    turn(128)

    def owned(zz):
        return pl.ds(pl.multiple_of(PART * (zz % 2), 16), PART)

    def a_copy(tail, got, phase, g, zz):
        return remote(
            tail.at[GROUP * g + zz // 2, owned(zz), :],
            got.at[g, z],
            a_ss.at[phase, g, zz],
            a_rs.at[phase, g, z],
            z_peer(zz),
        )

    def a_arrival(tail, got, phase, g, zz):
        return remote(
            tail.at[GROUP * g + zz // 2, owned(zz), :],
            got.at[g, zz],
            a_ss.at[phase, g, zz],
            a_rs.at[phase, g, zz],
            z_peer(zz),
        )

    def b_copy(send, take, phase, g, zz):
        return remote(
            send.at[g, zz],
            take.at[GROUP * g + z // 2, owned(z), :],
            b_ss.at[phase, g, zz],
            b_rs.at[phase, g, z],
            z_peer(zz),
        )

    def b_arrival(send, take, phase, g, zz):
        return remote(
            send.at[g, zz],
            take.at[GROUP * g + zz // 2, owned(zz), :],
            b_ss.at[phase, g, zz],
            b_rs.at[phase, g, zz],
            z_peer(zz),
        )

    def send_tail(tail, got, phase, g, p):
        for zz in (2 * p, 2 * p + 1):

            @pl.when(zz != z)
            def _():
                a_copy(tail, got, phase, g, zz).start()

    def wait_state(send, take, phase, g, p):
        for zz in (2 * p, 2 * p + 1):

            @pl.when(zz != z)
            def _():
                b_arrival(send, take, phase, g, zz).wait_recv()

    def tail_head(h):
        cols = head_cols(h)
        vc[h, 0:16, :] = conv(xv.at[h], wv_ref[:, cols], 16)
        value = vc[h]
        put_features(phik, h, uk[head_rows(h), 0:128], use_next[:, 0:128])
        tail1[h] = dot(phik[h], value, 1, 0).astype(BF16)

    for g in range(2):

        def tail_step(i, _, g=g):
            p = (z // 2 + 2 + i) % GROUP
            tail_head(GROUP * g + p)
            send_tail(tail1, got1, 0, g, p)
            return 0

        lax.fori_loop(0, GROUP, tail_step, 0)

    lane_head = lax.broadcasted_iota(jnp.int32, (1, HEADS * F), 1) // F

    def inner_step(h, _):
        chosen = jnp.where(lane_head == h, 0.25, 0.0).astype(BF16)
        scores = dot(qc[...] * chosen, kc[...], 1, 1)
        m = mask_ref[...]
        kernel_h = (m * (1.0 + scores + 0.5 * scores * scores)).astype(BF16)
        kern[h] = kernel_h
        saved[h] = m * (1.0 + scores)
        inner[h] = dot(kernel_h, vc[h], 1, 0)
        put_features(phiq, h, uq[head_rows(h), :], use_prev)
        return 0

    for h in range(HEADS):
        inner_step(h, 0)

    def scan(tail, got, tot, ytot, send, take, phase, reverse):
        order = range(ZN - 1, -1, -1) if reverse else range(ZN)
        keeps = [keep_of(y * ZN + i) for i in range(ZN)]

        def y_copy(g, j):
            yy = (y + j) % n_y
            return remote(
                tot.at[g], ytot.at[g, y], y_ss.at[phase, g, yy], y_rs.at[phase, g, y], y_peer(yy)
            )

        def y_arrival(g, j):
            yy = (y + j) % n_y
            return remote(
                tot.at[g], ytot.at[g, yy], y_ss.at[phase, g, yy], y_rs.at[phase, g, yy], y_peer(yy)
            )

        for g in range(2):
            got[g, z] = tail[GROUP * g + z // 2, owned(z), :]

            def wait_a(j, _, g=g):
                a_arrival(tail, got, phase, g, (z + j) % ZN).wait_recv()
                return 0

            lax.fori_loop(1, ZN, wait_a, 0)
            running = jnp.zeros((PART, HD), F32)
            for i in order:
                running = got[g, i].astype(F32) + keeps[i] * running
            total = running.astype(BF16)
            tot[g] = total
            ytot[g, y] = total
            for j in range(1, n_y):
                y_copy(g, j).start()
        for g in range(2):
            for j in range(1, n_y):
                y_arrival(g, j).wait_recv()
            carry = jnp.zeros((PART, HD), F32)
            for r in range(n_y - 1, 0, -1) if reverse else range(n_y - 1):
                counts = jnp.where(r > y if reverse else r < y, 1.0, 0.0)
                onward = ytot[g, r].astype(F32) + keep_group(r) * carry
                carry = counts * onward + (1.0 - counts) * carry
            running = carry
            for i in order:
                send[g, i] = running.astype(BF16)
                running = got[g, i].astype(F32) + keeps[i] * running
            for away in (4, 3, 5, 2, 6, 1, 7):
                b_copy(send, take, phase, g, (z + away) % ZN).start()
            take[GROUP * g + z // 2, owned(z), :] = send[g, z]

    scan(tail1, got1, tot1, ytot1, send1, inc, 0, False)

    def forward_head(h):
        cols = head_cols(h)
        attended = inner[h] + dot(phiq[h], inc[h], 0, 0)
        r = lax.rsqrt(jnp.mean(attended * attended, axis=-1, keepdims=True) + EPS)
        normed = attended * r
        gains = gain_ref[:, cols]
        mixed_ref[:, cols] = (normed * gains).astype(BF16)
        upstream = og_ref[:, cols].astype(F32)
        local[h, 3:4, :] = jnp.sum(upstream * normed, axis=0, keepdims=True)
        pulled = upstream * gains
        along = jnp.mean(pulled * normed, axis=-1, keepdims=True)
        grad = ((pulled - normed * along) * r).astype(BF16)
        ga_ref[h] = grad
        tail2[h] = dot(phiq[h], grad, 1, 0).astype(BF16)

    local[...] = jnp.zeros(local.shape, F32)

    for g in range(2):

        def forward_step(i, _, g=g):
            p = (z // 2 + 1 + i) % GROUP
            wait_state(send1, inc, 0, g, p)
            forward_head(GROUP * g + p)
            send_tail(tail2, got2, 1, g, p)
            return 0

        lax.fori_loop(0, GROUP, forward_step, 0)

    store_mixed = pltpu.make_async_copy(mixed_ref, mixed_hbm, out_s.at[0])
    store_mixed.start()

    def backward_step(h, _):
        grad = ga_ref[h]
        grad_scores = (dot(grad, vc[h], 1, 1) * saved[h]).astype(BF16)
        rows = head_rows(h)
        grad_phi = dot(inc[h], grad, 1, 1)
        gqt[rows, :] = 0.25 * dot(kt[rows, :], grad_scores, 1, 1) + pull_features(
            grad_phi, uq[rows, :], use_prev
        )
        gkt[rows, :] = 0.25 * dot(qt[rows, :], grad_scores, 1, 0)
        gvs[h, 0:T, :] = dot(kern[h], grad, 0, 0)
        return 0

    for h in range(HEADS):
        backward_step(h, 0)

    scan(tail2, got2, tot2, ytot2, send2, outg, 1, True)

    def taps(g, x):
        return [jnp.sum(g * x[8 - j : 8 - j + T], axis=0, keepdims=True) for j in range(3)]

    def last_head(h):
        rows = head_rows(h)
        later = outg[h]
        grad_phi = dot(later, vc[h], 1, 1)
        gkt[rows, :] = gkt[rows, :] + pull_features(grad_phi, uk[rows, :], use_next)
        g = gvs[h, 0:T, :] + dot(phik[h], later, 0, 0)
        gvs[h, 0:T, :] = g
        for j in range(3):
            local[h, j : j + 1, :] = jnp.sum(
                g * xv[h, 8 - j : 8 - j + T, :], axis=0, keepdims=True
            )

    for g in range(2):

        def last_step(i, _, g=g):
            p = (z // 2 + 1 + i) % GROUP
            wait_state(send2, outg, 1, g, p)
            last_head(GROUP * g + p)
            return 0

        lax.fori_loop(0, GROUP, last_step, 0)
    gq = gqt[...].T
    gk = gkt[...].T
    gqs[0:T, :] = gq
    gks[0:T, :] = gk

    back_rim[16:24, :] = jnp.zeros((8, HD), F32)
    for j in range(2):
        for h in range(HEADS):
            back_rim[8 * j + h : 8 * j + h + 1, :] = gvs[h, j : j + 1, :]
        back_rim[16 + j : 17 + j, :] = gqs[j : j + 1, :]
        back_rim[18 + j : 19 + j, :] = gks[j : j + 1, :]
    back = remote(back_rim, back_got, back_ss.at[0], back_rs.at[0], {"ctx": before})
    back.start()

    for j in range(3):
        local[0, 4 + j : 5 + j, :] = jnp.sum(gq * xq[8 - j : 8 - j + T, :], axis=0, keepdims=True)
        local[1, 4 + j : 5 + j, :] = jnp.sum(gk * xk[8 - j : 8 - j + T, :], axis=0, keepdims=True)

    halves[0, 16:24, :] = local[0]
    halves[1, 16:24, :] = local[1]
    for h in range(HEADS):
        halves[h // 4, 4 * (h % 4) : 4 * (h % 4) + 4, :] = local[h, 0:4, :]
    to_core = remote(halves.at[1 - core], red_c, rc_ss.at[0], rc_rs.at[0], other)
    to_core.start()
    to_core.wait_recv()
    mine = halves[core] + red_c[...]
    one_xy[...] = mine
    here = x * n_y + y
    red_xy[here] = mine
    to_plane = [
        (
            remote(one_xy, red_xy.at[here], rxy_ss.at[slot], rxy_rs.at[here], peer),
            remote(one_xy, red_xy.at[slot], rxy_ss.at[slot], rxy_rs.at[slot], peer),
        )
        for slot, peer in plane
    ]
    for c, _ in to_plane:
        c.start()

    for _, c in to_plane:
        c.wait_recv()
    mine = jnp.sum(red_xy[...], axis=0)
    one_z[...] = mine
    red_z[z] = mine

    def rz(zz, slot):
        return remote(one_z, red_z.at[slot], rz_ss.at[zz], rz_rs.at[slot], z_peer(zz))

    for away in (4, 3, 5, 2, 6, 1, 7):
        rz((z + away) % ZN, z).start()
    back.wait_recv()
    inside_next = jnp.where(me < n_ctx - 1, 1.0, 0.0)
    for j in range(2):
        row = T + j
        for h in range(HEADS):
            gvs[h, row : row + 1, :] = back_got[8 * j + h : 8 * j + h + 1, :] * inside_next
        gqs[row : row + 1, :] = back_got[16 + j : 17 + j, :] * inside_next
        gks[row : row + 1, :] = back_got[18 + j : 19 + j, :] * inside_next

    def conv_back(g, w):
        return (w[0:1] * g[0:T] + w[1:2] * g[1 : 1 + T] + w[2:3] * g[2 : 2 + T]).astype(BF16)

    gq_ref[...] = conv_back(gqs, wq_ref[...])
    gk_ref[...] = conv_back(gks, wk_ref[...])

    def value_step(h, _):
        cols = head_cols(h)
        w = wv_ref[:, cols]
        gv_ref[:, cols] = (
            w[0:1] * gvs[h, 0:T, :]
            + w[1:2] * gvs[h, 1 : 1 + T, :]
            + w[2:3] * gvs[h, 2 : 2 + T, :]
        ).astype(BF16)
        return 0

    for h in range(HEADS):
        value_step(h, 0)
    stores = [store_mixed]
    for i, (src, dst) in enumerate([(gq_ref, gq_hbm), (gk_ref, gk_hbm), (gv_ref, gv_hbm)]):
        stores.append(pltpu.make_async_copy(src, dst, out_s.at[1 + i]))
        stores[-1].start()

    for j in range(1, ZN):
        rz((z + j) % ZN, (z + j) % ZN).wait_recv()
    mine = jnp.sum(red_z[...], axis=0)
    one_c[core] = mine
    back_to_core = remote(one_c.at[core], one_c.at[core], ac_ss.at[0], ac_rs.at[0], other)
    back_to_core.start()
    remote(one_c.at[core], one_c.at[1 - core], ac_ss.at[0], ac_rs.at[0], other).wait_recv()
    sums_ref[...] = one_c[...]

    for c in stores:
        c.wait()
    halo.wait_send()
    back.wait_send()

    def left(j, _):
        zz = (z + j) % ZN
        for g in range(2):
            a_copy(tail1, got1, 0, g, zz).wait_send()
            a_copy(tail2, got2, 1, g, zz).wait_send()
            b_copy(send1, inc, 0, g, zz).wait_send()
            b_copy(send2, outg, 1, g, zz).wait_send()
        rz(zz, z).wait_send()
        return 0

    lax.fori_loop(1, ZN, left, 0)
    for j in range(1, n_y):
        yy = (y + j) % n_y
        for g in range(2):
            for phase, tot, ytot in ((0, tot1, ytot1), (1, tot2, ytot2)):
                remote(
                    tot.at[g], ytot.at[g, y], y_ss.at[phase, g, yy], y_rs.at[phase, g, y], y_peer(yy)
                ).wait_send()
    for c, _ in to_plane:
        c.wait_send()
    to_core.wait_send()
    back_to_core.wait_send()


def writer(*refs):
    mixed, gq, gk, gv, sums_hbm = refs[:5]
    outs = refs[5:13]
    held = refs[13:17]
    sums, gwq, gwk, gwv, gg, in_s, out_s = refs[17:]
    ins = [
        pltpu.make_async_copy(src, dst, in_s.at[i])
        for i, (src, dst) in enumerate(
            [(sums_hbm, sums), (mixed, held[0]), (gv, held[3]), (gq, held[1]), (gk, held[2])]
        )
    ]
    stores = [
        pltpu.make_async_copy(src, dst, out_s.at[i])
        for i, (src, dst) in enumerate(
            [
                (held[0], outs[0]),
                (held[3], outs[3]),
                (held[1], outs[1]),
                (held[2], outs[2]),
                (gwq, outs[4]),
                (gwk, outs[5]),
                (gwv, outs[6]),
                (gg, outs[7]),
            ]
        )
    ]
    for c in ins:
        c.start()
    for i in (1, 2, 3, 4):
        ins[i].wait()
        stores[i - 1].start()
    ins[0].wait()
    gwq[...] = sums[0, 20:23, :]
    gwk[...] = sums[1, 20:23, :]
    for h in range(HEADS):
        base = 4 * (h % 4)
        gwv[:, h * HD : (h + 1) * HD] = sums[h // 4, base : base + 3, :]
        gg[:, h * HD : (h + 1) * HD] = sums[h // 4, base + 3 : base + 4, :]
    for c in stores[4:]:
        c.start()
    for c in stores:
        c.wait()


def solution(mesh):
    n_dp, n_ctx = mesh.shape["dp"], mesh.shape["ctx"]
    n_y = n_ctx // ZN
    wide = HEADS * HD
    thin = HEADS * F

    def shards(q, k, v, wq, wk, wv, gain, lens, og):
        vmem = pl.BlockSpec(memory_space=pltpu.VMEM)
        state = (ROWS, HD)
        hbm = pl.BlockSpec(memory_space=pltpu.HBM)
        scratch = [
            pltpu.VMEM((T, wide), BF16),
            pltpu.VMEM((T, thin), BF16),
            pltpu.VMEM((T, thin), BF16),
            pltpu.VMEM((T, wide), BF16),
            pltpu.SemaphoreType.DMA((4,)),
            pltpu.SMEM((1, DOCS), jnp.int32),
            pltpu.VMEM((T, thin), BF16),
            pltpu.VMEM((T, thin), BF16),
            pltpu.VMEM((T, wide), BF16),
            pltpu.VMEM((T, wide), BF16),
            pltpu.VMEM((3, thin), F32),
            pltpu.VMEM((3, thin), F32),
            pltpu.VMEM((3, wide), F32),
            pltpu.VMEM((1, wide), F32),
            pltpu.VMEM((T + 8, thin), F32),
            pltpu.VMEM((T + 8, thin), F32),
            pltpu.VMEM((HEADS, T + 8, HD), F32),
            pltpu.VMEM((T, thin), BF16),
            pltpu.VMEM((T, thin), BF16),
            pltpu.VMEM((thin, T), BF16),
            pltpu.VMEM((thin, T), BF16),
            pltpu.VMEM((thin, T), F32),
            pltpu.VMEM((thin, T), F32),
            pltpu.VMEM((HEADS, T, HD), BF16),
            pltpu.VMEM((T, T), F32),
            pltpu.VMEM((HEADS, T, T), BF16),
            pltpu.VMEM((HEADS, T, T), F32),
            pltpu.VMEM((HEADS, T, HD), F32),
            pltpu.VMEM((HEADS, ROWS, T), BF16),
            pltpu.VMEM((HEADS, ROWS, T), BF16),
            pltpu.VMEM((HEADS, T, HD), BF16),
            pltpu.VMEM((HEADS, T + 8, HD), F32),
            pltpu.VMEM((thin, T), F32),
            pltpu.VMEM((thin, T), F32),
            pltpu.VMEM((T + 8, thin), F32),
            pltpu.VMEM((T + 8, thin), F32),
            pltpu.VMEM((HEADS, 8, HD), F32),
            pltpu.VMEM((24, HD), F32),
            pltpu.VMEM((24, HD), F32),
            pltpu.VMEM((24, HD), F32),
            pltpu.VMEM((24, HD), F32),
        ]
        for _ in range(2):
            scratch += [
                pltpu.VMEM((HEADS,) + state, BF16),
                pltpu.VMEM((2, ZN, PART, HD), BF16),
                pltpu.VMEM((2, PART, HD), BF16),
                pltpu.VMEM((2, n_y, PART, HD), BF16),
                pltpu.VMEM((2, ZN, PART, HD), BF16),
                pltpu.VMEM((HEADS,) + state, BF16),
            ]
        half = (24, HD)
        scratch += [
            pltpu.VMEM((2,) + half, F32),
            pltpu.VMEM(half, F32),
            pltpu.VMEM((n_dp // 2 * n_y,) + half, F32),
            pltpu.VMEM(half, F32),
            pltpu.VMEM((ZN,) + half, F32),
            pltpu.VMEM(half, F32),
            pltpu.VMEM((2,) + half, F32),
            pltpu.SemaphoreType.DMA((9,)),
        ]
        dma = pltpu.SemaphoreType.DMA
        for counts in ((1,), (1,), (2, 2, ZN), (2, 2, n_y), (2, 2, ZN), (1,), (n_dp // 2 * n_y,), (ZN,), (1,)):
            scratch += [dma(counts), dma(counts)]
        outs = pl.pallas_call(
            functools.partial(kernel, n_dp, n_ctx),
            out_shape=(
                jax.ShapeDtypeStruct((T, wide), BF16),
                jax.ShapeDtypeStruct((T, thin), BF16),
                jax.ShapeDtypeStruct((T, thin), BF16),
                jax.ShapeDtypeStruct((T, wide), BF16),
                jax.ShapeDtypeStruct((2,) + half, F32),
            ),
            in_specs=[hbm] * 9,
            out_specs=(hbm,) * 4 + (vmem,),
            scratch_shapes=scratch,
            compiler_params=pltpu.CompilerParams(
                collective_id=0, has_side_effects=True, vmem_limit_bytes=64 * 2**20 - 2**18
            ),
        )(lens, q[0], k[0], v[0], og[0], wq, wk, wv, gain[None])
        outs = pl.pallas_call(
            writer,
            out_shape=(
                jax.ShapeDtypeStruct((T, wide), BF16),
                jax.ShapeDtypeStruct((T, thin), BF16),
                jax.ShapeDtypeStruct((T, thin), BF16),
                jax.ShapeDtypeStruct((T, wide), BF16),
                jax.ShapeDtypeStruct((3, thin), F32),
                jax.ShapeDtypeStruct((3, thin), F32),
                jax.ShapeDtypeStruct((3, wide), F32),
                jax.ShapeDtypeStruct((1, wide), F32),
            ),
            in_specs=[hbm] * 5,
            out_specs=(hbm,) * 8,
            scratch_shapes=[
                pltpu.VMEM((T, wide), BF16),
                pltpu.VMEM((T, thin), BF16),
                pltpu.VMEM((T, thin), BF16),
                pltpu.VMEM((T, wide), BF16),
                pltpu.VMEM((2,) + half, F32),
                pltpu.VMEM((3, thin), F32),
                pltpu.VMEM((3, thin), F32),
                pltpu.VMEM((3, wide), F32),
                pltpu.VMEM((1, wide), F32),
                pltpu.SemaphoreType.DMA((5,)),
                pltpu.SemaphoreType.DMA((8,)),
            ],
        )(*outs)
        mixed, gq, gk, gv, gwq, gwk, gwv, gg = outs
        return mixed[None], gq[None], gk[None], gv[None], gwq, gwk, gwv, gg[0]

    tokens = P("dp", "ctx", None)
    return jax.shard_map(
        shards,
        mesh=mesh,
        in_specs=(tokens, tokens, tokens, P(), P(), P(), P(), P("dp", None), tokens),
        out_specs=(tokens, tokens, tokens, tokens, P(), P(), P(), P()),
        check_vma=False,
    )
```

```python
import functools

import jax
import jax.numpy as jnp
from jax import lax
from jax.experimental import pallas as pl
from jax.experimental.pallas import tpu as pltpu
from jax.sharding import PartitionSpec as P

HEADS = 8
F = 16
HD = 128
T = 256
DOCS = 8
ROWS = 160
PART = ROWS // 2
GROUP = HEADS // 2
ZN = 8
EPS = 1e-06
MESH = pl.DeviceIdType.MESH
F32 = jnp.float32
BF16 = jnp.bfloat16


def dot(a, b, ca, cb):
    return lax.dot_general(a, b, (((ca,), (cb,)), ((), ())), preferred_element_type=F32)


def turned(u, d):
    return pltpu.roll(u, F - d, 0) if d else u


def put_features(out, h, u, ones):
    n = u.shape[1]
    out[h, 0:16, 0:n] = (u * u * (0.5**0.5)).astype(BF16)
    for d in range(1, 8):
        out[h, 16 * d : 16 * d + 16, 0:n] = (u * turned(u, d)).astype(BF16)
    out[h, 128:144, 0:n] = u.astype(BF16)
    rest = jnp.where(lax.broadcasted_iota(jnp.int32, (8, n), 0) == 0, ones, 0.0)
    out[h, 144:160, 0:n] = jnp.concatenate([u[0:8] * u[8:16], rest], axis=0).astype(BF16)


def pull_features(g, u, ones):
    total = g[128:144] * ones + (2.0 * 0.5**0.5) * g[0:16] * u
    for d in range(1, 8):
        own = g[16 * d : 16 * d + 16]
        total = total + own * turned(u, d) + pltpu.roll(own * u, d, 0)
    half = g[144:152]
    total = total + jnp.concatenate([half * u[8:16], half * u[0:8]], axis=0)
    return 0.5 * total


def kernel(
    n_dp,
    n_ctx,
    lens_hbm,
    q_hbm,
    k_hbm,
    v_hbm,
    og_hbm,
    wq_hbm,
    wk_hbm,
    wv_hbm,
    gain_hbm,
    mixed_hbm,
    gq_hbm,
    gk_hbm,
    gv_hbm,
    sums_ref,
    mixed_ref,
    gq_ref,
    gk_ref,
    gv_ref,
    out_s,
    lens,
    q_ref,
    k_ref,
    v_ref,
    og_ref,
    wq_ref,
    wk_ref,
    wv_ref,
    gain_ref,
    xq,
    xk,
    xv,
    qc,
    kc,
    qt,
    kt,
    uq,
    uk,
    vc,
    mask_ref,
    kern,
    saved,
    inner,
    phiq,
    phik,
    ga_ref,
    gvs,
    gqt,
    gkt,
    gqs,
    gks,
    local,
    rim,
    rim_got,
    back_rim,
    back_got,
    tail1,
    got1,
    tot1,
    ytot1,
    send1,
    inc,
    tail2,
    got2,
    tot2,
    ytot2,
    send2,
    outg,
    halves,
    red_c,
    red_xy,
    one_xy,
    red_z,
    one_z,
    one_c,
    in_s,
    halo_ss,
    halo_rs,
    back_ss,
    back_rs,
    a_ss,
    a_rs,
    y_ss,
    y_rs,
    b_ss,
    b_rs,
    rc_ss,
    rc_rs,
    rxy_ss,
    rxy_rs,
    rz_ss,
    rz_rs,
    ac_ss,
    ac_rs,
):
    n_y = n_ctx // ZN
    me = lax.axis_index("ctx")
    dp = lax.axis_index("dp")
    n_x = n_dp // 2
    core = dp % 2
    x = dp // 2
    y = me // ZN
    z = me % ZN
    after = (me + 1) % n_ctx
    before = (me + n_ctx - 1) % n_ctx

    def z_peer(zz):
        return {"ctx": y * ZN + zz}

    def y_peer(yy):
        return {"ctx": yy * ZN + z}

    barrier = pltpu.get_barrier_semaphore()
    greeted = [z_peer((z + j) % ZN) for j in range(1, ZN)]
    other = {"dp": dp + 1 - 2 * core}
    plane = []
    for j in range(1, n_x * n_y):
        xx = (x + j // n_y) % n_x
        yy = (y + j % n_y) % n_y
        plane.append((xx * n_y + yy, {"dp": xx * 2 + core, "ctx": yy * ZN + z}))
    greeted += [peer for _, peer in plane]
    greeted += [other, {"ctx": after}, {"ctx": before}]
    for peer in greeted:
        pl.semaphore_signal(barrier, inc=1, device_id=peer, device_id_type=MESH)

    loads = [
        pltpu.make_async_copy(src, dst, in_s.at[i])
        for i, (src, dst) in enumerate(
            [
                (lens_hbm, lens),
                (q_hbm, q_ref),
                (k_hbm, k_ref),
                (wq_hbm, wq_ref),
                (wk_hbm, wk_ref),
                (v_hbm, v_ref),
                (wv_hbm, wv_ref),
                (gain_hbm, gain_ref),
                (og_hbm, og_ref),
            ]
        )
    ]
    for c in loads:
        c.start()
    for c in loads[:5]:
        c.wait()

    starts = []
    total = jnp.int32(0)
    for d in range(DOCS):
        starts.append(total)
        total = total + lens[0, d]
    first = me * T

    def doc_of(position):
        found = jnp.where(position >= starts[0], 1, 0)
        for d in range(1, DOCS):
            found = found + jnp.where(position >= starts[d], 1, 0)
        return found

    row_pos = first + lax.broadcasted_iota(jnp.int32, (1, T), 1)
    col_pos = first + lax.broadcasted_iota(jnp.int32, (T, 1), 0)
    row_doc, col_doc = doc_of(row_pos), doc_of(col_pos)
    prev_doc, last_doc = doc_of(first - 1), doc_of(first + T - 1)
    use_prev = jnp.where(row_doc == prev_doc, 1.0, 0.0)
    use_next = jnp.where(row_doc == last_doc, 1.0, 0.0)
    mask_ref[...] = jnp.where((row_pos <= col_pos) & (row_doc == col_doc), 1.0, 0.0)

    def keep_of(block):
        value = jnp.float32(1.0)
        for d in range(DOCS):
            value = jnp.where(starts[d] // T == block, 0.0, value)
        return value

    def keep_group(group):
        value = jnp.float32(1.0)
        for d in range(DOCS):
            value = jnp.where(starts[d] // (T * ZN) == group, 0.0, value)
        return value

    def conv(xs, w, rows):
        return (
            w[0:1] * xs[8 : 8 + rows, :] + w[1:2] * xs[7 : 7 + rows, :] + w[2:3] * xs[6 : 6 + rows, :]
        ).astype(BF16)

    def head_rows(h):
        return pl.ds(h * F if isinstance(h, int) else pl.multiple_of(h * F, F), F)

    def head_cols(h):
        return pl.ds(h * HD if isinstance(h, int) else pl.multiple_of(h * HD, HD), HD)

    xq[0:8, :] = jnp.zeros((8, HEADS * F), F32)
    xk[0:8, :] = jnp.zeros((8, HEADS * F), F32)
    xq[8:, :] = q_ref[...].astype(F32)
    xk[8:, :] = k_ref[...].astype(F32)
    qc[...] = conv(xq, wq_ref[...], T)
    kc[...] = conv(xk, wk_ref[...], T)

    def turn(tokens):
        q_turned = qc[0:tokens, :].astype(F32).T
        k_turned = kc[0:tokens, :].astype(F32).T
        qt[:, 0:tokens] = q_turned.astype(BF16)
        kt[:, 0:tokens] = k_turned.astype(BF16)
        uq[:, 0:tokens] = q_turned * (0.5 * use_prev[:, 0:tokens])
        uk[:, 0:tokens] = k_turned * (0.5 * use_next[:, 0:tokens])

    turn(T)
    for c in loads[5:]:
        c.wait()

    def value_head(h, _):
        cols = head_cols(h)
        xv[h, 0:8, :] = jnp.zeros((8, HD), F32)
        xv[h, 8:, :] = v_ref[:, cols].astype(F32)
        vc[h] = conv(xv.at[h], wv_ref[:, cols], T)
        return 0

    for h in range(HEADS):
        value_head(h, 0)

    pl.semaphore_wait(barrier, len(greeted))

    def remote(src, dst, ss, rs, peer):
        return pltpu.make_async_remote_copy(
            src_ref=src, dst_ref=dst, send_sem=ss, recv_sem=rs, device_id=peer, device_id_type=MESH
        )

    rim[16:24, :] = jnp.zeros((8, HD), F32)
    for j in range(2):
        row = T + 6 + j
        for h in range(HEADS):
            rim[8 * j + h : 8 * j + h + 1, :] = xv[h, row : row + 1, :]
        rim[16 + j : 17 + j, :] = xq[row : row + 1, :]
        rim[18 + j : 19 + j, :] = xk[row : row + 1, :]
    halo = remote(rim, rim_got, halo_ss.at[0], halo_rs.at[0], {"ctx": after})
    halo.start()
    for h in range(HEADS):
        put_features(phik, h, uk[head_rows(h), :], use_next)
    halo.wait_recv()
    inside = jnp.where(me > 0, 1.0, 0.0)
    for j in range(2):
        for h in range(HEADS):
            xv[h, 6 + j : 7 + j, :] = rim_got[8 * j + h : 8 * j + h + 1, :] * inside
        xq[6 + j : 7 + j, :] = rim_got[16 + j : 17 + j, :] * inside
        xk[6 + j : 7 + j, :] = rim_got[18 + j : 19 + j, :] * inside
    qc[0:16, :] = conv(xq, wq_ref[...], 16)
    kc[0:16, :] = conv(xk, wk_ref[...], 16)
    turn(128)

    def owned(zz):
        return pl.ds(pl.multiple_of(PART * (zz % 2), 16), PART)

    def a_copy(tail, got, phase, g, zz):
        return remote(
            tail.at[GROUP * g + zz // 2, owned(zz), :],
            got.at[g, z],
            a_ss.at[phase, g, zz],
            a_rs.at[phase, g, z],
            z_peer(zz),
        )

    def a_arrival(tail, got, phase, g, zz):
        return remote(
            tail.at[GROUP * g + zz // 2, owned(zz), :],
            got.at[g, zz],
            a_ss.at[phase, g, zz],
            a_rs.at[phase, g, zz],
            z_peer(zz),
        )

    def b_copy(send, take, phase, g, zz):
        return remote(
            send.at[g, zz],
            take.at[GROUP * g + z // 2, owned(z), :],
            b_ss.at[phase, g, zz],
            b_rs.at[phase, g, z],
            z_peer(zz),
        )

    def b_arrival(send, take, phase, g, zz):
        return remote(
            send.at[g, zz],
            take.at[GROUP * g + zz // 2, owned(zz), :],
            b_ss.at[phase, g, zz],
            b_rs.at[phase, g, zz],
            z_peer(zz),
        )

    def send_tail(tail, got, phase, g, p):
        for zz in (2 * p, 2 * p + 1):

            @pl.when(zz != z)
            def _():
                a_copy(tail, got, phase, g, zz).start()

    def wait_state(send, take, phase, g, p):
        for zz in (2 * p, 2 * p + 1):

            @pl.when(zz != z)
            def _():
                b_arrival(send, take, phase, g, zz).wait_recv()

    def tail_head(h):
        cols = head_cols(h)
        vc[h, 0:16, :] = conv(xv.at[h], wv_ref[:, cols], 16)
        value = vc[h]
        put_features(phik, h, uk[head_rows(h), 0:128], use_next[:, 0:128])
        tail1[h] = dot(phik[h], value, 1, 0).astype(BF16)

    for g in range(2):

        for p in range(GROUP):
            tail_head(GROUP * g + p)

        def tail_step(i, _, g=g):
            send_tail(tail1, got1, 0, g, (z // 2 + 2 + i) % GROUP)
            return 0

        lax.fori_loop(0, GROUP, tail_step, 0)

    lane_head = lax.broadcasted_iota(jnp.int32, (1, HEADS * F), 1) // F

    def inner_step(h, _):
        chosen = jnp.where(lane_head == h, 0.25, 0.0).astype(BF16)
        scores = dot(qc[...] * chosen, kc[...], 1, 1)
        m = mask_ref[...]
        kernel_h = (m * (1.0 + scores + 0.5 * scores * scores)).astype(BF16)
        kern[h] = kernel_h
        saved[h] = m * (1.0 + scores)
        inner[h] = dot(kernel_h, vc[h], 1, 0)
        put_features(phiq, h, uq[head_rows(h), :], use_prev)
        return 0

    for h in range(HEADS):
        inner_step(h, 0)

    def scan(tail, got, tot, ytot, send, take, phase, reverse):
        order = range(ZN - 1, -1, -1) if reverse else range(ZN)
        keeps = [keep_of(y * ZN + i) for i in range(ZN)]

        def y_copy(g, j):
            yy = (y + j) % n_y
            return remote(
                tot.at[g], ytot.at[g, y], y_ss.at[phase, g, yy], y_rs.at[phase, g, y], y_peer(yy)
            )

        def y_arrival(g, j):
            yy = (y + j) % n_y
            return remote(
                tot.at[g], ytot.at[g, yy], y_ss.at[phase, g, yy], y_rs.at[phase, g, yy], y_peer(yy)
            )

        for g in range(2):
            got[g, z] = tail[GROUP * g + z // 2, owned(z), :]

            def wait_a(j, _, g=g):
                a_arrival(tail, got, phase, g, (z + j) % ZN).wait_recv()
                return 0

            lax.fori_loop(1, ZN, wait_a, 0)
            running = jnp.zeros((PART, HD), F32)
            for i in order:
                running = got[g, i].astype(F32) + keeps[i] * running
            total = running.astype(BF16)
            tot[g] = total
            ytot[g, y] = total
            for j in range(1, n_y):
                y_copy(g, j).start()
        for g in range(2):
            for j in range(1, n_y):
                y_arrival(g, j).wait_recv()
            carry = jnp.zeros((PART, HD), F32)
            for r in range(n_y - 1, 0, -1) if reverse else range(n_y - 1):
                counts = jnp.where(r > y if reverse else r < y, 1.0, 0.0)
                onward = ytot[g, r].astype(F32) + keep_group(r) * carry
                carry = counts * onward + (1.0 - counts) * carry
            running = carry
            for i in order:
                send[g, i] = running.astype(BF16)
                running = got[g, i].astype(F32) + keeps[i] * running
            for away in (4, 3, 5, 2, 6, 1, 7):
                b_copy(send, take, phase, g, (z + away) % ZN).start()
            take[GROUP * g + z // 2, owned(z), :] = send[g, z]

    scan(tail1, got1, tot1, ytot1, send1, inc, 0, False)

    def forward_head(h):
        cols = head_cols(h)
        attended = inner[h] + dot(phiq[h], inc[h], 0, 0)
        r = lax.rsqrt(jnp.mean(attended * attended, axis=-1, keepdims=True) + EPS)
        normed = attended * r
        gains = gain_ref[:, cols]
        mixed_ref[:, cols] = (normed * gains).astype(BF16)
        upstream = og_ref[:, cols].astype(F32)
        local[h, 3:4, :] = jnp.sum(upstream * normed, axis=0, keepdims=True)
        pulled = upstream * gains
        along = jnp.mean(pulled * normed, axis=-1, keepdims=True)
        grad = ((pulled - normed * along) * r).astype(BF16)
        ga_ref[h] = grad
        tail2[h] = dot(phiq[h], grad, 1, 0).astype(BF16)

    local[...] = jnp.zeros(local.shape, F32)

    for g in range(2):

        def forward_step(i, _, g=g):
            p = (z // 2 + 1 + i) % GROUP
            wait_state(send1, inc, 0, g, p)
            forward_head(GROUP * g + p)
            send_tail(tail2, got2, 1, g, p)
            return 0

        lax.fori_loop(0, GROUP, forward_step, 0)

    store_mixed = pltpu.make_async_copy(mixed_ref, mixed_hbm, out_s.at[0])
    store_mixed.start()

    def backward_step(h, _):
        grad = ga_ref[h]
        grad_scores = (dot(grad, vc[h], 1, 1) * saved[h]).astype(BF16)
        rows = head_rows(h)
        grad_phi = dot(inc[h], grad, 1, 1)
        gqt[rows, :] = 0.25 * dot(kt[rows, :], grad_scores, 1, 1) + pull_features(
            grad_phi, uq[rows, :], use_prev
        )
        gkt[rows, :] = 0.25 * dot(qt[rows, :], grad_scores, 1, 0)
        gvs[h, 0:T, :] = dot(kern[h], grad, 0, 0)
        return 0

    for h in range(HEADS):
        backward_step(h, 0)

    scan(tail2, got2, tot2, ytot2, send2, outg, 1, True)

    def wait_states(send, take, phase, g):
        def one(j, _):
            b_arrival(send, take, phase, g, (z + j) % ZN).wait_recv()
            return 0

        lax.fori_loop(1, ZN, one, 0)

    def taps(g, x):
        return [jnp.sum(g * x[8 - j : 8 - j + T], axis=0, keepdims=True) for j in range(3)]

    def last_head(h):
        rows = head_rows(h)
        later = outg[h]
        grad_phi = dot(later, vc[h], 1, 1)
        gkt[rows, :] = gkt[rows, :] + pull_features(grad_phi, uk[rows, :], use_next)
        g = gvs[h, 0:T, :] + dot(phik[h], later, 0, 0)
        gvs[h, 0:T, :] = g
        for j in range(3):
            local[h, j : j + 1, :] = jnp.sum(
                g * xv[h, 8 - j : 8 - j + T, :], axis=0, keepdims=True
            )

    for g in range(2):
        wait_states(send2, outg, 1, g)
        for p in range(GROUP):
            last_head(GROUP * g + p)
    gq = gqt[...].T
    gk = gkt[...].T
    gqs[0:T, :] = gq
    gks[0:T, :] = gk

    back_rim[16:24, :] = jnp.zeros((8, HD), F32)
    for j in range(2):
        for h in range(HEADS):
            back_rim[8 * j + h : 8 * j + h + 1, :] = gvs[h, j : j + 1, :]
        back_rim[16 + j : 17 + j, :] = gqs[j : j + 1, :]
        back_rim[18 + j : 19 + j, :] = gks[j : j + 1, :]
    back = remote(back_rim, back_got, back_ss.at[0], back_rs.at[0], {"ctx": before})
    back.start()

    for j in range(3):
        local[0, 4 + j : 5 + j, :] = jnp.sum(gq * xq[8 - j : 8 - j + T, :], axis=0, keepdims=True)
        local[1, 4 + j : 5 + j, :] = jnp.sum(gk * xk[8 - j : 8 - j + T, :], axis=0, keepdims=True)

    halves[0, 16:24, :] = local[0]
    halves[1, 16:24, :] = local[1]
    for h in range(HEADS):
        halves[h // 4, 4 * (h % 4) : 4 * (h % 4) + 4, :] = local[h, 0:4, :]
    to_core = remote(halves.at[1 - core], red_c, rc_ss.at[0], rc_rs.at[0], other)
    to_core.start()
    to_core.wait_recv()
    mine = halves[core] + red_c[...]
    one_xy[...] = mine
    here = x * n_y + y
    red_xy[here] = mine
    to_plane = [
        (
            remote(one_xy, red_xy.at[here], rxy_ss.at[slot], rxy_rs.at[here], peer),
            remote(one_xy, red_xy.at[slot], rxy_ss.at[slot], rxy_rs.at[slot], peer),
        )
        for slot, peer in plane
    ]
    for c, _ in to_plane:
        c.start()

    for _, c in to_plane:
        c.wait_recv()
    mine = jnp.sum(red_xy[...], axis=0)
    one_z[...] = mine
    red_z[z] = mine

    def rz(zz, slot):
        return remote(one_z, red_z.at[slot], rz_ss.at[zz], rz_rs.at[slot], z_peer(zz))

    for away in (4, 3, 5, 2, 6, 1, 7):
        rz((z + away) % ZN, z).start()
    back.wait_recv()
    inside_next = jnp.where(me < n_ctx - 1, 1.0, 0.0)
    for j in range(2):
        row = T + j
        for h in range(HEADS):
            gvs[h, row : row + 1, :] = back_got[8 * j + h : 8 * j + h + 1, :] * inside_next
        gqs[row : row + 1, :] = back_got[16 + j : 17 + j, :] * inside_next
        gks[row : row + 1, :] = back_got[18 + j : 19 + j, :] * inside_next

    def conv_back(g, w):
        return (w[0:1] * g[0:T] + w[1:2] * g[1 : 1 + T] + w[2:3] * g[2 : 2 + T]).astype(BF16)

    gq_ref[...] = conv_back(gqs, wq_ref[...])
    gk_ref[...] = conv_back(gks, wk_ref[...])

    def value_step(h, _):
        cols = head_cols(h)
        w = wv_ref[:, cols]
        gv_ref[:, cols] = (
            w[0:1] * gvs[h, 0:T, :]
            + w[1:2] * gvs[h, 1 : 1 + T, :]
            + w[2:3] * gvs[h, 2 : 2 + T, :]
        ).astype(BF16)
        return 0

    for h in range(HEADS):
        value_step(h, 0)
    stores = [store_mixed]
    for i, (src, dst) in enumerate([(gq_ref, gq_hbm), (gk_ref, gk_hbm), (gv_ref, gv_hbm)]):
        stores.append(pltpu.make_async_copy(src, dst, out_s.at[1 + i]))
        stores[-1].start()

    for j in range(1, ZN):
        rz((z + j) % ZN, (z + j) % ZN).wait_recv()
    mine = jnp.sum(red_z[...], axis=0)
    one_c[core] = mine
    back_to_core = remote(one_c.at[core], one_c.at[core], ac_ss.at[0], ac_rs.at[0], other)
    back_to_core.start()
    remote(one_c.at[core], one_c.at[1 - core], ac_ss.at[0], ac_rs.at[0], other).wait_recv()
    sums_ref[...] = one_c[...]

    for c in stores:
        c.wait()
    halo.wait_send()
    back.wait_send()

    def left(j, _):
        zz = (z + j) % ZN
        for g in range(2):
            a_copy(tail1, got1, 0, g, zz).wait_send()
            a_copy(tail2, got2, 1, g, zz).wait_send()
            b_copy(send1, inc, 0, g, zz).wait_send()
            b_copy(send2, outg, 1, g, zz).wait_send()
        rz(zz, z).wait_send()
        return 0

    lax.fori_loop(1, ZN, left, 0)
    for j in range(1, n_y):
        yy = (y + j) % n_y
        for g in range(2):
            for phase, tot, ytot in ((0, tot1, ytot1), (1, tot2, ytot2)):
                remote(
                    tot.at[g], ytot.at[g, y], y_ss.at[phase, g, yy], y_rs.at[phase, g, y], y_peer(yy)
                ).wait_send()
    for c, _ in to_plane:
        c.wait_send()
    to_core.wait_send()
    back_to_core.wait_send()


def writer(*refs):
    mixed, gq, gk, gv, sums_hbm = refs[:5]
    outs = refs[5:13]
    held = refs[13:17]
    sums, gwq, gwk, gwv, gg, in_s, out_s = refs[17:]
    ins = [
        pltpu.make_async_copy(src, dst, in_s.at[i])
        for i, (src, dst) in enumerate(
            [(sums_hbm, sums), (mixed, held[0]), (gv, held[3]), (gq, held[1]), (gk, held[2])]
        )
    ]
    stores = [
        pltpu.make_async_copy(src, dst, out_s.at[i])
        for i, (src, dst) in enumerate(
            [
                (held[0], outs[0]),
                (held[3], outs[3]),
                (held[1], outs[1]),
                (held[2], outs[2]),
                (gwq, outs[4]),
                (gwk, outs[5]),
                (gwv, outs[6]),
                (gg, outs[7]),
            ]
        )
    ]
    for c in ins:
        c.start()
    for i in (1, 2, 3, 4):
        ins[i].wait()
        stores[i - 1].start()
    ins[0].wait()
    gwq[...] = sums[0, 20:23, :]
    gwk[...] = sums[1, 20:23, :]
    for h in range(HEADS):
        base = 4 * (h % 4)
        gwv[:, h * HD : (h + 1) * HD] = sums[h // 4, base : base + 3, :]
        gg[:, h * HD : (h + 1) * HD] = sums[h // 4, base + 3 : base + 4, :]
    for c in stores[4:]:
        c.start()
    for c in stores:
        c.wait()


def solution(mesh):
    n_dp, n_ctx = mesh.shape["dp"], mesh.shape["ctx"]
    n_y = n_ctx // ZN
    wide = HEADS * HD
    thin = HEADS * F

    def shards(q, k, v, wq, wk, wv, gain, lens, og):
        vmem = pl.BlockSpec(memory_space=pltpu.VMEM)
        state = (ROWS, HD)
        hbm = pl.BlockSpec(memory_space=pltpu.HBM)
        scratch = [
            pltpu.VMEM((T, wide), BF16),
            pltpu.VMEM((T, thin), BF16),
            pltpu.VMEM((T, thin), BF16),
            pltpu.VMEM((T, wide), BF16),
            pltpu.SemaphoreType.DMA((4,)),
            pltpu.SMEM((1, DOCS), jnp.int32),
            pltpu.VMEM((T, thin), BF16),
            pltpu.VMEM((T, thin), BF16),
            pltpu.VMEM((T, wide), BF16),
            pltpu.VMEM((T, wide), BF16),
            pltpu.VMEM((3, thin), F32),
            pltpu.VMEM((3, thin), F32),
            pltpu.VMEM((3, wide), F32),
            pltpu.VMEM((1, wide), F32),
            pltpu.VMEM((T + 8, thin), F32),
            pltpu.VMEM((T + 8, thin), F32),
            pltpu.VMEM((HEADS, T + 8, HD), F32),
            pltpu.VMEM((T, thin), BF16),
            pltpu.VMEM((T, thin), BF16),
            pltpu.VMEM((thin, T), BF16),
            pltpu.VMEM((thin, T), BF16),
            pltpu.VMEM((thin, T), F32),
            pltpu.VMEM((thin, T), F32),
            pltpu.VMEM((HEADS, T, HD), BF16),
            pltpu.VMEM((T, T), F32),
            pltpu.VMEM((HEADS, T, T), BF16),
            pltpu.VMEM((HEADS, T, T), F32),
            pltpu.VMEM((HEADS, T, HD), F32),
            pltpu.VMEM((HEADS, ROWS, T), BF16),
            pltpu.VMEM((HEADS, ROWS, T), BF16),
            pltpu.VMEM((HEADS, T, HD), BF16),
            pltpu.VMEM((HEADS, T + 8, HD), F32),
            pltpu.VMEM((thin, T), F32),
            pltpu.VMEM((thin, T), F32),
            pltpu.VMEM((T + 8, thin), F32),
            pltpu.VMEM((T + 8, thin), F32),
            pltpu.VMEM((HEADS, 8, HD), F32),
            pltpu.VMEM((24, HD), F32),
            pltpu.VMEM((24, HD), F32),
            pltpu.VMEM((24, HD), F32),
            pltpu.VMEM((24, HD), F32),
        ]
        for _ in range(2):
            scratch += [
                pltpu.VMEM((HEADS,) + state, BF16),
                pltpu.VMEM((2, ZN, PART, HD), BF16),
                pltpu.VMEM((2, PART, HD), BF16),
                pltpu.VMEM((2, n_y, PART, HD), BF16),
                pltpu.VMEM((2, ZN, PART, HD), BF16),
                pltpu.VMEM((HEADS,) + state, BF16),
            ]
        half = (24, HD)
        scratch += [
            pltpu.VMEM((2,) + half, F32),
            pltpu.VMEM(half, F32),
            pltpu.VMEM((n_dp // 2 * n_y,) + half, F32),
            pltpu.VMEM(half, F32),
            pltpu.VMEM((ZN,) + half, F32),
            pltpu.VMEM(half, F32),
            pltpu.VMEM((2,) + half, F32),
            pltpu.SemaphoreType.DMA((9,)),
        ]
        dma = pltpu.SemaphoreType.DMA
        for counts in ((1,), (1,), (2, 2, ZN), (2, 2, n_y), (2, 2, ZN), (1,), (n_dp // 2 * n_y,), (ZN,), (1,)):
            scratch += [dma(counts), dma(counts)]
        outs = pl.pallas_call(
            functools.partial(kernel, n_dp, n_ctx),
            out_shape=(
                jax.ShapeDtypeStruct((T, wide), BF16),
                jax.ShapeDtypeStruct((T, thin), BF16),
                jax.ShapeDtypeStruct((T, thin), BF16),
                jax.ShapeDtypeStruct((T, wide), BF16),
                jax.ShapeDtypeStruct((2,) + half, F32),
            ),
            in_specs=[hbm] * 9,
            out_specs=(hbm,) * 4 + (vmem,),
            scratch_shapes=scratch,
            compiler_params=pltpu.CompilerParams(
                collective_id=0, has_side_effects=True, vmem_limit_bytes=64 * 2**20 - 2**18
            ),
        )(lens, q[0], k[0], v[0], og[0], wq, wk, wv, gain[None])
        outs = pl.pallas_call(
            writer,
            out_shape=(
                jax.ShapeDtypeStruct((T, wide), BF16),
                jax.ShapeDtypeStruct((T, thin), BF16),
                jax.ShapeDtypeStruct((T, thin), BF16),
                jax.ShapeDtypeStruct((T, wide), BF16),
                jax.ShapeDtypeStruct((3, thin), F32),
                jax.ShapeDtypeStruct((3, thin), F32),
                jax.ShapeDtypeStruct((3, wide), F32),
                jax.ShapeDtypeStruct((1, wide), F32),
            ),
            in_specs=[hbm] * 5,
            out_specs=(hbm,) * 8,
            scratch_shapes=[
                pltpu.VMEM((T, wide), BF16),
                pltpu.VMEM((T, thin), BF16),
                pltpu.VMEM((T, thin), BF16),
                pltpu.VMEM((T, wide), BF16),
                pltpu.VMEM((2,) + half, F32),
                pltpu.VMEM((3, thin), F32),
                pltpu.VMEM((3, thin), F32),
                pltpu.VMEM((3, wide), F32),
                pltpu.VMEM((1, wide), F32),
                pltpu.SemaphoreType.DMA((5,)),
                pltpu.SemaphoreType.DMA((8,)),
            ],
        )(*outs)
        mixed, gq, gk, gv, gwq, gwk, gwv, gg = outs
        return mixed[None], gq[None], gk[None], gv[None], gwq, gwk, gwv, gg[0]

    tokens = P("dp", "ctx", None)
    return jax.shard_map(
        shards,
        mesh=mesh,
        in_specs=(tokens, tokens, tokens, P(), P(), P(), P(), P("dp", None), tokens),
        out_specs=(tokens, tokens, tokens, tokens, P(), P(), P(), P()),
        check_vma=False,
    )
```

```python
import functools

import jax
import jax.numpy as jnp
from jax import lax
from jax.experimental import pallas as pl
from jax.experimental.pallas import tpu as pltpu
from jax.sharding import PartitionSpec as P

HEADS = 8
F = 16
HD = 128
T = 256
DOCS = 8
ROWS = 160
PART = ROWS // 2
GROUP = HEADS // 2
ZN = 8
EPS = 1e-06
MESH = pl.DeviceIdType.MESH
F32 = jnp.float32
BF16 = jnp.bfloat16


def dot(a, b, ca, cb):
    return lax.dot_general(a, b, (((ca,), (cb,)), ((), ())), preferred_element_type=F32)


def turned(u, d):
    return pltpu.roll(u, F - d, 0) if d else u


def put_features(out, h, u, ones):
    n = u.shape[1]
    out[h, 0:16, 0:n] = (u * u * (0.5**0.5)).astype(BF16)
    for d in range(1, 8):
        out[h, 16 * d : 16 * d + 16, 0:n] = (u * turned(u, d)).astype(BF16)
    out[h, 128:144, 0:n] = u.astype(BF16)
    rest = jnp.where(lax.broadcasted_iota(jnp.int32, (8, n), 0) == 0, ones, 0.0)
    out[h, 144:160, 0:n] = jnp.concatenate([u[0:8] * u[8:16], rest], axis=0).astype(BF16)


def pull_features(g, u, ones):
    total = g[128:144] * ones + (2.0 * 0.5**0.5) * g[0:16] * u
    for d in range(1, 8):
        own = g[16 * d : 16 * d + 16]
        total = total + own * turned(u, d) + pltpu.roll(own * u, d, 0)
    half = g[144:152]
    total = total + jnp.concatenate([half * u[8:16], half * u[0:8]], axis=0)
    return 0.5 * total


def kernel(
    n_dp,
    n_ctx,
    lens_hbm,
    q_hbm,
    k_hbm,
    v_hbm,
    og_hbm,
    wq_hbm,
    wk_hbm,
    wv_hbm,
    gain_hbm,
    mixed_hbm,
    gq_hbm,
    gk_hbm,
    gv_hbm,
    sums_ref,
    mixed_ref,
    gq_ref,
    gk_ref,
    gv_ref,
    out_s,
    lens,
    q_ref,
    k_ref,
    v_ref,
    og_ref,
    wq_ref,
    wk_ref,
    wv_ref,
    gain_ref,
    xq,
    xk,
    xv,
    qc,
    kc,
    qt,
    kt,
    uq,
    uk,
    vc,
    mask_ref,
    kern,
    saved,
    inner,
    phiq,
    phik,
    ga_ref,
    gvs,
    gqt,
    gkt,
    gqs,
    gks,
    local,
    rim,
    rim_got,
    back_rim,
    back_got,
    tail1,
    got1,
    tot1,
    ytot1,
    send1,
    inc,
    tail2,
    got2,
    tot2,
    ytot2,
    send2,
    outg,
    halves,
    red_c,
    red_xy,
    one_xy,
    red_z,
    one_z,
    one_c,
    in_s,
    halo_ss,
    halo_rs,
    back_ss,
    back_rs,
    a_ss,
    a_rs,
    y_ss,
    y_rs,
    b_ss,
    b_rs,
    rc_ss,
    rc_rs,
    rxy_ss,
    rxy_rs,
    rz_ss,
    rz_rs,
    ac_ss,
    ac_rs,
):
    n_y = n_ctx // ZN
    me = lax.axis_index("ctx")
    dp = lax.axis_index("dp")
    n_x = n_dp // 2
    core = dp % 2
    x = dp // 2
    y = me // ZN
    z = me % ZN
    after = (me + 1) % n_ctx
    before = (me + n_ctx - 1) % n_ctx

    def z_peer(zz):
        return {"ctx": y * ZN + zz}

    def y_peer(yy):
        return {"ctx": yy * ZN + z}

    barrier = pltpu.get_barrier_semaphore()
    greeted = [z_peer((z + j) % ZN) for j in (4, 3, 5)] + [{"ctx": after}, {"ctx": before}]
    greeted += [z_peer((z + j) % ZN) for j in (2, 6, 1, 7)]
    other = {"dp": dp + 1 - 2 * core}
    plane = []
    for j in range(1, n_x * n_y):
        xx = (x + j // n_y) % n_x
        yy = (y + j % n_y) % n_y
        plane.append((xx * n_y + yy, {"dp": xx * 2 + core, "ctx": yy * ZN + z}))
    greeted += [peer for _, peer in plane]
    greeted += [other]
    for peer in greeted:
        pl.semaphore_signal(barrier, inc=1, device_id=peer, device_id_type=MESH)

    loads = [
        pltpu.make_async_copy(src, dst, in_s.at[i])
        for i, (src, dst) in enumerate(
            [
                (lens_hbm, lens),
                (q_hbm, q_ref),
                (k_hbm, k_ref),
                (wq_hbm, wq_ref),
                (wk_hbm, wk_ref),
                (v_hbm, v_ref),
                (wv_hbm, wv_ref),
                (gain_hbm, gain_ref),
                (og_hbm, og_ref),
            ]
        )
    ]
    for c in loads:
        c.start()
    for c in loads[:5]:
        c.wait()

    starts = []
    total = jnp.int32(0)
    for d in range(DOCS):
        starts.append(total)
        total = total + lens[0, d]
    first = me * T

    def doc_of(position):
        found = jnp.where(position >= starts[0], 1, 0)
        for d in range(1, DOCS):
            found = found + jnp.where(position >= starts[d], 1, 0)
        return found

    row_pos = first + lax.broadcasted_iota(jnp.int32, (1, T), 1)
    col_pos = first + lax.broadcasted_iota(jnp.int32, (T, 1), 0)
    row_doc, col_doc = doc_of(row_pos), doc_of(col_pos)
    prev_doc, last_doc = doc_of(first - 1), doc_of(first + T - 1)
    use_prev = jnp.where(row_doc == prev_doc, 1.0, 0.0)
    use_next = jnp.where(row_doc == last_doc, 1.0, 0.0)
    mask_ref[...] = jnp.where((row_pos <= col_pos) & (row_doc == col_doc), 1.0, 0.0)

    def keep_of(block):
        value = jnp.float32(1.0)
        for d in range(DOCS):
            value = jnp.where(starts[d] // T == block, 0.0, value)
        return value

    def keep_group(group):
        value = jnp.float32(1.0)
        for d in range(DOCS):
            value = jnp.where(starts[d] // (T * ZN) == group, 0.0, value)
        return value

    def conv(xs, w, rows):
        return (
            w[0:1] * xs[8 : 8 + rows, :] + w[1:2] * xs[7 : 7 + rows, :] + w[2:3] * xs[6 : 6 + rows, :]
        ).astype(BF16)

    def head_rows(h):
        return pl.ds(h * F if isinstance(h, int) else pl.multiple_of(h * F, F), F)

    def head_cols(h):
        return pl.ds(h * HD if isinstance(h, int) else pl.multiple_of(h * HD, HD), HD)

    xq[0:8, :] = jnp.zeros((8, HEADS * F), F32)
    xk[0:8, :] = jnp.zeros((8, HEADS * F), F32)
    xq[8:, :] = q_ref[...].astype(F32)
    xk[8:, :] = k_ref[...].astype(F32)
    qc[...] = conv(xq, wq_ref[...], T)
    kc[...] = conv(xk, wk_ref[...], T)

    def turn(tokens):
        q_turned = qc[0:tokens, :].astype(F32).T
        k_turned = kc[0:tokens, :].astype(F32).T
        qt[:, 0:tokens] = q_turned.astype(BF16)
        kt[:, 0:tokens] = k_turned.astype(BF16)
        uq[:, 0:tokens] = q_turned * (0.5 * use_prev[:, 0:tokens])
        uk[:, 0:tokens] = k_turned * (0.5 * use_next[:, 0:tokens])

    turn(T)
    for c in loads[5:]:
        c.wait()

    def value_head(h, _):
        cols = head_cols(h)
        xv[h, 0:8, :] = jnp.zeros((8, HD), F32)
        xv[h, 8:, :] = v_ref[:, cols].astype(F32)
        vc[h] = conv(xv.at[h], wv_ref[:, cols], T)
        return 0

    for h in range(HEADS):
        value_head(h, 0)

    pl.semaphore_wait(barrier, len(greeted))

    def remote(src, dst, ss, rs, peer):
        return pltpu.make_async_remote_copy(
            src_ref=src, dst_ref=dst, send_sem=ss, recv_sem=rs, device_id=peer, device_id_type=MESH
        )

    rim[16:24, :] = jnp.zeros((8, HD), F32)
    for j in range(2):
        row = T + 6 + j
        for h in range(HEADS):
            rim[8 * j + h : 8 * j + h + 1, :] = xv[h, row : row + 1, :]
        rim[16 + j : 17 + j, :] = xq[row : row + 1, :]
        rim[18 + j : 19 + j, :] = xk[row : row + 1, :]
    halo = remote(rim, rim_got, halo_ss.at[0], halo_rs.at[0], {"ctx": after})
    halo.start()
    for h in range(HEADS):
        put_features(phik, h, uk[head_rows(h), :], use_next)
    halo.wait_recv()
    inside = jnp.where(me > 0, 1.0, 0.0)
    for j in range(2):
        for h in range(HEADS):
            xv[h, 6 + j : 7 + j, :] = rim_got[8 * j + h : 8 * j + h + 1, :] * inside
        xq[6 + j : 7 + j, :] = rim_got[16 + j : 17 + j, :] * inside
        xk[6 + j : 7 + j, :] = rim_got[18 + j : 19 + j, :] * inside
    qc[0:16, :] = conv(xq, wq_ref[...], 16)
    kc[0:16, :] = conv(xk, wk_ref[...], 16)
    turn(128)

    def owned(zz):
        return pl.ds(pl.multiple_of(PART * (zz % 2), 16), PART)

    def a_copy(tail, got, phase, g, zz):
        return remote(
            tail.at[GROUP * g + zz // 2, owned(zz), :],
            got.at[g, z],
            a_ss.at[phase, g, zz],
            a_rs.at[phase, g, z],
            z_peer(zz),
        )

    def a_arrival(tail, got, phase, g, zz):
        return remote(
            tail.at[GROUP * g + zz // 2, owned(zz), :],
            got.at[g, zz],
            a_ss.at[phase, g, zz],
            a_rs.at[phase, g, zz],
            z_peer(zz),
        )

    def b_copy(send, take, phase, g, zz):
        return remote(
            send.at[g, zz],
            take.at[GROUP * g + z // 2, owned(z), :],
            b_ss.at[phase, g, zz],
            b_rs.at[phase, g, z],
            z_peer(zz),
        )

    def b_arrival(send, take, phase, g, zz):
        return remote(
            send.at[g, zz],
            take.at[GROUP * g + zz // 2, owned(zz), :],
            b_ss.at[phase, g, zz],
            b_rs.at[phase, g, zz],
            z_peer(zz),
        )

    def send_tail(tail, got, phase, g, p):
        for zz in (2 * p, 2 * p + 1):

            @pl.when(zz != z)
            def _():
                a_copy(tail, got, phase, g, zz).start()

    def wait_state(send, take, phase, g, p):
        for zz in (2 * p, 2 * p + 1):

            @pl.when(zz != z)
            def _():
                b_arrival(send, take, phase, g, zz).wait_recv()

    def tail_head(h):
        cols = head_cols(h)
        vc[h, 0:16, :] = conv(xv.at[h], wv_ref[:, cols], 16)
        value = vc[h]
        put_features(phik, h, uk[head_rows(h), 0:128], use_next[:, 0:128])
        tail1[h] = dot(phik[h], value, 1, 0).astype(BF16)

    for g in range(2):

        for p in range(GROUP):
            tail_head(GROUP * g + p)

        def tail_step(i, _, g=g):
            send_tail(tail1, got1, 0, g, (z // 2 + 2 + i) % GROUP)
            return 0

        lax.fori_loop(0, GROUP, tail_step, 0)

    lane_head = lax.broadcasted_iota(jnp.int32, (1, HEADS * F), 1) // F

    def inner_step(h, _):
        chosen = jnp.where(lane_head == h, 0.25, 0.0).astype(BF16)
        scores = dot(qc[...] * chosen, kc[...], 1, 1)
        m = mask_ref[...]
        kernel_h = (m * (1.0 + scores + 0.5 * scores * scores)).astype(BF16)
        kern[h] = kernel_h
        saved[h] = m * (1.0 + scores)
        inner[h] = dot(kernel_h, vc[h], 1, 0)
        put_features(phiq, h, uq[head_rows(h), :], use_prev)
        return 0

    for h in range(HEADS):
        inner_step(h, 0)

    def scan(tail, got, tot, ytot, send, take, phase, reverse):
        order = range(ZN - 1, -1, -1) if reverse else range(ZN)
        keeps = [keep_of(y * ZN + i) for i in range(ZN)]

        def y_copy(g, j):
            yy = (y + j) % n_y
            return remote(
                tot.at[g], ytot.at[g, y], y_ss.at[phase, g, yy], y_rs.at[phase, g, y], y_peer(yy)
            )

        def y_arrival(g, j):
            yy = (y + j) % n_y
            return remote(
                tot.at[g], ytot.at[g, yy], y_ss.at[phase, g, yy], y_rs.at[phase, g, yy], y_peer(yy)
            )

        for g in range(2):
            got[g, z] = tail[GROUP * g + z // 2, owned(z), :]

            def wait_a(j, _, g=g):
                a_arrival(tail, got, phase, g, (z + j) % ZN).wait_recv()
                return 0

            lax.fori_loop(1, ZN, wait_a, 0)
            running = jnp.zeros((PART, HD), F32)
            for i in order:
                running = got[g, i].astype(F32) + keeps[i] * running
            total = running.astype(BF16)
            tot[g] = total
            ytot[g, y] = total
            for j in range(1, n_y):
                y_copy(g, j).start()
        for g in range(2):
            for j in range(1, n_y):
                y_arrival(g, j).wait_recv()
            carry = jnp.zeros((PART, HD), F32)
            for r in range(n_y - 1, 0, -1) if reverse else range(n_y - 1):
                counts = jnp.where(r > y if reverse else r < y, 1.0, 0.0)
                onward = ytot[g, r].astype(F32) + keep_group(r) * carry
                carry = counts * onward + (1.0 - counts) * carry
            running = carry
            for i in order:
                send[g, i] = running.astype(BF16)
                running = got[g, i].astype(F32) + keeps[i] * running
            for away in (4, 3, 5, 2, 6, 1, 7):
                b_copy(send, take, phase, g, (z + away) % ZN).start()
            take[GROUP * g + z // 2, owned(z), :] = send[g, z]

    scan(tail1, got1, tot1, ytot1, send1, inc, 0, False)

    def forward_head(h):
        cols = head_cols(h)
        attended = inner[h] + dot(phiq[h], inc[h], 0, 0)
        r = lax.rsqrt(jnp.mean(attended * attended, axis=-1, keepdims=True) + EPS)
        normed = attended * r
        gains = gain_ref[:, cols]
        mixed_ref[:, cols] = (normed * gains).astype(BF16)
        upstream = og_ref[:, cols].astype(F32)
        local[h, 3:4, :] = jnp.sum(upstream * normed, axis=0, keepdims=True)
        pulled = upstream * gains
        along = jnp.mean(pulled * normed, axis=-1, keepdims=True)
        grad = ((pulled - normed * along) * r).astype(BF16)
        ga_ref[h] = grad
        tail2[h] = dot(phiq[h], grad, 1, 0).astype(BF16)

    local[...] = jnp.zeros(local.shape, F32)

    for g in range(2):

        def forward_step(i, _, g=g):
            p = (z // 2 + 1 + i) % GROUP
            wait_state(send1, inc, 0, g, p)
            forward_head(GROUP * g + p)
            send_tail(tail2, got2, 1, g, p)
            return 0

        lax.fori_loop(0, GROUP, forward_step, 0)

    store_mixed = pltpu.make_async_copy(mixed_ref, mixed_hbm, out_s.at[0])
    store_mixed.start()

    def backward_step(h, _):
        grad = ga_ref[h]
        grad_scores = (dot(grad, vc[h], 1, 1) * saved[h]).astype(BF16)
        rows = head_rows(h)
        grad_phi = dot(inc[h], grad, 1, 1)
        gqt[rows, :] = 0.25 * dot(kt[rows, :], grad_scores, 1, 1) + pull_features(
            grad_phi, uq[rows, :], use_prev
        )
        gkt[rows, :] = 0.25 * dot(qt[rows, :], grad_scores, 1, 0)
        gvs[h, 0:T, :] = dot(kern[h], grad, 0, 0)
        return 0

    for h in range(HEADS):
        backward_step(h, 0)

    scan(tail2, got2, tot2, ytot2, send2, outg, 1, True)

    def wait_states(send, take, phase, g):
        def one(j, _):
            b_arrival(send, take, phase, g, (z + j) % ZN).wait_recv()
            return 0

        lax.fori_loop(1, ZN, one, 0)

    def taps(g, x):
        return [jnp.sum(g * x[8 - j : 8 - j + T], axis=0, keepdims=True) for j in range(3)]

    def last_head(h):
        rows = head_rows(h)
        later = outg[h]
        grad_phi = dot(later, vc[h], 1, 1)
        gkt[rows, :] = gkt[rows, :] + pull_features(grad_phi, uk[rows, :], use_next)
        g = gvs[h, 0:T, :] + dot(phik[h], later, 0, 0)
        gvs[h, 0:T, :] = g
        for j in range(3):
            local[h, j : j + 1, :] = jnp.sum(
                g * xv[h, 8 - j : 8 - j + T, :], axis=0, keepdims=True
            )

    for g in range(2):
        wait_states(send2, outg, 1, g)
        for p in range(GROUP):
            last_head(GROUP * g + p)
    gq = gqt[...].T
    gk = gkt[...].T
    gqs[0:T, :] = gq
    gks[0:T, :] = gk

    back_rim[16:24, :] = jnp.zeros((8, HD), F32)
    for j in range(2):
        for h in range(HEADS):
            back_rim[8 * j + h : 8 * j + h + 1, :] = gvs[h, j : j + 1, :]
        back_rim[16 + j : 17 + j, :] = gqs[j : j + 1, :]
        back_rim[18 + j : 19 + j, :] = gks[j : j + 1, :]
    back = remote(back_rim, back_got, back_ss.at[0], back_rs.at[0], {"ctx": before})
    back.start()

    for j in range(3):
        local[0, 4 + j : 5 + j, :] = jnp.sum(gq * xq[8 - j : 8 - j + T, :], axis=0, keepdims=True)
        local[1, 4 + j : 5 + j, :] = jnp.sum(gk * xk[8 - j : 8 - j + T, :], axis=0, keepdims=True)

    halves[0, 16:24, :] = local[0]
    halves[1, 16:24, :] = local[1]
    for h in range(HEADS):
        halves[h // 4, 4 * (h % 4) : 4 * (h % 4) + 4, :] = local[h, 0:4, :]
    to_core = remote(halves.at[1 - core], red_c, rc_ss.at[0], rc_rs.at[0], other)
    to_core.start()
    to_core.wait_recv()
    mine = halves[core] + red_c[...]
    one_xy[...] = mine
    here = x * n_y + y
    red_xy[here] = mine
    to_plane = [
        (
            remote(one_xy, red_xy.at[here], rxy_ss.at[slot], rxy_rs.at[here], peer),
            remote(one_xy, red_xy.at[slot], rxy_ss.at[slot], rxy_rs.at[slot], peer),
        )
        for slot, peer in plane
    ]
    for c, _ in to_plane:
        c.start()

    for _, c in to_plane:
        c.wait_recv()
    mine = jnp.sum(red_xy[...], axis=0)
    one_z[...] = mine
    red_z[z] = mine

    def rz(zz, slot):
        return remote(one_z, red_z.at[slot], rz_ss.at[zz], rz_rs.at[slot], z_peer(zz))

    for away in (4, 3, 5, 2, 6, 1, 7):
        rz((z + away) % ZN, z).start()
    back.wait_recv()
    inside_next = jnp.where(me < n_ctx - 1, 1.0, 0.0)
    for j in range(2):
        row = T + j
        for h in range(HEADS):
            gvs[h, row : row + 1, :] = back_got[8 * j + h : 8 * j + h + 1, :] * inside_next
        gqs[row : row + 1, :] = back_got[16 + j : 17 + j, :] * inside_next
        gks[row : row + 1, :] = back_got[18 + j : 19 + j, :] * inside_next

    def conv_back(g, w):
        return (w[0:1] * g[0:T] + w[1:2] * g[1 : 1 + T] + w[2:3] * g[2 : 2 + T]).astype(BF16)

    gq_ref[...] = conv_back(gqs, wq_ref[...])
    gk_ref[...] = conv_back(gks, wk_ref[...])

    def value_step(h, _):
        cols = head_cols(h)
        w = wv_ref[:, cols]
        gv_ref[:, cols] = (
            w[0:1] * gvs[h, 0:T, :]
            + w[1:2] * gvs[h, 1 : 1 + T, :]
            + w[2:3] * gvs[h, 2 : 2 + T, :]
        ).astype(BF16)
        return 0

    for h in range(HEADS):
        value_step(h, 0)
    stores = [store_mixed]
    for i, (src, dst) in enumerate([(gq_ref, gq_hbm), (gk_ref, gk_hbm), (gv_ref, gv_hbm)]):
        stores.append(pltpu.make_async_copy(src, dst, out_s.at[1 + i]))
        stores[-1].start()

    for j in range(1, ZN):
        rz((z + j) % ZN, (z + j) % ZN).wait_recv()
    mine = jnp.sum(red_z[...], axis=0)
    one_c[core] = mine
    back_to_core = remote(one_c.at[core], one_c.at[core], ac_ss.at[0], ac_rs.at[0], other)
    back_to_core.start()
    remote(one_c.at[core], one_c.at[1 - core], ac_ss.at[0], ac_rs.at[0], other).wait_recv()
    sums_ref[...] = one_c[...]

    for c in stores:
        c.wait()
    halo.wait_send()
    back.wait_send()

    def left(j, _):
        zz = (z + j) % ZN
        for g in range(2):
            a_copy(tail1, got1, 0, g, zz).wait_send()
            a_copy(tail2, got2, 1, g, zz).wait_send()
            b_copy(send1, inc, 0, g, zz).wait_send()
            b_copy(send2, outg, 1, g, zz).wait_send()
        rz(zz, z).wait_send()
        return 0

    lax.fori_loop(1, ZN, left, 0)
    for j in range(1, n_y):
        yy = (y + j) % n_y
        for g in range(2):
            for phase, tot, ytot in ((0, tot1, ytot1), (1, tot2, ytot2)):
                remote(
                    tot.at[g], ytot.at[g, y], y_ss.at[phase, g, yy], y_rs.at[phase, g, y], y_peer(yy)
                ).wait_send()
    for c, _ in to_plane:
        c.wait_send()
    to_core.wait_send()
    back_to_core.wait_send()


def writer(*refs):
    mixed, gq, gk, gv, sums_hbm = refs[:5]
    outs = refs[5:13]
    held = refs[13:17]
    sums, gwq, gwk, gwv, gg, in_s, out_s = refs[17:]
    ins = [
        pltpu.make_async_copy(src, dst, in_s.at[i])
        for i, (src, dst) in enumerate(
            [(sums_hbm, sums), (mixed, held[0]), (gv, held[3]), (gq, held[1]), (gk, held[2])]
        )
    ]
    stores = [
        pltpu.make_async_copy(src, dst, out_s.at[i])
        for i, (src, dst) in enumerate(
            [
                (held[0], outs[0]),
                (held[3], outs[3]),
                (held[1], outs[1]),
                (held[2], outs[2]),
                (gwq, outs[4]),
                (gwk, outs[5]),
                (gwv, outs[6]),
                (gg, outs[7]),
            ]
        )
    ]
    for c in ins:
        c.start()
    for i in (1, 2, 3, 4):
        ins[i].wait()
        stores[i - 1].start()
    ins[0].wait()
    gwq[...] = sums[0, 20:23, :]
    gwk[...] = sums[1, 20:23, :]
    for h in range(HEADS):
        base = 4 * (h % 4)
        gwv[:, h * HD : (h + 1) * HD] = sums[h // 4, base : base + 3, :]
        gg[:, h * HD : (h + 1) * HD] = sums[h // 4, base + 3 : base + 4, :]
    for c in stores[4:]:
        c.start()
    for c in stores:
        c.wait()


def solution(mesh):
    n_dp, n_ctx = mesh.shape["dp"], mesh.shape["ctx"]
    n_y = n_ctx // ZN
    wide = HEADS * HD
    thin = HEADS * F

    def shards(q, k, v, wq, wk, wv, gain, lens, og):
        vmem = pl.BlockSpec(memory_space=pltpu.VMEM)
        state = (ROWS, HD)
        hbm = pl.BlockSpec(memory_space=pltpu.HBM)
        scratch = [
            pltpu.VMEM((T, wide), BF16),
            pltpu.VMEM((T, thin), BF16),
            pltpu.VMEM((T, thin), BF16),
            pltpu.VMEM((T, wide), BF16),
            pltpu.SemaphoreType.DMA((4,)),
            pltpu.SMEM((1, DOCS), jnp.int32),
            pltpu.VMEM((T, thin), BF16),
            pltpu.VMEM((T, thin), BF16),
            pltpu.VMEM((T, wide), BF16),
            pltpu.VMEM((T, wide), BF16),
            pltpu.VMEM((3, thin), F32),
            pltpu.VMEM((3, thin), F32),
            pltpu.VMEM((3, wide), F32),
            pltpu.VMEM((1, wide), F32),
            pltpu.VMEM((T + 8, thin), F32),
            pltpu.VMEM((T + 8, thin), F32),
            pltpu.VMEM((HEADS, T + 8, HD), F32),
            pltpu.VMEM((T, thin), BF16),
            pltpu.VMEM((T, thin), BF16),
            pltpu.VMEM((thin, T), BF16),
            pltpu.VMEM((thin, T), BF16),
            pltpu.VMEM((thin, T), F32),
            pltpu.VMEM((thin, T), F32),
            pltpu.VMEM((HEADS, T, HD), BF16),
            pltpu.VMEM((T, T), F32),
            pltpu.VMEM((HEADS, T, T), BF16),
            pltpu.VMEM((HEADS, T, T), F32),
            pltpu.VMEM((HEADS, T, HD), F32),
            pltpu.VMEM((HEADS, ROWS, T), BF16),
            pltpu.VMEM((HEADS, ROWS, T), BF16),
            pltpu.VMEM((HEADS, T, HD), BF16),
            pltpu.VMEM((HEADS, T + 8, HD), F32),
            pltpu.VMEM((thin, T), F32),
            pltpu.VMEM((thin, T), F32),
            pltpu.VMEM((T + 8, thin), F32),
            pltpu.VMEM((T + 8, thin), F32),
            pltpu.VMEM((HEADS, 8, HD), F32),
            pltpu.VMEM((24, HD), F32),
            pltpu.VMEM((24, HD), F32),
            pltpu.VMEM((24, HD), F32),
            pltpu.VMEM((24, HD), F32),
        ]
        for _ in range(2):
            scratch += [
                pltpu.VMEM((HEADS,) + state, BF16),
                pltpu.VMEM((2, ZN, PART, HD), BF16),
                pltpu.VMEM((2, PART, HD), BF16),
                pltpu.VMEM((2, n_y, PART, HD), BF16),
                pltpu.VMEM((2, ZN, PART, HD), BF16),
                pltpu.VMEM((HEADS,) + state, BF16),
            ]
        half = (24, HD)
        scratch += [
            pltpu.VMEM((2,) + half, F32),
            pltpu.VMEM(half, F32),
            pltpu.VMEM((n_dp // 2 * n_y,) + half, F32),
            pltpu.VMEM(half, F32),
            pltpu.VMEM((ZN,) + half, F32),
            pltpu.VMEM(half, F32),
            pltpu.VMEM((2,) + half, F32),
            pltpu.SemaphoreType.DMA((9,)),
        ]
        dma = pltpu.SemaphoreType.DMA
        for counts in ((1,), (1,), (2, 2, ZN), (2, 2, n_y), (2, 2, ZN), (1,), (n_dp // 2 * n_y,), (ZN,), (1,)):
            scratch += [dma(counts), dma(counts)]
        outs = pl.pallas_call(
            functools.partial(kernel, n_dp, n_ctx),
            out_shape=(
                jax.ShapeDtypeStruct((T, wide), BF16),
                jax.ShapeDtypeStruct((T, thin), BF16),
                jax.ShapeDtypeStruct((T, thin), BF16),
                jax.ShapeDtypeStruct((T, wide), BF16),
                jax.ShapeDtypeStruct((2,) + half, F32),
            ),
            in_specs=[hbm] * 9,
            out_specs=(hbm,) * 4 + (vmem,),
            scratch_shapes=scratch,
            compiler_params=pltpu.CompilerParams(
                collective_id=0, has_side_effects=True, vmem_limit_bytes=64 * 2**20 - 2**18
            ),
        )(lens, q[0], k[0], v[0], og[0], wq, wk, wv, gain[None])
        outs = pl.pallas_call(
            writer,
            out_shape=(
                jax.ShapeDtypeStruct((T, wide), BF16),
                jax.ShapeDtypeStruct((T, thin), BF16),
                jax.ShapeDtypeStruct((T, thin), BF16),
                jax.ShapeDtypeStruct((T, wide), BF16),
                jax.ShapeDtypeStruct((3, thin), F32),
                jax.ShapeDtypeStruct((3, thin), F32),
                jax.ShapeDtypeStruct((3, wide), F32),
                jax.ShapeDtypeStruct((1, wide), F32),
            ),
            in_specs=[hbm] * 5,
            out_specs=(hbm,) * 8,
            scratch_shapes=[
                pltpu.VMEM((T, wide), BF16),
                pltpu.VMEM((T, thin), BF16),
                pltpu.VMEM((T, thin), BF16),
                pltpu.VMEM((T, wide), BF16),
                pltpu.VMEM((2,) + half, F32),
                pltpu.VMEM((3, thin), F32),
                pltpu.VMEM((3, thin), F32),
                pltpu.VMEM((3, wide), F32),
                pltpu.VMEM((1, wide), F32),
                pltpu.SemaphoreType.DMA((5,)),
                pltpu.SemaphoreType.DMA((8,)),
            ],
        )(*outs)
        mixed, gq, gk, gv, gwq, gwk, gwv, gg = outs
        return mixed[None], gq[None], gk[None], gv[None], gwq, gwk, gwv, gg[0]

    tokens = P("dp", "ctx", None)
    return jax.shard_map(
        shards,
        mesh=mesh,
        in_specs=(tokens, tokens, tokens, P(), P(), P(), P(), P("dp", None), tokens),
        out_specs=(tokens, tokens, tokens, tokens, P(), P(), P(), P()),
        check_vma=False,
    )
```
